32 devices in a mesh: dp: 2 (over core), seq: 16 (over z, y, x).
Axes of the slice: x: 2, y: 2, z: 4, core: 2. Of those that a mesh axis runs over, the one named last changes fastest.
Arguments:
- block_input: bfloat16 [16, 2048, 1536], P('dp', 'seq'), may hold values from -6 to 6
- skip_input: bfloat16 [16, 4096, 1536], P('dp', 'seq'), may hold values from -6 to 6
- species: int32 [16], P('dp'), may hold values from 0 to 1
- cotangent: bfloat16 [16, 4096, 1536], P('dp', 'seq'), may hold values from -6 to 6
- params: float32 [18110976], P(('dp', 'seq')), may hold values from -2 to 2, as said below
- first_moment: float32 [18110976], P(('dp', 'seq')), may hold values from -768 to 768
- second_moment: float32 [18110976], P(('dp', 'seq')), may hold values from 65536 to 262144
Outputs:
- block_out: bfloat16 [16, 4096, 1536], P('dp', 'seq')
- input_grad: float32 [16, 2048, 1536], P('dp', 'seq')
- skip_grad: float32 [16, 4096, 1536], P('dp', 'seq')
- new_params: float32 [18110976], P(('dp', 'seq'))
- new_first: float32 [18110976], P(('dp', 'seq'))
- new_second: float32 [18110976], P(('dp', 'seq'))
- params_copy: bfloat16 [18110976], P(('dp', 'seq'))
The draws below stay inside these ranges and needn't reach their ends.
Inputs may be any that keep to these rules, and one draw needn't show every extreme that they name: `params`: entries of the weight matrices have spreads about the inverse root of their fan-in; gains lie near 1. `species`: 0 marks a human window, 1 a mouse window.
All inputs are finite; a program needn't handle non-finite values.
Results may differ from the reference program's by a relative error of at most 0.0096.
Values may be sent and summed in bfloat16 or wider, within the bound.
No kernel may reach another device: no remote copies, remote signals or barrier semaphores. Data moves between devices by JAX's collectives and lax.ppermute only.
A program may use at most 640 MiB of HBM per device.

```python
import math
import jax
import jax.numpy as jnp
from jax import lax

D = 1536
H = 8
KD = 64
VD = 192
FF = 3072
F = 192
LENGTH = 2048
QB = 512
STEP = 10
WINDOWS = 16
UPLEN = 4096


def segment_limits():
    counts = [D * H * KD, D * H * KD, D * H * VD, H * VD * D, D * FF, FF * D, D * D, F * H, FF, 12 * D]
    limits = []
    running = 0
    for amount in counts:
        running = running + amount
        limits.append(running)
    return limits


def segment_number(position):
    limits = segment_limits()
    number = jnp.zeros(position.shape, jnp.int32)
    for finish in limits[:-1]:
        number = number + (position >= finish).astype(jnp.int32)
    return number


def vector_row(position):
    return (position - segment_limits()[-2]) // D


def weight_spread(position):
    number = segment_number(position)
    spreads = jnp.array([1.0 / math.sqrt(D), 1.0 / math.sqrt(D), 1.0 / math.sqrt(D), 4.0 / math.sqrt(H * VD), 1.0 / math.sqrt(D), 1.0 / math.sqrt(FF), 1.0 / math.sqrt(D), 1.5 / math.sqrt(F), 0.2, 0.2], jnp.float32)
    spread = spreads[number]
    row_here = vector_row(position)
    is_kernel = (number == 9) & (row_here >= 7) & (row_here <= 9)
    return jnp.where(is_kernel, 0.5, spread)


def gain_entry(position):
    number = segment_number(position)
    row_here = vector_row(position)
    return (number == 9) & ((row_here == 0) | (row_here == 2) | (row_here >= 10))


def gradient_scale():
    return math.sqrt(2.0 * WINDOWS * LENGTH)


def draw_params(key, part):
    key = jax.random.fold_in(key, 11)
    count = segment_limits()[-1]
    position = jnp.arange(count).astype(jnp.int32)
    base = jnp.clip(jax.random.normal(key, (count,), jnp.float32), -4.0, 4.0)
    gains = 1.0 + 0.5 * jax.random.uniform(jax.random.fold_in(key, 1), (count,), jnp.float32, -1.0, 1.0)
    return jnp.where(gain_entry(position), gains, weight_spread(position) * base)


def draw_first_moment(key, part):
    key = jax.random.fold_in(key, 12)
    count = segment_limits()[-1]
    base = jnp.clip(jax.random.normal(key, (count,), jnp.float32), -3.0, 3.0)
    return gradient_scale() * base


def draw_second_moment(key, part):
    key = jax.random.fold_in(key, 13)
    count = segment_limits()[-1]
    spread = jax.random.uniform(key, (count,), jnp.float32, 0.0, 2.0)
    return 2.0 * WINDOWS * LENGTH * jnp.exp(spread * math.log(2.0))


def place_ends(values, rng, low, top_value):
    shape = values.shape
    index_at = [jax.random.randint(jax.random.fold_in(rng, axis), (), 0, shape[axis]) for axis in range(len(shape))]
    values = values.at[tuple(index_at)].set(low)
    longest = shape.index(max(shape))
    index_at[longest] = (index_at[longest] + 1) % shape[longest]
    return values.at[tuple(index_at)].set(top_value)


def levels(rng, shape, shards, least, largest):
    gain, own = 1.0, jax.random.fold_in(rng, 6)
    for dim, parts in shards:
        heights = jnp.exp(jax.random.uniform(jax.random.fold_in(own, dim), (parts,), jnp.float32, least / len(shards), largest / len(shards)))
        gain = gain * jnp.repeat(heights, shape[dim] // parts).reshape([-1 if axis == dim else 1 for axis in range(len(shape))])
    return gain


def noise(key, extent, deviation, limit, shards=(), held_as=jnp.bfloat16):
    values = jax.random.normal(key, extent, jnp.float32) * deviation
    if len(shards) > 0:
        values = levels(key, extent, shards, -0.22, 0.18) * values
    return jnp.clip(values, min=-limit, max=limit).astype(held_as)


def setup_inputs(seed: int = 0) -> dict:
    key_list = jax.random.split(jax.random.key(seed), 8)
    return {
        "block_input": noise(key_list[0], (WINDOWS, LENGTH, D), 1.0, 6.0, ((0, 2), (1, 16))),
        "skip_input": noise(key_list[1], (WINDOWS, UPLEN, D), 1.0, 6.0, ((0, 2), (1, 16))),
        "species": place_ends(jax.random.randint(key_list[2], (WINDOWS,), 0, 2), jax.random.fold_in(key_list[2], 1), 0, 1).astype(jnp.int32),
        "cotangent": noise(key_list[3], (WINDOWS, UPLEN, D), 1.0, 6.0, ((0, 2), (1, 16))),
        "params": draw_params(jax.random.fold_in(key_list[7], 71), 0),
        "first_moment": draw_first_moment(jax.random.fold_in(key_list[7], 71), 0),
        "second_moment": draw_second_moment(jax.random.fold_in(key_list[7], 71), 0),
    }


@jax.custom_vjp
def low(v):
    return lax.optimization_barrier(v.astype(jnp.bfloat16)).astype(jnp.float32)

@jax.custom_vjp
def low_back(v):
    return v

def low_keep(v):
    return (low(v), None)

def low_pass(kept, grad):
    return (grad,)

def back_keep(v):
    return (v, None)

def back_low(kept, grad):
    return (low(grad),)
low.defvjp(low_keep, low_pass)
low_back.defvjp(back_keep, back_low)
eps_norm = 1e-05
beta_one = 0.5
beta_two = 0.5
adam_eps = 1e-08
decay_rate = 0.01
highest = lax.Precision.HIGHEST

def segment_ends():
    counts = [D * H * KD, D * H * KD, D * H * VD, H * VD * D, D * FF, FF * D, D * D, F * H, FF, 12 * D]
    limits = []
    running = 0
    for amount in counts:
        running = running + amount
        limits.append(running)
    return limits

def rate_at(position):
    limits = segment_ends()
    step_rates = [2.0 / math.sqrt(D), 2.0 / math.sqrt(D), 2.0 / math.sqrt(D), 8.0 / math.sqrt(H * VD), 2.0 / math.sqrt(D), 2.0 / math.sqrt(FF), 2.0 / math.sqrt(D), 3.0 / math.sqrt(F), 0.4, 0.4]
    result = jnp.full(position.shape, step_rates[-1], jnp.float32)
    for segment in range(len(limits) - 2, -1, -1):
        result = jnp.where(position < limits[segment], step_rates[segment], result)
    return result

def adam_update(param_old, first_old, second_old, gradient, position):
    step_rate = rate_at(position)
    first_new = beta_one * first_old + (1.0 - beta_one) * gradient
    second_new = beta_two * second_old + (1.0 - beta_two) * gradient * gradient
    first_hat = first_new / (1.0 - beta_one ** STEP)
    second_hat = second_new / (1.0 - beta_two ** STEP)
    param_new = param_old - step_rate * (first_hat / (jnp.sqrt(second_hat) + adam_eps) + decay_rate * param_old)
    return (param_new, first_new, second_new)

def position_basis(length):
    offsets = jnp.arange(2 * length - 1).astype(jnp.float32) - (length - 1)
    halves = F // 2
    ladder = jnp.arange(halves).astype(jnp.float32) / max(halves - 1, 1)
    lifetimes = jnp.exp(ladder * math.log(length))
    decays = jnp.exp(-jnp.abs(offsets)[:, None] * (math.log(2.0) / lifetimes)[None, :])
    return jnp.concatenate([decays, jnp.sign(offsets)[:, None] * decays], axis=1)

def unpack(flat):
    limits = segment_ends()
    pieces = []
    opening = 0
    for finish in limits:
        pieces.append(flat[opening:finish])
        opening = finish
    return (pieces[0].reshape(D, H, KD), pieces[1].reshape(D, H, KD), pieces[2].reshape(D, H, VD), pieces[3].reshape(H, VD, D), pieces[4].reshape(D, FF), pieces[5].reshape(FF, D), pieces[6].reshape(D, D), pieces[7].reshape(F, H), pieces[8], pieces[9].reshape(12, D))

def layer_norm(inputs, norm_gain, norm_bias):
    centered = inputs - lax.optimization_barrier(jnp.mean(inputs, axis=-1, keepdims=True))
    variance = lax.optimization_barrier(jnp.mean(centered * centered, axis=-1, keepdims=True))
    return centered * lax.rsqrt(variance + eps_norm) * norm_gain + norm_bias

def attend(queries, key_rows, value_rows, tables):
    length = queries.shape[0]
    score_scale = 1.0 / math.sqrt(KD)
    columns = jnp.arange(length).astype(jnp.int32)

    def one_block(first_row):
        query_rows = lax.dynamic_slice_in_dim(queries, first_row, QB, 0)
        rows_here = first_row + jnp.arange(QB).astype(jnp.int32)
        offsets = rows_here[:, None] - columns[None, :] + (length - 1)
        biases = jnp.transpose(tables[offsets], (2, 0, 1))
        scores = jnp.einsum('qhk,lhk->hql', query_rows, key_rows, precision=highest) * score_scale + biases
        scores = low_back(scores)
        soft_max = low(jax.nn.softmax(scores, axis=-1))
        return jnp.einsum('hql,lhv->qhv', soft_max, value_rows, precision=highest)
    starts = (jnp.arange(length // QB) * QB).astype(jnp.int32)
    blocks = lax.map(jax.checkpoint(one_block), starts)
    return blocks.reshape(length, H, VD)

def forward(flat, inputs_all, skip_all, species):
    rounded = low(flat)
    w_query, w_key, w_value, w_out, w_up, w_down, w_point, pos_weight, up_bias, vectors = unpack(rounded)
    length = inputs_all.shape[1]
    tables = jnp.dot(position_basis(length), pos_weight, precision=highest)

    def window(carry, window_in):
        inputs, skip_rows, species_id = window_in
        normed_one = low(layer_norm(inputs, vectors[0], vectors[1]))
        queries = low_back(low(jnp.einsum('ld,dhk->lhk', normed_one, w_query, precision=highest)))
        key_rows = low_back(low(jnp.einsum('ld,dhk->lhk', normed_one, w_key, precision=highest)))
        value_rows = low_back(low(jnp.einsum('ld,dhv->lhv', normed_one, w_value, precision=highest)))
        heads = low_back(low(attend(queries, key_rows, value_rows, tables)))
        attention = low_back(jnp.einsum('lhv,hvd->ld', heads, w_out, precision=highest) + vectors[4])
        hidden_one = inputs + attention
        normed_two = low(layer_norm(hidden_one, vectors[2], vectors[3]))
        before = low_back(jnp.dot(normed_two, w_up, precision=highest) + up_bias)
        activated = low(jax.nn.gelu(before, approximate=False))
        branch = low_back(jnp.dot(activated, w_down, precision=highest) + vectors[5])
        hidden_two = hidden_one + branch
        summed = jnp.repeat(hidden_two, 2, axis=0) + skip_rows
        summed_low = low(summed)
        padded = jnp.pad(summed_low, ((1, 1), (0, 0)))
        convolved = vectors[7] * padded[:-2] + vectors[8] * padded[1:-1] + vectors[9] * padded[2:]
        convolved = low_back(low(convolved))
        pointed = low_back(jnp.dot(convolved, w_point, precision=highest) + vectors[6])
        species_gain = jnp.where(species_id == 1, vectors[11], vectors[10])
        return (carry, summed + species_gain * pointed)
    start_carry = jnp.zeros((), jnp.float32)
    _, outputs = lax.scan(jax.checkpoint(window), start_carry, (inputs_all, skip_all, species))
    return outputs

def reference(block_input, skip_input, species, cotangent, params, first_moment, second_moment):
    inputs_all = block_input.astype(jnp.float32)
    skip_all = skip_input.astype(jnp.float32)

    def wrapped(flat, inputs, skip_rows):
        return forward(flat, inputs, skip_rows, species)
    outputs, pullback = jax.vjp(wrapped, params, inputs_all, skip_all)
    grad_params, grad_input, grad_skip = pullback(cotangent.astype(jnp.float32))
    position = jnp.arange(params.shape[0]).astype(jnp.int32)
    param_new, first_new, second_new = adam_update(params, first_moment, second_moment, grad_params, position)
    return (outputs.astype(jnp.bfloat16), grad_input, grad_skip, param_new, first_new, second_new, param_new.astype(jnp.bfloat16))
```

```python
import functools
import math

import jax
import jax.numpy as jnp
from jax import lax
from jax.experimental import pallas as pl
from jax.experimental.pallas import tpu as pltpu
from jax.sharding import PartitionSpec as P

D = 1536
H = 8
KD = 64
VD = 192
FF = 3072
F = 192
STEP = 10
BLOCK = 256
ROWS = 11776
QKV_ROWS = 2560
TAIL = 24576
MARGIN = 320


eps_norm = 1e-05
beta_one = 0.5
beta_two = 0.5
adam_eps = 1e-08
decay_rate = 0.01
highest = lax.Precision.HIGHEST


def padded_2(array, sides, width):
    for axis, dim in sides:
        devices, length = (lax.axis_size(axis), array.shape[dim])
        up = [(i, (i + 1) % devices) for i in range(devices - 1)]
        down = [(j, i) for i, j in up]
        last = lax.slice_in_dim(array, length - width, length, axis=dim)
        initial = lax.slice_in_dim(array, 0, width, axis=dim)
        before = lax.ppermute(last, axis, up)
        after = lax.ppermute(initial, axis, down)
        array = jnp.concatenate([before, array, after], axis=dim)
    return array


def segment_ends():
    counts = [
        D * H * KD,
        D * H * KD,
        D * H * VD,
        H * VD * D,
        D * FF,
        FF * D,
        D * D,
        F * H,
        FF,
        12 * D,
    ]
    limits = []
    running = 0
    for amount in counts:
        running = running + amount
        limits.append(running)
    return limits


def rate_at(position):
    limits = segment_ends()
    step_rates = [
        2.0 / math.sqrt(D),
        2.0 / math.sqrt(D),
        2.0 / math.sqrt(D),
        8.0 / math.sqrt(H * VD),
        2.0 / math.sqrt(D),
        2.0 / math.sqrt(FF),
        2.0 / math.sqrt(D),
        3.0 / math.sqrt(F),
        0.4,
        0.4,
    ]
    result = jnp.full(position.shape, step_rates[-1], jnp.float32)
    for segment in range(len(limits) - 2, -1, -1):
        result = jnp.where(position < limits[segment], step_rates[segment], result)
    return result


def adam_update(param_old, first_old, second_old, gradient, position):
    step_rate = rate_at(position)
    first_new = beta_one * first_old + (1.0 - beta_one) * gradient
    second_new = beta_two * second_old + (1.0 - beta_two) * gradient * gradient
    first_hat = first_new / (1.0 - beta_one**STEP)
    second_hat = second_new / (1.0 - beta_two**STEP)
    param_new = param_old - step_rate * (
        first_hat / (jnp.sqrt(second_hat) + adam_eps) + decay_rate * param_old
    )
    return (param_new, first_new, second_new)


def position_basis(length):
    offsets = jnp.arange(2 * length - 1).astype(jnp.float32) - (length - 1)
    halves = F // 2
    ladder = jnp.arange(halves).astype(jnp.float32) / max(halves - 1, 1)
    lifetimes = jnp.exp(ladder * math.log(length))
    decays = jnp.exp(-jnp.abs(offsets)[:, None] * (math.log(2.0) / lifetimes)[None, :])
    return jnp.concatenate([decays, jnp.sign(offsets)[:, None] * decays], axis=1)


def layer_stats(inputs, norm_gain, norm_bias):
    centered = inputs - jnp.mean(inputs, axis=-1, keepdims=True)
    inverse = lax.rsqrt(jnp.mean(centered * centered, axis=-1, keepdims=True) + eps_norm)
    normed = centered * inverse
    return (normed * norm_gain + norm_bias, normed, inverse)


def norm_back(upstream, normed, inverse, norm_gain):
    scaled = upstream * norm_gain
    return inverse * (
        scaled
        - jnp.mean(scaled, axis=-1, keepdims=True)
        - normed * jnp.mean(scaled * normed, axis=-1, keepdims=True)
    )


def gelu_slope(before):
    return 0.5 * (1.0 + lax.erf(before * (1.0 / math.sqrt(2.0)))) + before * jnp.exp(
        -0.5 * before * before
    ) * (1.0 / math.sqrt(2.0 * math.pi))


def spread_rows(first_row, bands):
    start = pltpu.roll(first_row, 0, 1, stride=1, stride_axis=0)
    bands[0:8, :] = start
    height = 8
    while height < BLOCK:
        bands[height : 2 * height, :] = pltpu.roll(bands[0:height, :], height, 1)
        height *= 2


def collect_rows(bands, width):
    height = BLOCK // 2
    while height >= 8:
        bands[0:height, :] = bands[0:height, :] + pltpu.roll(
            bands[height : 2 * height, :], width - height, 1
        )
        height //= 2
    total = bands[0:1, :]
    for row in range(1, 8):
        total = total + pltpu.roll(bands[row : row + 1, :], width - row, 1)
    return total


def forward_kernel(table_ref, q_ref, k_ref, v_ref, out_ref, lse_ref, bands, scores, *, blocks):
    block = pl.program_id(0)

    @pl.when(block == 0)
    def _():
        spread_rows(table_ref[...], bands)

    queries = q_ref[...]
    top = jnp.full((1, BLOCK), -jnp.inf, jnp.float32)
    for j in range(blocks):
        at = pl.multiple_of((block - j + blocks - 1) * BLOCK, BLOCK)
        part = (
            jnp.dot(
                k_ref[j * BLOCK : (j + 1) * BLOCK, :], queries, preferred_element_type=jnp.float32
            )
            + bands[:, pl.ds(at, BLOCK)]
        )
        scores[j * BLOCK : (j + 1) * BLOCK, :] = part
        top = jnp.maximum(top, jnp.max(part, axis=0, keepdims=True))
    total = jnp.zeros((1, BLOCK), jnp.float32)
    result = jnp.zeros((VD, BLOCK), jnp.float32)
    for j in range(blocks):
        grown = jnp.exp(scores[j * BLOCK : (j + 1) * BLOCK, :] - top)
        total = total + jnp.sum(grown, axis=0, keepdims=True)
        result = result + jnp.dot(
            v_ref[:, j * BLOCK : (j + 1) * BLOCK],
            grown.astype(jnp.bfloat16),
            preferred_element_type=jnp.float32,
        )
    result = (result * (1.0 / total)).astype(jnp.bfloat16)
    for part in range(BLOCK // 128):
        out_ref[part] = result[:, part * 128 : (part + 1) * 128]
    lse_ref[...] = top + jnp.log(total)


def attention_forward(table, queries, key_rows, values):
    length = key_rows.shape[0]
    blocks = length // BLOCK
    parts = BLOCK // 128
    return pl.pallas_call(
        functools.partial(forward_kernel, blocks=blocks),
        grid=(blocks,),
        in_specs=[
            pl.BlockSpec((8, 2 * length), lambda i: (0, 0)),
            pl.BlockSpec((KD, BLOCK), lambda i: (0, i)),
            pl.BlockSpec((length, KD), lambda i: (0, 0)),
            pl.BlockSpec((VD, length), lambda i: (0, 0)),
        ],
        out_specs=[
            pl.BlockSpec((parts, VD, 128), lambda i: (i, 0, 0)),
            pl.BlockSpec((1, BLOCK), lambda i: (0, i)),
        ],
        out_shape=[
            jax.ShapeDtypeStruct((length // 128, VD, 128), jnp.bfloat16),
            jax.ShapeDtypeStruct((1, length), jnp.float32),
        ],
        scratch_shapes=[
            pltpu.VMEM((BLOCK, 2 * length), jnp.float32),
            pltpu.VMEM((length, BLOCK), jnp.float32),
        ],
        compiler_params=pltpu.CompilerParams(vmem_limit_bytes=40 * 2**20),
        cost_estimate=pl.CostEstimate(
            flops=4 * length * length * 256,
            bytes_accessed=8 * length * (KD + VD),
            transcendentals=length * length,
        ),
    )(table, queries, key_rows, values)


def backward_kernel(
    table_ref,
    q_ref,
    k_ref,
    kt_ref,
    v_ref,
    out_ref,
    grad_ref,
    lse_ref,
    dq_ref,
    dk_ref,
    dv_ref,
    dt_ref,
    bands,
    grad_bands,
    dk_sum,
    dv_sum,
    *,
    blocks,
):
    block = pl.program_id(0)

    @pl.when(block == 0)
    def _():
        spread_rows(table_ref[...], bands)
        grad_bands[...] = jnp.zeros_like(grad_bands)
        dk_sum[...] = jnp.zeros_like(dk_sum)
        dv_sum[...] = jnp.zeros_like(dv_sum)

    parts = BLOCK // 128
    grad_t = jnp.concatenate([grad_ref[part] for part in range(parts)], axis=1)
    out_t = jnp.concatenate([out_ref[part] for part in range(parts)], axis=1)
    delta = jnp.sum(
        grad_t.astype(jnp.float32) * out_t.astype(jnp.float32), axis=0, keepdims=True
    )
    grad_rows = grad_t.T
    queries = q_ref[...]
    query_rows = queries.T
    lse = lse_ref[...]
    dq = jnp.zeros((KD, BLOCK), jnp.float32)
    for j in range(blocks):
        span = slice(j * BLOCK, (j + 1) * BLOCK)
        at = pl.multiple_of((block - j + blocks - 1) * BLOCK, BLOCK)
        part = (
            jnp.dot(k_ref[span, :], queries, preferred_element_type=jnp.float32)
            + bands[:, pl.ds(at, BLOCK)]
        )
        soft = jnp.exp(part - lse)
        grad_soft = jnp.dot(v_ref[span, :], grad_t, preferred_element_type=jnp.float32)
        grad_scores = soft * (grad_soft - delta)
        grad_bands[:, pl.ds(at, BLOCK)] = grad_bands[:, pl.ds(at, BLOCK)] + grad_scores
        low = grad_scores.astype(jnp.bfloat16)
        dv_sum[span, :] = dv_sum[span, :] + jnp.dot(
            soft.astype(jnp.bfloat16), grad_rows, preferred_element_type=jnp.float32
        )
        dk_sum[span, :] = dk_sum[span, :] + jnp.dot(
            low, query_rows, preferred_element_type=jnp.float32
        )
        dq = dq + jnp.dot(kt_ref[:, span], low, preferred_element_type=jnp.float32)
    dq_ref[...] = (dq * (1.0 / math.sqrt(KD))).astype(jnp.bfloat16)

    @pl.when(block == blocks - 1)
    def _():
        dk_ref[...] = dk_sum[...].astype(jnp.bfloat16)
        dv_ref[...] = dv_sum[...].astype(jnp.bfloat16)
        dt_ref[...] = collect_rows(grad_bands, grad_bands.shape[1])


def attention_backward(table, queries, key_rows, keys, value_rows, heads, grad_heads, lse):
    length = key_rows.shape[0]
    blocks = length // BLOCK
    parts = BLOCK // 128
    return pl.pallas_call(
        functools.partial(backward_kernel, blocks=blocks),
        grid=(blocks,),
        in_specs=[
            pl.BlockSpec((8, 2 * length), lambda i: (0, 0)),
            pl.BlockSpec((KD, BLOCK), lambda i: (0, i)),
            pl.BlockSpec((length, KD), lambda i: (0, 0)),
            pl.BlockSpec((KD, length), lambda i: (0, 0)),
            pl.BlockSpec((length, VD), lambda i: (0, 0)),
            pl.BlockSpec((parts, VD, 128), lambda i: (i, 0, 0)),
            pl.BlockSpec((parts, VD, 128), lambda i: (i, 0, 0)),
            pl.BlockSpec((1, BLOCK), lambda i: (0, i)),
        ],
        out_specs=[
            pl.BlockSpec((KD, BLOCK), lambda i: (0, i)),
            pl.BlockSpec((length, KD), lambda i: (0, 0)),
            pl.BlockSpec((length, VD), lambda i: (0, 0)),
            pl.BlockSpec((1, 2 * length), lambda i: (0, 0)),
        ],
        out_shape=[
            jax.ShapeDtypeStruct((KD, length), jnp.bfloat16),
            jax.ShapeDtypeStruct((length, KD), jnp.bfloat16),
            jax.ShapeDtypeStruct((length, VD), jnp.bfloat16),
            jax.ShapeDtypeStruct((1, 2 * length), jnp.float32),
        ],
        scratch_shapes=[
            pltpu.VMEM((BLOCK, 2 * length), jnp.float32),
            pltpu.VMEM((BLOCK, 2 * length), jnp.float32),
            pltpu.VMEM((length, KD), jnp.float32),
            pltpu.VMEM((length, VD), jnp.float32),
        ],
        compiler_params=pltpu.CompilerParams(vmem_limit_bytes=48 * 2**20),
        cost_estimate=pl.CostEstimate(
            flops=10 * length * length * 256,
            bytes_accessed=16 * length * (KD + VD),
            transcendentals=length * length,
        ),
    )(table, queries, key_rows, keys, value_rows, heads, grad_heads, lse)


def ordered(own, other, is_first, axis):
    return jnp.concatenate(
        [jnp.where(is_first, own, other), jnp.where(is_first, other, own)], axis=axis
    )


class Places:
    def __init__(self, windows, local_rows):
        self.dp = lax.axis_size("dp")
        self.seq = lax.axis_size("seq")
        self.windows = windows
        self.rows = local_rows
        self.length = local_rows * self.seq
        self.group = self.seq // (2 * windows)
        self.heads = H // (2 * self.group)
        self.core = lax.axis_index("dp") % 2
        self.is_first = self.core == 0
        self.place = lax.axis_index("seq") % self.group
        self.part = self.rows // (2 * self.group)
        self.head_start = (self.core * self.group + self.place) * self.heads

    def swap(self, array):
        return lax.ppermute(array, "dp", [(i, i ^ 1) for i in range(self.dp)])

    def rows_to_windows(self, own):
        kept, sent = own
        return ordered(kept, self.swap(sent), self.is_first, 0)

    def halves(self, array, axis):
        size = array.shape[axis] // 2
        kept = lax.dynamic_slice_in_dim(array, self.core * size, size, axis)
        sent = lax.dynamic_slice_in_dim(array, (1 - self.core) * size, size, axis)
        return (kept, sent)

    def exchange(self, array):
        return lax.all_to_all(array, "seq", split_axis=0, concat_axis=0, tiled=True)

    def inputs_to_windows(self, inputs):
        features = inputs.shape[2]
        both = self.rows_to_windows(self.halves(inputs, 1))
        return self.exchange(both.reshape(self.seq, self.part, features))

    def gather_rows(self, array):
        features = array.shape[2]
        array = array[:, None]
        if self.group > 1:
            hops = [
                (i, i - i % self.group + (i + 1) % self.group) for i in range(self.seq)
            ]
            pieces = [array]
            for _ in range(self.group - 1):
                pieces.append(lax.ppermute(pieces[-1], "seq", hops))
            pieces = jnp.concatenate(pieces, axis=1)
            order = (self.place - jnp.arange(self.group)) % self.group
            array = jnp.take(pieces, order, axis=1)
        array = ordered(
            array[:, None], self.swap(array)[:, None], self.is_first, 1
        )
        return array.reshape(self.length, features)

    def sum_rows(self, partial):
        features = partial.shape[1]
        partial = partial.reshape(self.seq, 2, self.group * self.part, features)
        kept, sent = self.halves(partial, 1)
        total = kept[:, 0].astype(jnp.float32) + self.swap(
            sent[:, 0].astype(jnp.bfloat16)
        ).astype(jnp.float32)
        if self.group > 1:
            total = lax.psum_scatter(
                total.reshape(self.seq, self.group, self.part, features),
                "seq",
                scatter_dimension=1,
                axis_index_groups=[
                    list(range(i, i + self.group)) for i in range(0, self.seq, self.group)
                ],
                tiled=True,
            )
            total = total[:, 0]
        return total.astype(jnp.bfloat16)

    def sums_to_rows(self, array):
        features = array.shape[2]
        back = self.exchange(array).reshape(2 * self.windows, self.group * self.part, features)
        kept, sent = self.halves(back, 0)
        return ordered(kept, self.swap(sent), self.is_first, 1)

    def heads_to_rows(self, chunk):
        count = chunk.shape[1]
        back = self.exchange(chunk).reshape(
            2 * self.windows, 1, self.group, count, VD, self.rows
        )
        kept, sent = self.halves(back, 0)
        return ordered(kept, self.swap(sent), self.is_first, 1)

    def rows_to_heads(self, chunk):
        count = chunk.shape[3]
        kept, sent = self.halves(chunk, 1)
        both = self.rows_to_windows((kept[:, 0], sent[:, 0]))
        return self.exchange(both.reshape(self.seq, count, VD, self.rows))

    def to_lanes(self, array):
        if self.rows == 128:
            return array
        together = 128 // self.rows
        array = array.reshape(self.seq // together, together, VD, self.rows)
        return jnp.swapaxes(array, 1, 2).reshape(self.seq // together, VD, 128)

    def from_lanes(self, array):
        if self.rows == 128:
            return array
        together = 128 // self.rows
        array = array.reshape(self.seq // together, VD, together, self.rows)
        return jnp.swapaxes(array, 1, 2).reshape(self.seq, VD, self.rows)


def gather_weights(params):
    devices = lax.axis_size(("dp", "seq"))
    index = lax.axis_index(("dp", "seq"))
    dp, seq = lax.axis_size("dp"), lax.axis_size("seq")
    shard = params.shape[0]
    own_rows = ROWS // devices
    extra = shard - own_rows * D
    rest = extra * devices
    tail = params[shard - TAIL :].astype(jnp.bfloat16)
    before = lax.ppermute(tail, ("dp", "seq"), [(i, i + 1) for i in range(devices - 1)])
    joined = jnp.concatenate([before.astype(jnp.float32), params])
    piece = lax.dynamic_slice_in_dim(joined, TAIL - extra * index, own_rows * D)
    piece = piece.astype(jnp.bfloat16).reshape(own_rows, D)
    tail = tail.reshape(TAIL // D, D)
    owners = -(-QKV_ROWS // own_rows)
    if dp == 2 and 2 * owners <= seq and own_rows == 368:
        other = lax.ppermute(
            piece[176:368], ("dp", "seq"), [(i, i + seq) for i in range(owners)]
        )
        half = jnp.where(lax.axis_index("dp") == 0, piece[:192], other)
        hop = seq // 2
        far = lax.ppermute(half[96:], "seq", [(i, i + hop) for i in range(owners)])
        quarter = jnp.where(lax.axis_index("seq") < hop, half[:96], far)
        spread = lax.all_gather(
            jnp.concatenate([quarter, tail]), ("dp", "seq"), axis=0, tiled=True
        ).reshape(2, 2, hop, 112, D)
        special = spread[1, 1, hop - 1, 96:]
        spread = spread[:, :, :owners, :96]
        early = jnp.concatenate(
            [spread[0, 0], spread[0, 1], spread[1, 0, :, 16:], spread[1, 1]], axis=1
        ).reshape(owners * own_rows, D)
        everything = lax.all_gather(piece, ("dp", "seq"), axis=0, tiled=True)
    else:
        everything = lax.all_gather(
            jnp.concatenate([piece, tail]), ("dp", "seq"), axis=0
        )
        special = everything[-1, own_rows:]
        everything = everything[:, :own_rows].reshape(ROWS, D)
        early = everything
    special = special.astype(jnp.float32).reshape(-1)[TAIL - rest :]
    return (early, everything, special)


def sum_everywhere(array):
    for axis in ("dp", "seq"):
        devices, step = (lax.axis_size(axis), 1)
        while step < devices:
            array = array + lax.ppermute(array, axis, [(i, i ^ step) for i in range(devices)])
            step *= 2
    return array


def scatter_sums(rows):
    return lax.psum_scatter(rows, ("dp", "seq"), scatter_dimension=0, tiled=True)


def to_owners(buffer, piece, first):
    devices = lax.axis_size(("dp", "seq"))
    index = lax.axis_index(("dp", "seq"))
    own_rows = ROWS // devices
    count = piece.shape[0]
    rounds = {}
    for i in range(devices):
        low, high = (own_rows * i, own_rows * (i + 1) + TAIL // D)
        nearest = (low - first) // count
        for t in range(max(nearest, 0), devices):
            if first + count * t < high and first + count * (t + 1) > low:
                rounds.setdefault(t - nearest, []).append((t, i))
    for pairs in rounds.values():
        moved = lax.ppermute(piece, ("dp", "seq"), pairs)
        places = [0] * devices
        for source, i in pairs:
            places[i] = MARGIN + first + count * source - own_rows * i
        place = jnp.array(places, jnp.int32)[index]
        buffer = lax.dynamic_update_slice_in_dim(buffer, moved, place, 0)
    return buffer


def own_entries(buffer, special):
    devices = lax.axis_size(("dp", "seq"))
    index = lax.axis_index(("dp", "seq"))
    own_rows = ROWS // devices
    rest = special.shape[0]
    extra = rest // devices
    held = buffer[MARGIN : MARGIN + own_rows + TAIL // D].astype(jnp.float32)
    after = held[own_rows:].reshape(-1)
    after = jnp.where(index == devices - 1, jnp.pad(special, (0, TAIL - rest)), after)
    joined = jnp.concatenate([held[:own_rows].reshape(-1), after])
    return lax.dynamic_slice_in_dim(joined, extra * index, own_rows * D + extra)


def body(block_input, skip_input, species, cotangent, params, first_moment, second_moment):
    windows, local_rows, _ = block_input.shape
    at = Places(windows, local_rows)
    length = at.length
    own = at.heads
    scale = 1.0 / math.sqrt(KD)
    f32, bf16 = jnp.float32, jnp.bfloat16

    moved = at.inputs_to_windows(block_input)
    early, everything, special = gather_weights(params)
    pos_low = special[: F * H].reshape(F, H)
    up_bias = special[F * H : F * H + FF]
    vectors = special[F * H + FF :].reshape(12, D)

    def columns(matrix, width):
        return lax.dynamic_slice_in_dim(matrix, at.head_start * width, own * width, 1)

    w_query = columns(early[:512].reshape(D, H * KD), KD)
    w_key = columns(early[512:1024].reshape(D, H * KD), KD)
    w_value = columns(early[1024:2560].reshape(D, H * VD), VD)
    w_out = everything[2560:4096]
    w_up = everything[4096:7168].reshape(D, FF)
    w_down = everything[7168:10240]
    w_point = everything[10240:11776]

    pos_basis = position_basis(length)
    own_pos = lax.dynamic_slice_in_dim(pos_low, at.head_start, own, 1)
    tables = jnp.dot(own_pos.T, pos_basis.T, precision=highest)
    tables = jnp.roll(jnp.pad(tables, ((0, 0), (0, 1))), 1 - BLOCK, axis=1)
    tables = jnp.broadcast_to(tables[:, None, :], (own, 8, 2 * length))

    low_part, _, _ = layer_stats(moved.astype(f32), vectors[0], vectors[1])
    low_all = at.gather_rows(low_part.astype(bf16))
    queries = (
        jnp.einsum("rd,dk->kr", low_all, w_query, preferred_element_type=f32) * scale
    ).astype(bf16)
    keys = jnp.einsum("rd,dk->kr", low_all, w_key, preferred_element_type=f32).astype(bf16)
    values = jnp.einsum("rd,dk->kr", low_all, w_value, preferred_element_type=f32).astype(bf16)
    queries = queries.reshape(own, KD, length)
    keys = keys.reshape(own, KD, length)
    values = values.reshape(own, VD, length)
    key_rows = jnp.swapaxes(keys, 1, 2)
    value_rows = jnp.swapaxes(values, 1, 2)

    heads_out, lse, chunks = ([], [], [])
    for head in range(own):
        result, log_total = attention_forward(
            tables[head], queries[head], key_rows[head], values[head]
        )
        heads_out.append(result)
        lse.append(log_total)
        chunks.append(at.heads_to_rows(at.from_lanes(result)[:, None]))
    heads = jnp.concatenate(chunks, axis=3).reshape(windows, H * VD, local_rows)

    inputs = block_input.astype(f32)
    _, stats_one, inverse_one = layer_stats(inputs, vectors[0], vectors[1])
    attention = jnp.einsum("wcr,cd->wrd", heads, w_out, preferred_element_type=f32) + vectors[4]
    hidden_one = inputs + attention
    normed_two, stats_two, inverse_two = layer_stats(hidden_one, vectors[2], vectors[3])
    low_two = normed_two.astype(bf16)
    before = jnp.einsum("wrd,df->wrf", low_two, w_up, preferred_element_type=f32) + up_bias
    activated = jax.nn.gelu(before, approximate=False).astype(bf16)
    hidden_two = hidden_one + (
        jnp.einsum("wrf,fd->wrd", activated, w_down, preferred_element_type=f32) + vectors[5]
    )
    summed = jnp.repeat(hidden_two, 2, axis=1) + skip_input.astype(f32)
    padded = padded_2(summed.astype(bf16), (("seq", 1),), 1)
    convolved = (
        vectors[7] * padded[:, :-2] + vectors[8] * padded[:, 1:-1] + vectors[9] * padded[:, 2:]
    )
    conv_low = convolved.astype(bf16)
    pointed = jnp.einsum("wrd,de->wre", conv_low, w_point, preferred_element_type=f32) + vectors[6]
    is_mouse = (species == 1).astype(f32)[:, None]
    species_gain = (1.0 - is_mouse) * vectors[10] + is_mouse * vectors[11]
    block_out = (summed + species_gain[:, None, :] * pointed).astype(bf16)

    upstream = cotangent.astype(f32)
    grad_point = (species_gain[:, None, :] * upstream).astype(bf16)
    gain_rows = jnp.sum(upstream * pointed, axis=1)
    grad_human = jnp.sum((1.0 - is_mouse) * gain_rows, axis=0)
    grad_mouse = jnp.sum(is_mouse * gain_rows, axis=0)
    grad_w_point = jnp.einsum("wrd,wre->de", conv_low, grad_point, preferred_element_type=f32)
    grad_point_bias = jnp.sum(grad_point.astype(f32), axis=(0, 1))
    grad_conv = jnp.einsum("wre,de->wrd", grad_point, w_point, preferred_element_type=f32)
    grad_conv = grad_conv.astype(bf16)
    grad_padded = padded_2(grad_conv, (("seq", 1),), 1)
    skip_grad = (
        upstream
        + vectors[7] * grad_padded[:, 2:]
        + vectors[8] * grad_padded[:, 1:-1]
        + vectors[9] * grad_padded[:, :-2]
    )
    grad_conv_wide = grad_conv.astype(f32)
    grad_tap_zero = jnp.sum(grad_conv_wide * padded[:, :-2], axis=(0, 1))
    grad_tap_one = jnp.sum(grad_conv_wide * padded[:, 1:-1], axis=(0, 1))
    grad_tap_two = jnp.sum(grad_conv_wide * padded[:, 2:], axis=(0, 1))
    grad_hidden = jnp.sum(skip_grad.reshape(windows, local_rows, 2, D), axis=2)
    grad_down_low = grad_hidden.astype(bf16)
    grad_w_down = jnp.einsum("wrf,wrd->fd", activated, grad_down_low, preferred_element_type=f32)
    grad_down_bias = jnp.sum(grad_down_low.astype(f32), axis=(0, 1))
    grad_active = jnp.einsum("wrd,fd->wrf", grad_down_low, w_down, preferred_element_type=f32)
    grad_before = (grad_active * gelu_slope(before)).astype(bf16)
    grad_w_up = jnp.einsum("wrd,wrf->df", low_two, grad_before, preferred_element_type=f32)
    grad_up_bias = jnp.sum(grad_before.astype(f32), axis=(0, 1))
    grad_norm_two = jnp.einsum("wrf,df->wrd", grad_before, w_up, preferred_element_type=f32)
    grad_mid = grad_hidden + norm_back(grad_norm_two, stats_two, inverse_two, vectors[2])
    grad_gain_two = jnp.sum(grad_norm_two * stats_two, axis=(0, 1))
    grad_bias_two = jnp.sum(grad_norm_two, axis=(0, 1))
    grad_attn_low = grad_mid.astype(bf16)
    grad_w_out = jnp.einsum("wcr,wrd->cd", heads, grad_attn_low, preferred_element_type=f32)
    grad_out_bias = jnp.sum(grad_attn_low.astype(f32), axis=(0, 1))
    grad_heads = jnp.einsum("wrd,cd->wcr", grad_attn_low, w_out, preferred_element_type=f32)
    grad_heads = grad_heads.astype(bf16).reshape(windows, 2, at.group, own, VD, local_rows)

    middle = jnp.concatenate(
        [
            grad_up_bias,
            grad_gain_two,
            grad_bias_two,
            grad_out_bias,
            grad_down_bias,
            grad_point_bias,
            grad_tap_zero,
            grad_tap_one,
            grad_tap_two,
            grad_human,
            grad_mouse,
        ]
    )
    middle = sum_everywhere(middle)
    later_rows = jnp.zeros((ROWS - QKV_ROWS, D), bf16)
    start = 0
    for matrix in (grad_w_out, grad_w_up, grad_w_down, grad_w_point):
        matrix = matrix.astype(bf16).reshape(-1, D)
        later_rows = lax.dynamic_update_slice_in_dim(later_rows, matrix, start, 0)
        start += matrix.shape[0]
    grad_heads = [grad_heads[:, :, :, head : head + 1] for head in range(own)]
    later_rows, grad_heads[1:] = lax.optimization_barrier((later_rows, grad_heads[1:]))
    own_rows = ROWS // lax.axis_size(("dp", "seq"))
    buffer = jnp.zeros((own_rows + TAIL // D + 2 * MARGIN, D), bf16)
    later_piece = scatter_sums(later_rows)

    dq, dk, dv, dt = ([], [], [], [])
    for head in range(own):
        chunk = at.rows_to_heads(grad_heads[head])
        pieces = attention_backward(
            tables[head],
            queries[head],
            key_rows[head],
            keys[head],
            value_rows[head],
            heads_out[head],
            at.to_lanes(chunk[:, 0]),
            lse[head],
        )
        for piece, held in zip(pieces, (dq, dk, dv, dt), strict=True):
            held.append(piece)
    grad_query = jnp.concatenate(dq, axis=0)
    grad_key = jnp.concatenate(dk, axis=1)
    grad_value = jnp.concatenate(dv, axis=1)
    partial = (
        jnp.einsum("kr,dk->rd", grad_query, w_query, preferred_element_type=f32)
        + jnp.einsum("rk,dk->rd", grad_key, w_key, preferred_element_type=f32)
        + jnp.einsum("rk,dk->rd", grad_value, w_value, preferred_element_type=f32)
    )
    grad_norm_one = at.sums_to_rows(at.sum_rows(partial)).astype(f32)
    grad_w_query = jnp.einsum("rd,kr->dk", low_all, grad_query, preferred_element_type=f32)
    grad_w_key = jnp.einsum("rd,rk->dk", low_all, grad_key, preferred_element_type=f32)
    grad_w_value = jnp.einsum("rd,rk->dk", low_all, grad_value, preferred_element_type=f32)

    def all_columns(matrix, width):
        whole = jnp.zeros((D, H * width), bf16)
        return lax.dynamic_update_slice_in_dim(
            whole, matrix.astype(bf16), at.head_start * width, 1
        ).reshape(-1, D)

    input_grad = grad_mid + norm_back(grad_norm_one, stats_one, inverse_one, vectors[0])
    grad_gain_one = jnp.sum(grad_norm_one * stats_one, axis=(0, 1))
    grad_bias_one = jnp.sum(grad_norm_one, axis=(0, 1))
    grad_tables = jnp.roll(jnp.concatenate(dt, axis=0), BLOCK - 1, axis=1)[:, : 2 * length - 1]
    grad_pos = jnp.dot(pos_basis.T, grad_tables.T, precision=highest)
    grad_pos = lax.dynamic_update_slice_in_dim(
        jnp.zeros((F, H), f32), grad_pos, at.head_start, 1
    )
    late = jnp.concatenate([grad_pos.reshape(-1), grad_gain_one, grad_bias_one])
    late = sum_everywhere(late)
    special_grads = jnp.concatenate(
        [late[: F * H], middle[:FF], late[F * H :], middle[FF:]]
    )
    first_rows = jnp.concatenate(
        [
            all_columns(grad_w_query, KD),
            all_columns(grad_w_key, KD),
            all_columns(grad_w_value, VD),
        ],
        axis=0,
    )
    first_rows, later_piece = lax.optimization_barrier((first_rows, later_piece))
    buffer = to_owners(buffer, later_piece, QKV_ROWS)
    buffer = to_owners(buffer, scatter_sums(first_rows), 0)
    reduced = own_entries(buffer, special_grads)
    shard_len = params.shape[0]
    position = lax.axis_index(("dp", "seq")) * shard_len + jnp.arange(shard_len)
    param_new, first_new, second_new = adam_update(
        params, first_moment, second_moment, reduced, position
    )
    return (
        block_out,
        input_grad,
        skip_grad,
        param_new,
        first_new,
        second_new,
        param_new.astype(bf16),
    )


def solution(mesh):
    return jax.shard_map(
        body,
        mesh=mesh,
        in_specs=(
            P("dp", "seq", None),
            P("dp", "seq", None),
            P("dp"),
            P("dp", "seq", None),
            P(("dp", "seq")),
            P(("dp", "seq")),
            P(("dp", "seq")),
        ),
        out_specs=(
            P("dp", "seq", None),
            P("dp", "seq", None),
            P("dp", "seq", None),
            P(("dp", "seq")),
            P(("dp", "seq")),
            P(("dp", "seq")),
            P(("dp", "seq")),
        ),
        check_vma=False,
    )
```

```python
import functools
import math

import jax
import jax.numpy as jnp
from jax import lax
from jax.experimental import pallas as pl
from jax.experimental.pallas import tpu as pltpu
from jax.sharding import PartitionSpec as P

D = 1536
H = 8
KD = 64
VD = 192
FF = 3072
F = 192
STEP = 10
BLOCK = 256
PAIR = 2
CHUNK = 512
WIDE = 768
LANES = 128
ROWS = 11776
QKV_ROWS = 2560
TAIL = 24576
MARGIN = 288
UNIT = 16
UNITS = 288


eps_norm = 1e-05
beta_one = 0.5
beta_two = 0.5
adam_eps = 1e-08
decay_rate = 0.01
highest = lax.Precision.HIGHEST


def edge_rows(array):
    devices = lax.axis_size("seq")
    up = [(i, i + 1) for i in range(devices - 1)]
    first = lax.ppermute(array[1], "seq", up)
    last = lax.ppermute(array[0], "seq", [(j, i) for i, j in up])
    return (first, last)


def segment_ends():
    counts = [
        D * H * KD,
        D * H * KD,
        D * H * VD,
        H * VD * D,
        D * FF,
        FF * D,
        D * D,
        F * H,
        FF,
        12 * D,
    ]
    limits = []
    running = 0
    for amount in counts:
        running = running + amount
        limits.append(running)
    return limits


def rate_at(position):
    limits = segment_ends()
    step_rates = [
        2.0 / math.sqrt(D),
        2.0 / math.sqrt(D),
        2.0 / math.sqrt(D),
        8.0 / math.sqrt(H * VD),
        2.0 / math.sqrt(D),
        2.0 / math.sqrt(FF),
        2.0 / math.sqrt(D),
        3.0 / math.sqrt(F),
        0.4,
        0.4,
    ]
    result = jnp.full(position.shape, step_rates[-1], jnp.float32)
    for segment in range(len(limits) - 2, -1, -1):
        result = jnp.where(position < limits[segment], step_rates[segment], result)
    return result


def adam_update(param_old, first_old, second_old, gradient, position):
    step_rate = rate_at(position)
    first_new = beta_one * first_old + (1.0 - beta_one) * gradient
    second_new = beta_two * second_old + (1.0 - beta_two) * gradient * gradient
    first_hat = first_new / (1.0 - beta_one**STEP)
    second_hat = second_new / (1.0 - beta_two**STEP)
    param_new = param_old - step_rate * (
        first_hat / (jnp.sqrt(second_hat) + adam_eps) + decay_rate * param_old
    )
    return (param_new, first_new, second_new)


def position_basis(length):
    offsets = jnp.arange(2 * length - 1).astype(jnp.float32) - (length - 1)
    halves = F // 2
    ladder = jnp.arange(halves).astype(jnp.float32) / max(halves - 1, 1)
    lifetimes = jnp.exp(ladder * math.log(length))
    decays = jnp.exp(-jnp.abs(offsets)[:, None] * (math.log(2.0) / lifetimes)[None, :])
    return jnp.concatenate([decays, jnp.sign(offsets)[:, None] * decays], axis=1)


def layer_stats(inputs, norm_gain, norm_bias):
    centered = inputs - jnp.mean(inputs, axis=-1, keepdims=True)
    inverse = lax.rsqrt(jnp.mean(centered * centered, axis=-1, keepdims=True) + eps_norm)
    normed = centered * inverse
    return (normed * norm_gain + norm_bias, normed, inverse)


def norm_back(upstream, normed, inverse, norm_gain):
    scaled = upstream * norm_gain
    return inverse * (
        scaled
        - jnp.mean(scaled, axis=-1, keepdims=True)
        - normed * jnp.mean(scaled * normed, axis=-1, keepdims=True)
    )


def spread_rows(first_row, bands):
    start = pltpu.roll(first_row, 0, 1, stride=1, stride_axis=0)
    bands[0:8, :] = start
    height = 8
    while height < BLOCK:
        bands[height : 2 * height, :] = pltpu.roll(bands[0:height, :], height, 1)
        height *= 2


def collect_rows(bands, width):
    height = BLOCK // 2
    while height >= 8:
        bands[0:height, :] = bands[0:height, :] + pltpu.roll(
            bands[height : 2 * height, :], width - height, 1
        )
        height //= 2
    total = bands[0:1, :]
    for row in range(1, 8):
        total = total + pltpu.roll(bands[row : row + 1, :], width - row, 1)
    return total


def forward_kernel(
    table_ref, q_ref, k_ref, v_ref, out_ref, lse_ref, bands, key_rows, scores, *, blocks
):
    block = pl.program_id(0)

    @pl.when(block == 0)
    def _():
        for head in range(PAIR):
            spread_rows(table_ref[head], bands.at[head])
            key_rows[head] = k_ref[head * KD : (head + 1) * KD, :].T

    results = []
    for head in range(PAIR):
        queries = q_ref[head * KD : (head + 1) * KD, :]
        top = jnp.full((1, BLOCK), -jnp.inf, jnp.float32)
        for j in range(blocks):
            at = pl.multiple_of((block - j + blocks - 1) * BLOCK, BLOCK)
            span = slice(j * BLOCK, (j + 1) * BLOCK)
            part = (
                jnp.dot(key_rows[head, span, :], queries, preferred_element_type=jnp.float32)
                + bands[head, :, pl.ds(at, BLOCK)]
            )
            scores[span, :] = part
            top = jnp.maximum(top, jnp.max(part, axis=0, keepdims=True))
        total = jnp.zeros((1, BLOCK), jnp.float32)
        result = jnp.zeros((VD, BLOCK), jnp.float32)
        for j in range(blocks):
            span = slice(j * BLOCK, (j + 1) * BLOCK)
            grown = jnp.exp(scores[span, :] - top)
            total = total + jnp.sum(grown, axis=0, keepdims=True)
            result = result + jnp.dot(
                v_ref[head * VD : (head + 1) * VD, span],
                grown.astype(jnp.bfloat16),
                preferred_element_type=jnp.float32,
            )
        results.append(result * (1.0 / total))
        lse_ref[head : head + 1, :] = top + jnp.log(total)
    out_ref[...] = jnp.concatenate(results, axis=0).T.astype(jnp.bfloat16)


def attention_forward(tables, queries, keys, values):
    length = keys.shape[1]
    blocks = length // BLOCK
    return pl.pallas_call(
        functools.partial(forward_kernel, blocks=blocks),
        grid=(blocks,),
        in_specs=[
            pl.BlockSpec((PAIR, 8, 2 * length), lambda i: (0, 0, 0)),
            pl.BlockSpec((PAIR * KD, BLOCK), lambda i: (0, i)),
            pl.BlockSpec((PAIR * KD, length), lambda i: (0, 0)),
            pl.BlockSpec((PAIR * VD, length), lambda i: (0, 0)),
        ],
        out_specs=[
            pl.BlockSpec((BLOCK, PAIR * VD), lambda i: (i, 0)),
            pl.BlockSpec((PAIR, BLOCK), lambda i: (0, i)),
        ],
        out_shape=[
            jax.ShapeDtypeStruct((length, PAIR * VD), jnp.bfloat16),
            jax.ShapeDtypeStruct((PAIR, length), jnp.float32),
        ],
        scratch_shapes=[
            pltpu.VMEM((PAIR, BLOCK, 2 * length), jnp.float32),
            pltpu.VMEM((PAIR, length, KD), jnp.bfloat16),
            pltpu.VMEM((length, BLOCK), jnp.float32),
        ],
        compiler_params=pltpu.CompilerParams(vmem_limit_bytes=48 * 2**20),
        cost_estimate=pl.CostEstimate(
            flops=(4 * PAIR * length * length * 256) // 16,
            bytes_accessed=(8 * PAIR * length * (KD + VD)) // 16,
            transcendentals=PAIR * length * length // 16,
        ),
    )(tables, queries, keys, values)


def backward_kernel(
    table_ref,
    q_ref,
    k_ref,
    v_ref,
    out_ref,
    grad_ref,
    lse_ref,
    dq_ref,
    dk_ref,
    dv_ref,
    dt_ref,
    bands,
    grad_bands,
    key_rows,
    value_rows,
    dk_sum,
    dv_sum,
    *,
    blocks,
):
    block = pl.program_id(0)

    @pl.when(block == 0)
    def _():
        for head in range(PAIR):
            spread_rows(table_ref[head], bands.at[head])
            key_rows[head] = k_ref[head * KD : (head + 1) * KD, :].T
            value_rows[head] = v_ref[head * VD : (head + 1) * VD, :].T
        grad_bands[...] = jnp.zeros_like(grad_bands)
        dk_sum[...] = jnp.zeros_like(dk_sum)
        dv_sum[...] = jnp.zeros_like(dv_sum)

    grad_t = grad_ref[...].T
    out_t = out_ref[...].T
    products = grad_t.astype(jnp.float32) * out_t.astype(jnp.float32)
    results = []
    for head in range(PAIR):
        wide = slice(head * VD, (head + 1) * VD)
        delta = jnp.sum(products[wide, :], axis=0, keepdims=True)
        grad_here = grad_t[wide, :]
        grad_rows = grad_here.T
        queries = q_ref[head * KD : (head + 1) * KD, :]
        query_rows = queries.T
        lse = lse_ref[head : head + 1, :]
        dq = jnp.zeros((KD, BLOCK), jnp.float32)
        for j in range(blocks):
            span = slice(j * BLOCK, (j + 1) * BLOCK)
            at = pl.multiple_of((block - j + blocks - 1) * BLOCK, BLOCK)
            part = (
                jnp.dot(key_rows[head, span, :], queries, preferred_element_type=jnp.float32)
                + bands[head, :, pl.ds(at, BLOCK)]
            )
            soft = jnp.exp(part - lse)
            grad_soft = jnp.dot(
                value_rows[head, span, :], grad_here, preferred_element_type=jnp.float32
            )
            grad_scores = soft * (grad_soft - delta)
            grad_bands[head, :, pl.ds(at, BLOCK)] = (
                grad_bands[head, :, pl.ds(at, BLOCK)] + grad_scores
            )
            low = grad_scores.astype(jnp.bfloat16)
            dv_sum[head, span, :] = dv_sum[head, span, :] + jnp.dot(
                soft.astype(jnp.bfloat16), grad_rows, preferred_element_type=jnp.float32
            )
            dk_sum[head, span, :] = dk_sum[head, span, :] + jnp.dot(
                low, query_rows, preferred_element_type=jnp.float32
            )
            dq = dq + jnp.dot(
                k_ref[head * KD : (head + 1) * KD, span], low, preferred_element_type=jnp.float32
            )
        results.append(dq)
    dq_ref[...] = jnp.concatenate(results, axis=0).T.astype(jnp.bfloat16)

    @pl.when(block == blocks - 1)
    def _():
        dk_ref[...] = jnp.concatenate(
            [dk_sum[head] for head in range(PAIR)], axis=1
        ).astype(jnp.bfloat16)
        dv_ref[...] = jnp.concatenate(
            [dv_sum[head] for head in range(PAIR)], axis=1
        ).astype(jnp.bfloat16)
        for head in range(PAIR):
            dt_ref[head : head + 1, :] = collect_rows(
                grad_bands.at[head], grad_bands.shape[2]
            )


def attention_backward(tables, queries, keys, values, heads, grad_heads, lse):
    length = keys.shape[1]
    blocks = length // BLOCK
    return pl.pallas_call(
        functools.partial(backward_kernel, blocks=blocks),
        grid=(blocks,),
        in_specs=[
            pl.BlockSpec((PAIR, 8, 2 * length), lambda i: (0, 0, 0)),
            pl.BlockSpec((PAIR * KD, BLOCK), lambda i: (0, i)),
            pl.BlockSpec((PAIR * KD, length), lambda i: (0, 0)),
            pl.BlockSpec((PAIR * VD, length), lambda i: (0, 0)),
            pl.BlockSpec((BLOCK, PAIR * VD), lambda i: (i, 0)),
            pl.BlockSpec((BLOCK, PAIR * VD), lambda i: (i, 0)),
            pl.BlockSpec((PAIR, BLOCK), lambda i: (0, i)),
        ],
        out_specs=[
            pl.BlockSpec((BLOCK, PAIR * KD), lambda i: (i, 0)),
            pl.BlockSpec((length, PAIR * KD), lambda i: (0, 0)),
            pl.BlockSpec((length, PAIR * VD), lambda i: (0, 0)),
            pl.BlockSpec((PAIR, 2 * length), lambda i: (0, 0)),
        ],
        out_shape=[
            jax.ShapeDtypeStruct((length, PAIR * KD), jnp.bfloat16),
            jax.ShapeDtypeStruct((length, PAIR * KD), jnp.bfloat16),
            jax.ShapeDtypeStruct((length, PAIR * VD), jnp.bfloat16),
            jax.ShapeDtypeStruct((PAIR, 2 * length), jnp.float32),
        ],
        scratch_shapes=[
            pltpu.VMEM((PAIR, BLOCK, 2 * length), jnp.float32),
            pltpu.VMEM((PAIR, BLOCK, 2 * length), jnp.float32),
            pltpu.VMEM((PAIR, length, KD), jnp.bfloat16),
            pltpu.VMEM((PAIR, length, VD), jnp.bfloat16),
            pltpu.VMEM((PAIR, length, KD), jnp.float32),
            pltpu.VMEM((PAIR, length, VD), jnp.float32),
        ],
        compiler_params=pltpu.CompilerParams(vmem_limit_bytes=56 * 2**20),
        cost_estimate=pl.CostEstimate(
            flops=(10 * PAIR * length * length * 256) // 16,
            bytes_accessed=(16 * PAIR * length * (KD + VD)) // 16,
            transcendentals=PAIR * length * length // 16,
        ),
    )(tables, queries, keys, values, heads, grad_heads, lse)


def whole_block(array):
    zeros = (0,) * array.ndim
    return pl.BlockSpec(array.shape, lambda i: zeros, pipeline_mode=pl.Buffered(1))


LEFT, DOWN = ((96, 1, UNIT, D), (0, 0)), ((96, 2, UNIT, D), (1, 0))
OUT, POINT = ((48, 2, UNIT, D), (4, 0)), ((48, 2, UNIT, D), (5, 0))


def weight_block(weight):
    shape, place = weight
    return pl.BlockSpec(shape, lambda *i: place + (0, 0), pipeline_mode=pl.Buffered(1))


def up_half(half):
    return pl.BlockSpec(
        (96, 1, UNIT, D), lambda i: (0, half, 0, 0), pipeline_mode=pl.Buffered(1)
    )


def unit_rows(first, rows):
    first, units = (first // (2 * UNIT), rows // (2 * UNIT))
    return pl.BlockSpec(
        (pl.Element(units), pl.Element(2), pl.Element(UNIT), pl.Element(D)),
        lambda i: (first, 0, 0, 0),
        pipeline_mode=pl.Buffered(1),
    )


def up_units_kernel(lower_ref, upper_ref, out_ref, *, steps):
    units = out_ref.shape[0]

    def put(rows_ref):
        rows = rows_ref[...].astype(jnp.float32).reshape(units, 2, 2, 8, D)
        out_ref[...] = (
            jnp.swapaxes(rows, 1, 2).reshape(units, 2, UNIT, D).astype(jnp.bfloat16)
        )

    pl.when(pl.program_id(0) < steps)(lambda: put(lower_ref))
    pl.when(pl.program_id(0) >= steps)(lambda: put(upper_ref))


def up_units(lower, upper):
    units = 8
    start = UP_ROWS[0] // UNIT // (2 * units)
    steps = lower.shape[0] // (2 * units) - start
    return pl.pallas_call(
        functools.partial(up_units_kernel, steps=steps),
        grid=(96 // units,),
        in_specs=[
            pl.BlockSpec(
                (2 * units, UNIT, D), lambda i: (start + jnp.minimum(i, steps - 1), 0, 0)
            ),
            pl.BlockSpec((2 * units, UNIT, D), lambda i: (jnp.maximum(i - steps, 0), 0, 0)),
        ],
        out_specs=pl.BlockSpec((units, 2, UNIT, D), lambda i: (i, 0, 0, 0)),
        out_shape=jax.ShapeDtypeStruct((96, 2, UNIT, D), jnp.bfloat16),
        compiler_params=pltpu.CompilerParams(vmem_limit_bytes=32 * 2**20),
    )(lower, upper)


OUT_ROWS, UP_ROWS, DOWN_ROWS, POINT_ROWS = (2560, D), (4096, FF), (1280, FF), (4352, D)


def step_block(array, count):
    shape = (count,) + array.shape[1:]
    rest = (0,) * (array.ndim - 1)
    return pl.BlockSpec(shape, lambda i: (i,) + rest)


def times_transposed(left, right):
    return lax.dot_general(
        left, right, (((1,), (1,)), ((), ())), preferred_element_type=jnp.float32
    )


def dense_kernel(
    core_ref,
    inputs_ref,
    own_a,
    own_b,
    other_a,
    other_b,
    vectors_ref,
    up_bias_ref,
    w_out_ref,
    w_left_ref,
    w_right_ref,
    w_down_ref,
    heads_ref,
    hidden_ref,
    low_ref,
    active_ref,
    slope_ref,
    after_ref,
    *,
    count,
    rows,
):
    core = core_ref[0]
    total = count * rows
    width = own_a.shape[2]
    hidden = inputs_ref[...].reshape(total, D).astype(jnp.float32) + vectors_ref[4:5, :]
    for number, piece in enumerate((own_a, own_b, other_a, other_b)):
        group = core if number < 2 else 1 - core
        at = pl.multiple_of(group * (2 * width) + (number % 2) * width, 128)
        unit = group * 24 + (number % 2) * 12
        held = piece[...]
        heads_ref[:, :, pl.ds(at, width)] = held
        hidden = hidden + jnp.dot(
            held.reshape(total, width),
            w_out_ref[pl.ds(unit, 12)].reshape(width, D),
            preferred_element_type=jnp.float32,
        )
    hidden_ref[...] = hidden.reshape(count, rows, D)
    normed, _, _ = layer_stats(hidden, vectors_ref[2:3, :], vectors_ref[3:4, :])
    low = normed.astype(jnp.bfloat16)
    low_ref[...] = low.reshape(count, rows, D)
    after = hidden + vectors_ref[5:6, :]
    for number in range(FF // WIDE):
        span = slice(number * WIDE, (number + 1) * WIDE)
        half = (w_left_ref, w_right_ref)[number * WIDE // D]
        start = number * WIDE % D
        units = slice(number * WIDE // 32, (number + 1) * WIDE // 32)
        before = (
            jnp.dot(
                low,
                half[:, 0, :, start : start + WIDE].reshape(D, WIDE),
                preferred_element_type=jnp.float32,
            )
            + up_bias_ref[:, span]
        )
        phi = 0.5 * (1.0 + lax.erf(before * (1.0 / math.sqrt(2.0))))
        slope = phi + before * jnp.exp(-0.5 * before * before) * (1.0 / math.sqrt(2.0 * math.pi))
        active = (before * phi).astype(jnp.bfloat16)
        active_ref[:, :, span] = active.reshape(count, rows, WIDE)
        slope_ref[:, :, span] = slope.astype(jnp.bfloat16).reshape(count, rows, WIDE)
        after = after + jnp.dot(
            active, w_down_ref[units].reshape(WIDE, D), preferred_element_type=jnp.float32
        )
    after_ref[...] = after.reshape(count, rows, D)


def dense_forward(core, inputs, pieces, vectors, up_bias, weights):
    windows, rows, _ = inputs.shape
    count = max(1, 256 // rows)
    shapes = [
        jax.ShapeDtypeStruct((windows, rows, D), jnp.bfloat16),
        jax.ShapeDtypeStruct((windows, rows, D), jnp.float32),
        jax.ShapeDtypeStruct((windows, rows, D), jnp.bfloat16),
        jax.ShapeDtypeStruct((windows, rows, FF), jnp.bfloat16),
        jax.ShapeDtypeStruct((windows, rows, FF), jnp.bfloat16),
        jax.ShapeDtypeStruct((windows, rows, D), jnp.float32),
    ]
    lower, upper, w_up = weights
    return pl.pallas_call(
        functools.partial(dense_kernel, count=count, rows=rows),
        grid=(windows // count,),
        in_specs=[pl.BlockSpec(memory_space=pltpu.SMEM), step_block(inputs, count)]
        + [step_block(piece, count) for piece in pieces]
        + [whole_block(vectors), whole_block(up_bias)]
        + [unit_rows(*OUT_ROWS), up_half(0), up_half(1), unit_rows(*DOWN_ROWS)],
        out_specs=[step_block(shape, count) for shape in shapes],
        out_shape=shapes,
        compiler_params=pltpu.CompilerParams(vmem_limit_bytes=60 * 2**20),
        cost_estimate=pl.CostEstimate(
            flops=(2 * windows * rows * D * (D + 2 * FF)) // 16,
            bytes_accessed=(2 * D * (D + 2 * FF) + 26 * windows * rows * D) // 16,
            transcendentals=2 * windows * rows * FF // 16,
        ),
    )(core, inputs, *pieces, vectors, up_bias, lower, w_up, w_up, upper)


def shifted(rows, first, last):
    count = rows.shape[0]
    place = lax.broadcasted_iota(jnp.int32, rows.shape, 0)
    earlier = jnp.where(place == 0, first, pltpu.roll(rows, 1, 0))
    later = jnp.where(place == count - 1, last, pltpu.roll(rows, count - 1, 0))
    return (earlier, later)


def point_kernel(
    after_ref,
    skip_ref,
    upstream_ref,
    first_ref,
    last_ref,
    gain_ref,
    vectors_ref,
    w_ref,
    out_ref,
    grad_conv_ref,
    grad_w_ref,
    gain_rows_ref,
    sums_ref,
    doubled,
    summed,
    grad_w,
    *,
    rows,
):
    step = pl.program_id(0)

    @pl.when(step == 0)
    def _():
        grad_w[...] = jnp.zeros_like(grad_w)
        sums_ref[...] = jnp.zeros_like(sums_ref)

    for number in range(D // LANES):
        span = slice(number * LANES, (number + 1) * LANES)
        after = after_ref[0, :, span]
        doubled[number, pl.ds(0, rows, stride=2), :] = after
        doubled[number, pl.ds(1, rows, stride=2), :] = after
        summed[:, span] = doubled[number] + skip_ref[0, :, span].astype(jnp.float32)
    low = summed[...].astype(jnp.bfloat16).astype(jnp.float32)
    earlier, later = shifted(
        low, first_ref[0].astype(jnp.float32), last_ref[0].astype(jnp.float32)
    )
    conv = (
        vectors_ref[7:8, :] * earlier + vectors_ref[8:9, :] * low + vectors_ref[9:10, :] * later
    ).astype(jnp.bfloat16)
    conv_t = conv.T
    grad_conv = jnp.zeros((2 * rows, D), jnp.float32)
    for number in range(D // CHUNK):
        span = slice(number * CHUNK, (number + 1) * CHUNK)
        weight = w_ref[:, :, :, span].reshape(D, CHUNK)
        gain = gain_ref[0, :, span]
        upstream = upstream_ref[0, :, span].astype(jnp.float32)
        pointed = (
            jnp.dot(conv, weight, preferred_element_type=jnp.float32) + vectors_ref[6:7, span]
        )
        out_ref[0, :, span] = (summed[:, span] + gain * pointed).astype(jnp.bfloat16)
        gain_rows_ref[0, :, span] = jnp.sum(upstream * pointed, axis=0, keepdims=True)
        grad_point = (gain * upstream).astype(jnp.bfloat16)
        sums_ref[0:1, span] = sums_ref[0:1, span] + jnp.sum(
            grad_point.astype(jnp.float32), axis=0, keepdims=True
        )
        grad_conv = grad_conv + times_transposed(grad_point, weight)
        grad_w[:, span] = grad_w[:, span] + jnp.dot(
            conv_t, grad_point, preferred_element_type=jnp.float32
        )
    grad_low = grad_conv.astype(jnp.bfloat16)
    grad_conv_ref[0] = grad_low
    grad_wide = grad_low.astype(jnp.float32)
    for number, rows_here in enumerate((earlier, low, later)):
        sums_ref[number + 1 : number + 2, :] = sums_ref[number + 1 : number + 2, :] + jnp.sum(
            grad_wide * rows_here, axis=0, keepdims=True
        )

    @pl.when(step == pl.num_programs(0) - 1)
    def _():
        grad_w_ref[...] = grad_w[...].astype(jnp.bfloat16).reshape(POINT[0])


def point_layer(after, skip, upstream, first, last, gains, vectors, weights):
    windows, rows, _ = after.shape
    shapes = [
        jax.ShapeDtypeStruct((windows, 2 * rows, D), jnp.bfloat16),
        jax.ShapeDtypeStruct((windows, 2 * rows, D), jnp.bfloat16),
        jax.ShapeDtypeStruct((UNITS, 2, UNIT, D), jnp.bfloat16),
        jax.ShapeDtypeStruct((windows, 1, D), jnp.float32),
        jax.ShapeDtypeStruct((8, D), jnp.float32),
    ]
    moving = (after, skip, upstream, first, last, gains)
    return pl.pallas_call(
        functools.partial(point_kernel, rows=rows),
        grid=(windows,),
        in_specs=[step_block(array, 1) for array in moving]
        + [whole_block(vectors), unit_rows(*POINT_ROWS)],
        out_specs=[
            step_block(shapes[0], 1),
            step_block(shapes[1], 1),
            weight_block(POINT),
            step_block(shapes[3], 1),
            whole_block(shapes[4]),
        ],
        out_shape=shapes,
        scratch_shapes=[
            pltpu.VMEM((D // LANES, 2 * rows, LANES), jnp.float32),
            pltpu.VMEM((2 * rows, D), jnp.float32),
            pltpu.VMEM((D, D), jnp.float32),
        ],
        compiler_params=pltpu.CompilerParams(vmem_limit_bytes=60 * 2**20),
        cost_estimate=pl.CostEstimate(
            flops=(12 * windows * rows * D * D) // 16,
            bytes_accessed=(4 * D * D + 20 * windows * rows * D) // 16,
            transcendentals=0,
        ),
    )(*moving, vectors, weights[1])


def dense_back_kernel(
    core_ref,
    upstream_ref,
    grad_conv_ref,
    first_ref,
    last_ref,
    slope_ref,
    hidden_ref,
    vectors_ref,
    w_out_ref,
    w_left_ref,
    w_right_ref,
    w_down_ref,
    skip_grad_ref,
    grad_mid_ref,
    grad_down_ref,
    grad_before_ref,
    grad_att_ref,
    own_a,
    own_b,
    other_a,
    other_b,
    sums_ref,
    up_sums_ref,
    doubled,
    *,
    count,
    rows,
):
    core = core_ref[0]
    total = count * rows
    width = own_a.shape[2]

    @pl.when(pl.program_id(0) == 0)
    def _():
        sums_ref[...] = jnp.zeros_like(sums_ref)
        up_sums_ref[...] = jnp.zeros_like(up_sums_ref)

    grads = []
    for window in range(count):
        here = grad_conv_ref[window].astype(jnp.float32)
        earlier, later = shifted(
            here, first_ref[window].astype(jnp.float32), last_ref[window].astype(jnp.float32)
        )
        skip_grad = (
            upstream_ref[window].astype(jnp.float32)
            + vectors_ref[7:8, :] * later
            + vectors_ref[8:9, :] * here
            + vectors_ref[9:10, :] * earlier
        )
        skip_grad_ref[window] = skip_grad
        for number in range(D // LANES):
            doubled[number] = skip_grad[:, number * LANES : (number + 1) * LANES]
        grads.append(
            jnp.concatenate(
                [
                    doubled[number, pl.ds(0, rows, stride=2), :]
                    + doubled[number, pl.ds(1, rows, stride=2), :]
                    for number in range(D // LANES)
                ],
                axis=1,
            )
        )
    grad = jnp.concatenate(grads, axis=0)
    low = grad.astype(jnp.bfloat16)
    grad_down_ref[...] = low.reshape(count, rows, D)
    sums_ref[0:1, :] = sums_ref[0:1, :] + jnp.sum(
        low.astype(jnp.float32), axis=0, keepdims=True
    )
    grad_norm = jnp.zeros((total, D), jnp.float32)
    for number in range(FF // WIDE):
        span = slice(number * WIDE, (number + 1) * WIDE)
        half = (w_left_ref, w_right_ref)[number * WIDE // D]
        start = number * WIDE % D
        units = slice(number * WIDE // 32, (number + 1) * WIDE // 32)
        slope = slope_ref[:, :, span].reshape(total, WIDE).astype(jnp.float32)
        grad_active = times_transposed(low, w_down_ref[units].reshape(WIDE, D))
        grad_before = (grad_active * slope).astype(jnp.bfloat16)
        grad_before_ref[:, :, span] = grad_before.reshape(count, rows, WIDE)
        up_sums_ref[0:1, span] = up_sums_ref[0:1, span] + jnp.sum(
            grad_before.astype(jnp.float32), axis=0, keepdims=True
        )
        grad_norm = grad_norm + times_transposed(
            grad_before, half[:, 0, :, start : start + WIDE].reshape(D, WIDE)
        )
    hidden = hidden_ref[...].reshape(total, D)
    gain = vectors_ref[2:3, :]
    _, stats, inverse = layer_stats(hidden, gain, vectors_ref[3:4, :])
    sums_ref[1:2, :] = sums_ref[1:2, :] + jnp.sum(grad_norm * stats, axis=0, keepdims=True)
    sums_ref[2:3, :] = sums_ref[2:3, :] + jnp.sum(grad_norm, axis=0, keepdims=True)
    mid = grad + norm_back(grad_norm, stats, inverse, gain)
    grad_mid_ref[...] = mid.reshape(count, rows, D)
    mid_low = mid.astype(jnp.bfloat16)
    grad_att_ref[...] = mid_low.reshape(count, rows, D)
    sums_ref[3:4, :] = sums_ref[3:4, :] + jnp.sum(
        mid_low.astype(jnp.float32), axis=0, keepdims=True
    )
    for number, piece in enumerate((own_a, own_b, other_a, other_b)):
        group = core if number < 2 else 1 - core
        unit = group * 24 + (number % 2) * 12
        piece[...] = (
            times_transposed(mid_low, w_out_ref[pl.ds(unit, 12)].reshape(width, D))
            .astype(jnp.bfloat16)
            .reshape(count, rows, width)
        )


def dense_backward(
    core, upstream, grad_conv, first, last, slope, hidden, vectors, weights
):
    windows, rows, _ = hidden.shape
    count = max(1, 256 // rows)
    width = H * VD // 4
    shapes = (
        [
            jax.ShapeDtypeStruct((windows, 2 * rows, D), jnp.float32),
            jax.ShapeDtypeStruct((windows, rows, D), jnp.float32),
            jax.ShapeDtypeStruct((windows, rows, D), jnp.bfloat16),
            jax.ShapeDtypeStruct((windows, rows, FF), jnp.bfloat16),
            jax.ShapeDtypeStruct((windows, rows, D), jnp.bfloat16),
        ]
        + [jax.ShapeDtypeStruct((windows, rows, width), jnp.bfloat16)] * 4
        + [jax.ShapeDtypeStruct((8, D), jnp.float32), jax.ShapeDtypeStruct((8, FF), jnp.float32)]
    )
    moving = (upstream, grad_conv, first, last, slope, hidden)
    lower, upper, w_up = weights
    return pl.pallas_call(
        functools.partial(dense_back_kernel, count=count, rows=rows),
        grid=(windows // count,),
        in_specs=[pl.BlockSpec(memory_space=pltpu.SMEM)]
        + [step_block(array, count) for array in moving]
        + [whole_block(vectors)]
        + [unit_rows(*OUT_ROWS), up_half(0), up_half(1), unit_rows(*DOWN_ROWS)],
        out_specs=[step_block(shape, count) for shape in shapes[:9]]
        + [whole_block(shape) for shape in shapes[9:]],
        out_shape=shapes,
        scratch_shapes=[pltpu.VMEM((D // LANES, 2 * rows, LANES), jnp.float32)],
        compiler_params=pltpu.CompilerParams(vmem_limit_bytes=62 * 2**20),
        cost_estimate=pl.CostEstimate(
            flops=(2 * windows * rows * D * (D + 2 * FF)) // 16,
            bytes_accessed=(2 * D * (D + 2 * FF) + 40 * windows * rows * D) // 16,
            transcendentals=0,
        ),
    )(core, *moving, vectors, lower, w_up, w_up, upper)


def weight_grad_kernel(left_ref, right_ref, *refs):
    out_ref = refs[-1]
    total = left_ref.shape[0] * left_ref.shape[1]
    left = left_ref[...].reshape(total, left_ref.shape[2])
    right = right_ref[...].reshape(total, D)
    out_ref[...] = (
        jnp.dot(left.T, right, preferred_element_type=jnp.float32)
        .astype(jnp.bfloat16)
        .reshape(out_ref.shape)
    )


def weight_grad(left, right, held, place):
    windows, rows, depth = left.shape
    halves = right.shape[2] // D
    step = D // 4
    count = step // UNIT // (2 // halves)
    first = place[0][0] * place[1][0] // count
    return pl.pallas_call(
        weight_grad_kernel,
        grid=(halves, depth // step),
        in_specs=[
            pl.BlockSpec((windows, rows, step), lambda h, m: (0, 0, m)),
            pl.BlockSpec((windows, rows, D), lambda h, m: (0, 0, h)),
            pl.BlockSpec(memory_space=pl.ANY),
        ],
        out_specs=pl.BlockSpec(
            (count, 2 // halves, UNIT, D), lambda h, m: (first + m, h, 0, 0)
        ),
        out_shape=jax.ShapeDtypeStruct(held.shape, held.dtype),
        input_output_aliases={2: 0},
        compiler_params=pltpu.CompilerParams(vmem_limit_bytes=48 * 2**20),
        cost_estimate=pl.CostEstimate(
            flops=(2 * windows * rows * depth * right.shape[2]) // 16,
            bytes_accessed=(2 * (windows * rows * (depth + right.shape[2]) + depth * right.shape[2])) // 16,
            transcendentals=0,
        ),
    )(left, right, held)


def ordered(own, other, is_first, axis):
    return jnp.concatenate(
        [jnp.where(is_first, own, other), jnp.where(is_first, other, own)], axis=axis
    )


class Places:
    def __init__(self, windows, local_rows):
        self.dp = lax.axis_size("dp")
        self.seq = lax.axis_size("seq")
        self.windows = windows
        self.rows = local_rows
        self.length = local_rows * self.seq
        self.group = self.seq // (2 * windows)
        self.heads = H // (2 * self.group)
        self.core = lax.axis_index("dp") % 2
        self.is_first = self.core == 0
        self.place = lax.axis_index("seq") % self.group
        self.part = self.rows // (2 * self.group)
        self.head_start = (self.core * self.group + self.place) * self.heads

    def swap(self, array):
        return lax.ppermute(array, "dp", [(i, i ^ 1) for i in range(self.dp)])

    def rows_to_windows(self, own):
        kept, sent = own
        return ordered(kept, self.swap(sent), self.is_first, 0)

    def halves(self, array, axis):
        size = array.shape[axis] // 2
        kept = lax.dynamic_slice_in_dim(array, self.core * size, size, axis)
        sent = lax.dynamic_slice_in_dim(array, (1 - self.core) * size, size, axis)
        return (kept, sent)

    def exchange(self, array):
        return lax.all_to_all(array, "seq", split_axis=0, concat_axis=0, tiled=True)

    def inputs_to_windows(self, inputs):
        both = self.rows_to_windows(self.halves(inputs, 1))
        return both.reshape(self.seq, self.part, inputs.shape[2])

    def gather_rows(self, array):
        features = array.shape[2]
        array = array[:, None]
        if self.group > 1:
            hops = [
                (i, i - i % self.group + (i + 1) % self.group) for i in range(self.seq)
            ]
            pieces = [array]
            for _ in range(self.group - 1):
                pieces.append(lax.ppermute(pieces[-1], "seq", hops))
            pieces = jnp.concatenate(pieces, axis=1)
            order = (self.place - jnp.arange(self.group)) % self.group
            array = jnp.take(pieces, order, axis=1)
        array = ordered(
            array[:, None], self.swap(array)[:, None], self.is_first, 1
        )
        return array.reshape(self.length, features)

    def sum_rows(self, partial):
        features = partial.shape[1]
        partial = partial.reshape(self.seq, 2, self.group * self.part, features)
        kept, sent = self.halves(partial, 1)
        total = kept[:, 0].astype(jnp.float32) + self.swap(
            sent[:, 0].astype(jnp.bfloat16)
        ).astype(jnp.float32)
        if self.group > 1:
            total = lax.psum_scatter(
                total.reshape(self.seq, self.group, self.part, features),
                "seq",
                scatter_dimension=1,
                axis_index_groups=[
                    list(range(i, i + self.group)) for i in range(0, self.seq, self.group)
                ],
                tiled=True,
            )
            total = total[:, 0]
        return total.astype(jnp.bfloat16)

    def sums_to_rows(self, array):
        features = array.shape[2]
        back = array.reshape(2 * self.windows, self.group * self.part, features)
        kept, sent = self.halves(back, 0)
        return ordered(kept, self.swap(sent), self.is_first, 1)

    def heads_to_rows(self, chunk):
        count = chunk.shape[1]
        back = self.exchange(chunk.reshape(self.seq, self.rows, count))
        kept, sent = self.halves(
            back.reshape(2 * self.windows, self.group, self.rows, count), 0
        )
        return (kept, self.swap(sent))

    def rows_to_heads(self, kept, sent):
        count = kept.shape[3]
        both = self.rows_to_windows((kept, sent))
        back = self.exchange(both.reshape(self.seq, self.rows, count))
        return back.reshape(self.length, count)


def gather_weights(params, sent):
    devices = lax.axis_size(("dp", "seq"))
    index = lax.axis_index(("dp", "seq"))
    dp, seq = lax.axis_size("dp"), lax.axis_size("seq")
    shard = params.shape[0]
    own_rows = ROWS // devices
    extra = shard - own_rows * D
    rest = extra * devices
    tail = params[shard - TAIL :].astype(jnp.bfloat16)
    before = lax.ppermute(tail, ("dp", "seq"), [(i, i + 1) for i in range(devices - 1)])
    joined = jnp.concatenate([before.astype(jnp.float32), params])
    piece = lax.dynamic_slice_in_dim(joined, TAIL - extra * index, own_rows * D)
    piece = piece.astype(jnp.bfloat16).reshape(own_rows, D)
    special = jnp.where(index == devices - 1, tail, jnp.zeros_like(tail))
    for axis, bit in axis_bits("dp"):
        special = special + partner(special, axis, bit)
    special = jnp.broadcast_to(special.reshape(1, TAIL // D, D), (seq, TAIL // D, D))
    special = lax.all_to_all(special, "seq", split_axis=0, concat_axis=0, tiled=True)[seq - 1]
    special, sent = lax.optimization_barrier((special, sent))
    ready = lax.all_to_all(sent, "seq", split_axis=0, concat_axis=0, tiled=True)
    special = special.astype(jnp.float32).reshape(-1)[TAIL - rest :]
    if own_rows % UNIT == 0:
        here = piece.reshape(own_rows // UNIT, UNIT, D)
        other = jnp.swapaxes(piece.reshape(own_rows // UNIT, 8, 2, D), 1, 2).reshape(here.shape)
        row = own_rows * index + UNIT * jnp.arange(own_rows // UNIT)
        inside = (row >= UP_ROWS[0]) & (row < UP_ROWS[0] + UP_ROWS[1])
        piece = jnp.where(inside[:, None, None], other, here).reshape(piece.shape)
    half = own_rows // 2
    if dp == 2 and half % 8 == 0:
        second = lax.axis_index("dp") == 1
        given = jnp.where(second, piece[:half], piece[half:])
        taken = partner(given, "dp", 0)
        low = jnp.where(second, taken, piece[:half])
        high = jnp.where(second, piece[half:], taken)
        lower = lax.all_gather(low, ("seq", "dp"), axis=0, tiled=True)
        high, lower, ready = lax.optimization_barrier((high, lower, ready))
        upper = lax.all_gather(high, ("seq", "dp"), axis=0, tiled=True)
    else:
        everything = lax.all_gather(piece, ("dp", "seq"), axis=0, tiled=True)
        lower, upper = (everything[: ROWS // 2], everything[ROWS // 2 :])
    if own_rows % UNIT == 0:
        w_up = up_units(lower.reshape(-1, UNIT, D), upper.reshape(-1, UNIT, D))
    else:
        w_up = jnp.concatenate([lower[UP_ROWS[0] :], upper[: UP_ROWS[0] + UP_ROWS[1] - ROWS // 2]])
        w_up = jnp.swapaxes(w_up.reshape(96, UNIT, 2, D), 1, 2)
    views = [array.reshape(-1, 2, UNIT, D) for array in (lower, upper)]
    return (lower, (*views, w_up), special, ready)


def axis_bits(axis):
    return [(axis, bit) for bit in range(lax.axis_size(axis).bit_length() - 2, -1, -1)]


def partner(array, axis, bit):
    pairs = [(i, i ^ (1 << bit)) for i in range(lax.axis_size(axis))]
    return lax.ppermute(array, axis, pairs)


def turned(number):
    along = axis_bits("seq")[::-1]
    return (along, along[1:2] + along[:1] + along[2:], along[2:] + along[:2])[number % 3]


def halves_apart(rows, first, outer, inner):
    units = rows.shape[0] // (2 * UNIT)
    here = rows.reshape(units, 2 * UNIT, D)
    other = jnp.swapaxes(rows.reshape(units, outer, inner, D), 1, 2).reshape(here.shape)
    inside = first + 2 * UNIT * jnp.arange(units) < 2 * D
    return jnp.where(inside[:, None, None], other, here).reshape(rows.shape)


class Sums:
    def __init__(self, rows):
        self.bits = axis_bits("dp") + axis_bits("seq")
        self.states = [rows.reshape((2,) * len(self.bits) + (-1, D))]
        self.left = [list(self.bits)]
        self.orders = [axis_bits("dp")[::-1]]
        self.steps = len(self.bits)

    def send(self):
        self.steps -= 1
        if not self.orders[0]:
            band = D // 3
            self.states = [self.states[0][..., k * band : (k + 1) * band] for k in range(3)]
            self.left = [list(self.left[0]) for _ in range(3)]
            self.orders = [turned(k) for k in range(3)]
        for k, state in enumerate(self.states):
            axis, bit = self.orders[k][0]
            self.orders[k] = self.orders[k][1:]
            dim = self.left[k].index((axis, bit))
            self.left[k].pop(dim)
            mine = (lax.axis_index(axis) >> bit) & 1
            sent = lax.dynamic_index_in_dim(state, 1 - mine, dim, False)
            kept = lax.dynamic_index_in_dim(state, mine, dim, False)
            self.states[k] = (kept, sent, axis, bit)

    def before(self, array):
        sent, array = lax.optimization_barrier(([state[1] for state in self.states], array))
        self.states = [
            (kept, there, axis, bit)
            for (kept, _, axis, bit), there in zip(self.states, sent, strict=True)
        ]
        return array

    def move(self):
        self.states = [
            (kept, partner(sent, axis, bit), axis, bit) for kept, sent, axis, bit in self.states
        ]

    def add(self):
        self.states = [
            (kept.astype(jnp.float32) + other.astype(jnp.float32)).astype(jnp.bfloat16)
            for kept, other, _, _ in self.states
        ]

    def finish(self, left=0):
        while self.steps > left:
            self.send()
            self.move()
            self.add()
        return jnp.concatenate(self.states, axis=1) if left == 0 else None


PARTS = ((4096, 6144), (2560, 1536), (10240, 1536))
QKV_PARTS = ((0, 2560),)


def moves(parts, more):
    devices = lax.axis_size(("dp", "seq"))
    own_rows = ROWS // devices
    count = sum(rows for _, rows in parts) // devices
    found, start = ([], 0)
    for first, rows in parts:
        for t in range(devices):
            low, high = (max(count * t, start), min(count * (t + 1), start + rows))
            if low >= high:
                continue
            row = first + low - start
            for i in range(devices):
                if row < own_rows * (i + 1) + more and row + high - low > own_rows * i:
                    found.append((i, t, high - low, row - own_rows * i, low - count * t))
        start += rows
    rounds = []
    for move in found:
        for held in rounds:
            if all(move[0] != other[0] and move[1] != other[1] for other in held):
                held.append(move)
                break
        else:
            rounds.append([move])
    return (rounds, count)


def per_device(values):
    index = lax.axis_index(("dp", "seq"))
    result = jnp.zeros((), jnp.int32)
    for place, value in values:
        if value != 0:
            result = jnp.where(index == place, value, result)
    return result


def add_rows(buffer, moved, place, count):
    row = lax.broadcasted_iota(jnp.int32, moved.shape, 0)
    moved = jnp.where(row < count, moved, jnp.zeros_like(moved))
    there = lax.dynamic_slice_in_dim(buffer, place, moved.shape[0], 0)
    return lax.dynamic_update_slice_in_dim(buffer, there + moved, place, 0)


def to_owners(buffer, share, parts):
    rounds, most = moves(parts, TAIL // D)
    share = jnp.pad(share, ((0, most), (0, 0)))
    for held in rounds:
        start = per_device([(t, offset) for _, t, _, _, offset in held])
        moved = lax.ppermute(
            lax.dynamic_slice_in_dim(share, start, most, 0),
            ("dp", "seq"),
            [(t, i) for i, t, _, _, _ in held],
        )
        place = per_device([(i, MARGIN + low) for i, _, _, low, _ in held])
        count = per_device([(i, rows) for i, _, rows, _, _ in held])
        buffer = add_rows(buffer, moved, place, count)
    return buffer


def own_entries(buffer, special):
    devices = lax.axis_size(("dp", "seq"))
    index = lax.axis_index(("dp", "seq"))
    own_rows = ROWS // devices
    rest = special.shape[0]
    extra = rest // devices
    held = buffer[MARGIN : MARGIN + own_rows + TAIL // D].astype(jnp.float32)
    after = held[own_rows:].reshape(-1)
    after = jnp.where(index == devices - 1, jnp.pad(special, (0, TAIL - rest)), after)
    joined = jnp.concatenate([held[:own_rows].reshape(-1), after])
    return lax.dynamic_slice_in_dim(joined, extra * index, own_rows * D + extra)


def body(block_input, skip_input, species, cotangent, params, first_moment, second_moment):
    windows, local_rows, _ = block_input.shape
    at = Places(windows, local_rows)
    length = at.length
    own = at.heads
    scale = 1.0 / math.sqrt(KD)
    f32, bf16 = jnp.float32, jnp.bfloat16

    early, weights, special, moved = gather_weights(params, at.inputs_to_windows(block_input))
    pos_low = special[: F * H].reshape(F, H)
    up_bias = special[F * H : F * H + FF]
    vectors = special[F * H + FF :].reshape(12, D)

    def columns(matrix, width):
        return lax.dynamic_slice_in_dim(matrix, at.head_start * width, own * width, 1)

    w_own = jnp.concatenate(
        [
            columns(early[:512].reshape(D, H * KD), KD) * jnp.asarray(scale, bf16),
            columns(early[512:1024].reshape(D, H * KD), KD),
            columns(early[1024:2560].reshape(D, H * VD), VD),
        ],
        axis=1,
    )
    pos_basis = position_basis(length)
    own_pos = lax.dynamic_slice_in_dim(pos_low, at.head_start, own, 1)
    tables = jnp.dot(own_pos.T, pos_basis.T, precision=highest)
    tables = jnp.roll(jnp.pad(tables, ((0, 0), (0, 1))), 1 - BLOCK, axis=1)
    tables = jnp.broadcast_to(tables[:, None, :], (own, 8, 2 * length))

    low_part, _, _ = layer_stats(moved.astype(f32), vectors[0], vectors[1])
    low_all = at.gather_rows(low_part.astype(bf16))
    projected = jnp.einsum("rd,dk->kr", low_all, w_own, preferred_element_type=f32).astype(bf16)
    queries, keys, values = (
        projected[: own * KD],
        projected[own * KD : 2 * own * KD],
        projected[2 * own * KD :],
    )

    operands, saved, pieces = ([], [], ([], []))
    for pair in range(own // PAIR):
        narrow = slice(pair * PAIR * KD, (pair + 1) * PAIR * KD)
        wide = slice(pair * PAIR * VD, (pair + 1) * PAIR * VD)
        given = (
            tables[pair * PAIR : (pair + 1) * PAIR],
            queries[narrow],
            keys[narrow],
            values[wide],
        )
        result, log_total = attention_forward(*given)
        operands.append(given)
        saved.append((result, log_total))
        for held, part in zip(pieces, at.heads_to_rows(result), strict=True):
            held.append(part)
    pairs = own // PAIR
    pieces = [
        held[pair][:, place] for held in pieces for place in range(at.group) for pair in range(pairs)
    ]

    core = jnp.asarray(at.core, jnp.int32).reshape(1)
    heads, hidden_one, low_two, activated, slope, hidden_two = dense_forward(
        core, block_input, pieces, vectors, up_bias[None], weights
    )
    ends = [
        (hidden_two[:, row : row + 1] + skip_input[:, up : up + 1].astype(f32)).astype(bf16)
        for row, up in ((0, 0), (local_rows - 1, 2 * local_rows - 1))
    ]
    first, last = edge_rows(ends)
    is_mouse = (species == 1).astype(f32)[:, None]
    species_gain = (1.0 - is_mouse) * vectors[10] + is_mouse * vectors[11]
    block_out, grad_conv, dense_grads, gain_rows, point_sums = point_layer(
        hidden_two,
        skip_input,
        cotangent,
        first,
        last,
        species_gain[:, None, :],
        vectors,
        weights,
    )
    gain_rows = gain_rows[:, 0]
    grad_human = jnp.sum((1.0 - is_mouse) * gain_rows, axis=0)
    grad_mouse = jnp.sum(is_mouse * gain_rows, axis=0)
    first, last = edge_rows([grad_conv[:, :1], grad_conv[:, 2 * local_rows - 1 :]])
    (
        skip_grad,
        grad_mid,
        grad_down_low,
        grad_before,
        grad_attn_low,
        *grad_pieces,
        dense_sums,
        up_sums,
    ) = dense_backward(
        core,
        cotangent,
        grad_conv,
        first,
        last,
        slope,
        hidden_one,
        vectors,
        weights,
    )
    grad_pieces = [
        jnp.stack(
            [
                grad_pieces[2 * group + place * pairs + pair]
                for place in range(at.group)
            ],
            axis=1,
        )
        for group in range(2)
        for pair in range(pairs)
    ]

    middle = jnp.concatenate(
        [
            up_sums[0],
            dense_sums[1],
            dense_sums[2],
            dense_sums[3],
            dense_sums[0],
            point_sums[:4].reshape(-1),
            grad_human,
            grad_mouse,
        ]
    )
    devices = lax.axis_size(("dp", "seq"))
    chunks = [at.rows_to_heads(grad_pieces[pair], grad_pieces[pairs + pair]) for pair in range(pairs)]
    dense_grads = weight_grad(activated, grad_down_low, dense_grads, DOWN)
    dense_grads = weight_grad(low_two, grad_before, dense_grads, LEFT)
    dense_grads = weight_grad(heads, grad_attn_low, dense_grads, OUT).reshape(-1, D)
    even = dense_grads.shape[0] // devices % (2 * UNIT) == 0
    if not even:
        dense_grads = halves_apart(dense_grads, 0, 2, UNIT)
    dense_grads, chunks[0] = lax.optimization_barrier((dense_grads, chunks[0]))
    dense = lax.psum_scatter(dense_grads, ("dp", "seq"), scatter_dimension=0, tiled=True)

    dq, dk, dv, dt = ([], [], [], [])
    for pair in range(pairs):
        result, log_total = saved[pair]
        grads = attention_backward(*operands[pair], result, chunks[pair], log_total)
        for piece, held in zip(grads, (dq, dk, dv, dt), strict=True):
            held.append(piece)
    grad_own = jnp.concatenate(dq + dk + dv, axis=1)
    partial = jnp.einsum("rk,dk->rd", grad_own, w_own, preferred_element_type=f32).astype(bf16)
    partial, grad_own = lax.optimization_barrier((partial, grad_own))
    back = at.exchange(at.sum_rows(partial))
    grad_w_own = jnp.einsum("rd,rk->dk", low_all, grad_own, preferred_element_type=f32)
    grad_w_query = grad_w_own[:, : own * KD] * scale
    grad_w_key = grad_w_own[:, own * KD : 2 * own * KD]
    grad_w_value = grad_w_own[:, 2 * own * KD :]

    def all_columns(matrix, width):
        whole = jnp.zeros((D, H * width), bf16)
        return lax.dynamic_update_slice_in_dim(
            whole, matrix.astype(bf16), at.head_start * width, 1
        ).reshape(-1, D)

    first_rows = jnp.concatenate(
        [
            all_columns(grad_w_query, KD),
            all_columns(grad_w_key, KD),
            all_columns(grad_w_value, VD),
        ],
        axis=0,
    )
    first_sums = Sums(first_rows)
    first_sums.finish(2)
    first_sums.states, back = lax.optimization_barrier((first_sums.states, back))
    grad_norm_one = at.sums_to_rows(back).astype(f32)
    _, stats_one, inverse_one = layer_stats(block_input.astype(f32), vectors[0], vectors[1])
    input_grad = grad_mid + norm_back(grad_norm_one, stats_one, inverse_one, vectors[0])
    grad_gain_one = jnp.sum(grad_norm_one * stats_one, axis=(0, 1))
    grad_bias_one = jnp.sum(grad_norm_one, axis=(0, 1))
    grad_tables = jnp.roll(jnp.concatenate(dt, axis=0), BLOCK - 1, axis=1)[:, : 2 * length - 1]
    grad_pos = jnp.dot(pos_basis.T, grad_tables.T, precision=highest)
    grad_pos = lax.dynamic_update_slice_in_dim(
        jnp.zeros((F, H), f32), grad_pos, at.head_start, 1
    )
    late = jnp.concatenate([grad_pos.reshape(-1), grad_gain_one, grad_bias_one])
    summed = jnp.concatenate([late, middle])
    for axis, bit in axis_bits("dp") + axis_bits("seq"):
        summed = summed + partner(summed, axis, bit)
    late, middle = (summed[: late.shape[0]], summed[late.shape[0] :])
    special_grads = jnp.concatenate(
        [late[: F * H], middle[:FF], late[F * H :], middle[FF:]]
    )
    share = dense
    if even:
        share = halves_apart(share, lax.axis_index(("dp", "seq")) * share.shape[0], 2, UNIT)
    buffer = jnp.zeros((ROWS // devices + TAIL // D + 2 * MARGIN, D), bf16)
    buffer = to_owners(buffer, share, PARTS)
    buffer = to_owners(buffer, first_sums.finish(), QKV_PARTS)
    reduced = own_entries(buffer, special_grads)
    shard_len = params.shape[0]
    position = lax.axis_index(("dp", "seq")) * shard_len + jnp.arange(shard_len)
    param_new, first_new, second_new = adam_update(
        params, first_moment, second_moment, reduced, position
    )
    return (
        block_out,
        input_grad,
        skip_grad,
        param_new,
        first_new,
        second_new,
        param_new.astype(bf16),
    )


def solution(mesh):
    return jax.shard_map(
        body,
        mesh=mesh,
        in_specs=(
            P("dp", "seq", None),
            P("dp", "seq", None),
            P("dp"),
            P("dp", "seq", None),
            P(("dp", "seq")),
            P(("dp", "seq")),
            P(("dp", "seq")),
        ),
        out_specs=(
            P("dp", "seq", None),
            P("dp", "seq", None),
            P("dp", "seq", None),
            P(("dp", "seq")),
            P(("dp", "seq")),
            P(("dp", "seq")),
            P(("dp", "seq")),
        ),
        check_vma=False,
    )
```

```python
import functools
import math

import jax
import jax.numpy as jnp
from jax import lax
from jax.experimental import pallas as pl
from jax.experimental.pallas import tpu as pltpu
from jax.sharding import PartitionSpec as P

D = 1536
H = 8
KD = 64
VD = 192
FF = 3072
F = 192
STEP = 10
BLOCK = 256
PAIR = 2
CHUNK = 512
WIDE = 768
LANES = 128
ROWS = 11776
QKV_ROWS = 2560
TAIL = 24576
MARGIN = 288
UNIT = 16
UNITS = 288


eps_norm = 1e-05
beta_one = 0.5
beta_two = 0.5
adam_eps = 1e-08
decay_rate = 0.01
highest = lax.Precision.HIGHEST


def edge_rows(array):
    devices = lax.axis_size("seq")
    up = [(i, i + 1) for i in range(devices - 1)]
    first = lax.ppermute(array[1], "seq", up)
    last = lax.ppermute(array[0], "seq", [(j, i) for i, j in up])
    return (first, last)


def segment_ends():
    counts = [
        D * H * KD,
        D * H * KD,
        D * H * VD,
        H * VD * D,
        D * FF,
        FF * D,
        D * D,
        F * H,
        FF,
        12 * D,
    ]
    limits = []
    running = 0
    for amount in counts:
        running = running + amount
        limits.append(running)
    return limits


def rate_at(position):
    limits = segment_ends()
    step_rates = [
        2.0 / math.sqrt(D),
        2.0 / math.sqrt(D),
        2.0 / math.sqrt(D),
        8.0 / math.sqrt(H * VD),
        2.0 / math.sqrt(D),
        2.0 / math.sqrt(FF),
        2.0 / math.sqrt(D),
        3.0 / math.sqrt(F),
        0.4,
        0.4,
    ]
    result = jnp.full(position.shape, step_rates[-1], jnp.float32)
    for segment in range(len(limits) - 2, -1, -1):
        result = jnp.where(position < limits[segment], step_rates[segment], result)
    return result


def adam_update(param_old, first_old, second_old, gradient, position):
    step_rate = rate_at(position)
    first_new = beta_one * first_old + (1.0 - beta_one) * gradient
    second_new = beta_two * second_old + (1.0 - beta_two) * gradient * gradient
    first_hat = first_new / (1.0 - beta_one**STEP)
    second_hat = second_new / (1.0 - beta_two**STEP)
    param_new = param_old - step_rate * (
        first_hat / (jnp.sqrt(second_hat) + adam_eps) + decay_rate * param_old
    )
    return (param_new, first_new, second_new)


def position_basis(length):
    offsets = jnp.arange(2 * length - 1).astype(jnp.float32) - (length - 1)
    halves = F // 2
    ladder = jnp.arange(halves).astype(jnp.float32) / max(halves - 1, 1)
    lifetimes = jnp.exp(ladder * math.log(length))
    decays = jnp.exp(-jnp.abs(offsets)[:, None] * (math.log(2.0) / lifetimes)[None, :])
    return jnp.concatenate([decays, jnp.sign(offsets)[:, None] * decays], axis=1)


def layer_stats(inputs, norm_gain, norm_bias):
    centered = inputs - jnp.mean(inputs, axis=-1, keepdims=True)
    inverse = lax.rsqrt(jnp.mean(centered * centered, axis=-1, keepdims=True) + eps_norm)
    normed = centered * inverse
    return (normed * norm_gain + norm_bias, normed, inverse)


def norm_back(upstream, normed, inverse, norm_gain):
    scaled = upstream * norm_gain
    return inverse * (
        scaled
        - jnp.mean(scaled, axis=-1, keepdims=True)
        - normed * jnp.mean(scaled * normed, axis=-1, keepdims=True)
    )


def spread_rows(first_row, bands):
    start = pltpu.roll(first_row, 0, 1, stride=1, stride_axis=0)
    bands[0:8, :] = start
    height = 8
    while height < BLOCK:
        bands[height : 2 * height, :] = pltpu.roll(bands[0:height, :], height, 1)
        height *= 2


def collect_rows(bands, width):
    height = BLOCK // 2
    while height >= 8:
        bands[0:height, :] = bands[0:height, :] + pltpu.roll(
            bands[height : 2 * height, :], width - height, 1
        )
        height //= 2
    total = bands[0:1, :]
    for row in range(1, 8):
        total = total + pltpu.roll(bands[row : row + 1, :], width - row, 1)
    return total


def forward_kernel(
    table_ref, q_ref, k_ref, v_ref, out_ref, lse_ref, bands, key_rows, scores, *, blocks
):
    block = pl.program_id(0)

    @pl.when(block == 0)
    def _():
        for head in range(PAIR):
            spread_rows(table_ref[head], bands.at[head])
            key_rows[head] = k_ref[head * KD : (head + 1) * KD, :].T

    results = []
    for head in range(PAIR):
        queries = q_ref[head * KD : (head + 1) * KD, :]
        top = jnp.full((1, BLOCK), -jnp.inf, jnp.float32)
        for j in range(blocks):
            at = pl.multiple_of((block - j + blocks - 1) * BLOCK, BLOCK)
            span = slice(j * BLOCK, (j + 1) * BLOCK)
            part = (
                jnp.dot(key_rows[head, span, :], queries, preferred_element_type=jnp.float32)
                + bands[head, :, pl.ds(at, BLOCK)]
            )
            scores[span, :] = part
            top = jnp.maximum(top, jnp.max(part, axis=0, keepdims=True))
        total = jnp.zeros((1, BLOCK), jnp.float32)
        result = jnp.zeros((VD, BLOCK), jnp.float32)
        for j in range(blocks):
            span = slice(j * BLOCK, (j + 1) * BLOCK)
            grown = jnp.exp(scores[span, :] - top)
            total = total + jnp.sum(grown, axis=0, keepdims=True)
            result = result + jnp.dot(
                v_ref[head * VD : (head + 1) * VD, span],
                grown.astype(jnp.bfloat16),
                preferred_element_type=jnp.float32,
            )
        results.append(result * (1.0 / total))
        lse_ref[head : head + 1, :] = top + jnp.log(total)
    out_ref[...] = jnp.concatenate(results, axis=0).T.astype(jnp.bfloat16)


def attention_forward(tables, queries, keys, values):
    length = keys.shape[1]
    blocks = length // BLOCK
    return pl.pallas_call(
        functools.partial(forward_kernel, blocks=blocks),
        grid=(blocks,),
        in_specs=[
            pl.BlockSpec((PAIR, 8, 2 * length), lambda i: (0, 0, 0)),
            pl.BlockSpec((PAIR * KD, BLOCK), lambda i: (0, i)),
            pl.BlockSpec((PAIR * KD, length), lambda i: (0, 0)),
            pl.BlockSpec((PAIR * VD, length), lambda i: (0, 0)),
        ],
        out_specs=[
            pl.BlockSpec((BLOCK, PAIR * VD), lambda i: (i, 0)),
            pl.BlockSpec((PAIR, BLOCK), lambda i: (0, i)),
        ],
        out_shape=[
            jax.ShapeDtypeStruct((length, PAIR * VD), jnp.bfloat16),
            jax.ShapeDtypeStruct((PAIR, length), jnp.float32),
        ],
        scratch_shapes=[
            pltpu.VMEM((PAIR, BLOCK, 2 * length), jnp.float32),
            pltpu.VMEM((PAIR, length, KD), jnp.bfloat16),
            pltpu.VMEM((length, BLOCK), jnp.float32),
        ],
        compiler_params=pltpu.CompilerParams(vmem_limit_bytes=48 * 2**20),
        cost_estimate=pl.CostEstimate(
            flops=(4 * PAIR * length * length * 256) // 16,
            bytes_accessed=(8 * PAIR * length * (KD + VD)) // 16,
            transcendentals=PAIR * length * length // 16,
        ),
    )(tables, queries, keys, values)


def backward_kernel(
    table_ref,
    q_ref,
    k_ref,
    v_ref,
    out_ref,
    grad_ref,
    lse_ref,
    dq_ref,
    dk_ref,
    dv_ref,
    dt_ref,
    bands,
    grad_bands,
    key_rows,
    value_rows,
    dk_sum,
    dv_sum,
    *,
    blocks,
):
    block = pl.program_id(0)

    @pl.when(block == 0)
    def _():
        for head in range(PAIR):
            spread_rows(table_ref[head], bands.at[head])
            key_rows[head] = k_ref[head * KD : (head + 1) * KD, :].T
            value_rows[head] = v_ref[head * VD : (head + 1) * VD, :].T
        grad_bands[...] = jnp.zeros_like(grad_bands)
        dk_sum[...] = jnp.zeros_like(dk_sum)
        dv_sum[...] = jnp.zeros_like(dv_sum)

    grad_t = grad_ref[...].T
    out_t = out_ref[...].T
    products = grad_t.astype(jnp.float32) * out_t.astype(jnp.float32)
    results = []
    for head in range(PAIR):
        wide = slice(head * VD, (head + 1) * VD)
        delta = jnp.sum(products[wide, :], axis=0, keepdims=True)
        grad_here = grad_t[wide, :]
        grad_rows = grad_here.T
        queries = q_ref[head * KD : (head + 1) * KD, :]
        query_rows = queries.T
        lse = lse_ref[head : head + 1, :]
        dq = jnp.zeros((KD, BLOCK), jnp.float32)
        for j in range(blocks):
            span = slice(j * BLOCK, (j + 1) * BLOCK)
            at = pl.multiple_of((block - j + blocks - 1) * BLOCK, BLOCK)
            part = (
                jnp.dot(key_rows[head, span, :], queries, preferred_element_type=jnp.float32)
                + bands[head, :, pl.ds(at, BLOCK)]
            )
            soft = jnp.exp(part - lse)
            grad_soft = jnp.dot(
                value_rows[head, span, :], grad_here, preferred_element_type=jnp.float32
            )
            grad_scores = soft * (grad_soft - delta)
            grad_bands[head, :, pl.ds(at, BLOCK)] = (
                grad_bands[head, :, pl.ds(at, BLOCK)] + grad_scores
            )
            low = grad_scores.astype(jnp.bfloat16)
            dv_sum[head, span, :] = dv_sum[head, span, :] + jnp.dot(
                soft.astype(jnp.bfloat16), grad_rows, preferred_element_type=jnp.float32
            )
            dk_sum[head, span, :] = dk_sum[head, span, :] + jnp.dot(
                low, query_rows, preferred_element_type=jnp.float32
            )
            dq = dq + jnp.dot(
                k_ref[head * KD : (head + 1) * KD, span], low, preferred_element_type=jnp.float32
            )
        results.append(dq)
    dq_ref[...] = jnp.concatenate(results, axis=0).T.astype(jnp.bfloat16)

    @pl.when(block == blocks - 1)
    def _():
        dk_ref[...] = jnp.concatenate(
            [dk_sum[head] for head in range(PAIR)], axis=1
        ).astype(jnp.bfloat16)
        dv_ref[...] = jnp.concatenate(
            [dv_sum[head] for head in range(PAIR)], axis=1
        ).astype(jnp.bfloat16)
        for head in range(PAIR):
            dt_ref[head : head + 1, :] = collect_rows(
                grad_bands.at[head], grad_bands.shape[2]
            )


def attention_backward(tables, queries, keys, values, heads, grad_heads, lse):
    length = keys.shape[1]
    blocks = length // BLOCK
    return pl.pallas_call(
        functools.partial(backward_kernel, blocks=blocks),
        grid=(blocks,),
        in_specs=[
            pl.BlockSpec((PAIR, 8, 2 * length), lambda i: (0, 0, 0)),
            pl.BlockSpec((PAIR * KD, BLOCK), lambda i: (0, i)),
            pl.BlockSpec((PAIR * KD, length), lambda i: (0, 0)),
            pl.BlockSpec((PAIR * VD, length), lambda i: (0, 0)),
            pl.BlockSpec((BLOCK, PAIR * VD), lambda i: (i, 0)),
            pl.BlockSpec((BLOCK, PAIR * VD), lambda i: (i, 0)),
            pl.BlockSpec((PAIR, BLOCK), lambda i: (0, i)),
        ],
        out_specs=[
            pl.BlockSpec((BLOCK, PAIR * KD), lambda i: (i, 0)),
            pl.BlockSpec((length, PAIR * KD), lambda i: (0, 0)),
            pl.BlockSpec((length, PAIR * VD), lambda i: (0, 0)),
            pl.BlockSpec((PAIR, 2 * length), lambda i: (0, 0)),
        ],
        out_shape=[
            jax.ShapeDtypeStruct((length, PAIR * KD), jnp.bfloat16),
            jax.ShapeDtypeStruct((length, PAIR * KD), jnp.bfloat16),
            jax.ShapeDtypeStruct((length, PAIR * VD), jnp.bfloat16),
            jax.ShapeDtypeStruct((PAIR, 2 * length), jnp.float32),
        ],
        scratch_shapes=[
            pltpu.VMEM((PAIR, BLOCK, 2 * length), jnp.float32),
            pltpu.VMEM((PAIR, BLOCK, 2 * length), jnp.float32),
            pltpu.VMEM((PAIR, length, KD), jnp.bfloat16),
            pltpu.VMEM((PAIR, length, VD), jnp.bfloat16),
            pltpu.VMEM((PAIR, length, KD), jnp.float32),
            pltpu.VMEM((PAIR, length, VD), jnp.float32),
        ],
        compiler_params=pltpu.CompilerParams(vmem_limit_bytes=56 * 2**20),
        cost_estimate=pl.CostEstimate(
            flops=(10 * PAIR * length * length * 256) // 16,
            bytes_accessed=(16 * PAIR * length * (KD + VD)) // 16,
            transcendentals=PAIR * length * length // 16,
        ),
    )(tables, queries, keys, values, heads, grad_heads, lse)


def whole_block(array):
    zeros = (0,) * array.ndim
    return pl.BlockSpec(array.shape, lambda i: zeros, pipeline_mode=pl.Buffered(1))


LEFT, DOWN = ((96, 1, UNIT, D), (0, 0)), ((96, 2, UNIT, D), (1, 0))
OUT, POINT = ((48, 2, UNIT, D), (4, 0)), ((48, 2, UNIT, D), (5, 0))


def weight_block(weight):
    shape, place = weight
    return pl.BlockSpec(shape, lambda *i: place + (0, 0), pipeline_mode=pl.Buffered(1))


def up_half(half):
    return pl.BlockSpec(
        (96, 1, UNIT, D), lambda i: (0, half, 0, 0), pipeline_mode=pl.Buffered(1)
    )


def unit_rows(first, rows):
    first, units = (first // (2 * UNIT), rows // (2 * UNIT))
    return pl.BlockSpec(
        (pl.Element(units), pl.Element(2), pl.Element(UNIT), pl.Element(D)),
        lambda i: (first, 0, 0, 0),
        pipeline_mode=pl.Buffered(1),
    )


def up_units_kernel(lower_ref, upper_ref, out_ref, *, steps):
    units = out_ref.shape[0]

    def put(rows_ref):
        rows = rows_ref[...].astype(jnp.float32).reshape(units, 2, 2, 8, D)
        out_ref[...] = (
            jnp.swapaxes(rows, 1, 2).reshape(units, 2, UNIT, D).astype(jnp.bfloat16)
        )

    pl.when(pl.program_id(0) < steps)(lambda: put(lower_ref))
    pl.when(pl.program_id(0) >= steps)(lambda: put(upper_ref))


def up_units(lower, upper):
    units = 8
    start = UP_ROWS[0] // UNIT // (2 * units)
    steps = lower.shape[0] // (2 * units) - start
    return pl.pallas_call(
        functools.partial(up_units_kernel, steps=steps),
        grid=(96 // units,),
        in_specs=[
            pl.BlockSpec(
                (2 * units, UNIT, D), lambda i: (start + jnp.minimum(i, steps - 1), 0, 0)
            ),
            pl.BlockSpec((2 * units, UNIT, D), lambda i: (jnp.maximum(i - steps, 0), 0, 0)),
        ],
        out_specs=pl.BlockSpec((units, 2, UNIT, D), lambda i: (i, 0, 0, 0)),
        out_shape=jax.ShapeDtypeStruct((96, 2, UNIT, D), jnp.bfloat16),
        compiler_params=pltpu.CompilerParams(vmem_limit_bytes=32 * 2**20),
    )(lower, upper)


OUT_ROWS, UP_ROWS, DOWN_ROWS, POINT_ROWS = (2560, D), (4096, FF), (1280, FF), (4352, D)


def step_block(array, count):
    shape = (count,) + array.shape[1:]
    rest = (0,) * (array.ndim - 1)
    return pl.BlockSpec(shape, lambda i: (i,) + rest)


def times_transposed(left, right):
    return lax.dot_general(
        left, right, (((1,), (1,)), ((), ())), preferred_element_type=jnp.float32
    )


def dense_kernel(
    core_ref,
    inputs_ref,
    own_a,
    own_b,
    other_a,
    other_b,
    vectors_ref,
    up_bias_ref,
    w_out_ref,
    w_left_ref,
    w_right_ref,
    w_down_ref,
    heads_ref,
    hidden_ref,
    low_ref,
    active_ref,
    slope_ref,
    after_ref,
    *,
    count,
    rows,
):
    core = core_ref[0]
    total = count * rows
    width = own_a.shape[2]
    hidden = inputs_ref[...].reshape(total, D).astype(jnp.float32) + vectors_ref[4:5, :]
    for number, piece in enumerate((own_a, own_b, other_a, other_b)):
        group = core if number < 2 else 1 - core
        at = pl.multiple_of(group * (2 * width) + (number % 2) * width, 128)
        unit = group * 24 + (number % 2) * 12
        held = piece[...]
        heads_ref[:, :, pl.ds(at, width)] = held
        hidden = hidden + jnp.dot(
            held.reshape(total, width),
            w_out_ref[pl.ds(unit, 12)].reshape(width, D),
            preferred_element_type=jnp.float32,
        )
    hidden_ref[...] = hidden.reshape(count, rows, D)
    normed, _, _ = layer_stats(hidden, vectors_ref[2:3, :], vectors_ref[3:4, :])
    low = normed.astype(jnp.bfloat16)
    low_ref[...] = low.reshape(count, rows, D)
    after = hidden + vectors_ref[5:6, :]
    for number in range(FF // WIDE):
        span = slice(number * WIDE, (number + 1) * WIDE)
        half = (w_left_ref, w_right_ref)[number * WIDE // D]
        start = number * WIDE % D
        units = slice(number * WIDE // 32, (number + 1) * WIDE // 32)
        before = (
            jnp.dot(
                low,
                half[:, 0, :, start : start + WIDE].reshape(D, WIDE),
                preferred_element_type=jnp.float32,
            )
            + up_bias_ref[:, span]
        )
        phi = 0.5 * (1.0 + lax.erf(before * (1.0 / math.sqrt(2.0))))
        slope = phi + before * jnp.exp(-0.5 * before * before) * (1.0 / math.sqrt(2.0 * math.pi))
        active = (before * phi).astype(jnp.bfloat16)
        active_ref[:, :, span] = active.reshape(count, rows, WIDE)
        slope_ref[:, :, span] = slope.astype(jnp.bfloat16).reshape(count, rows, WIDE)
        after = after + jnp.dot(
            active, w_down_ref[units].reshape(WIDE, D), preferred_element_type=jnp.float32
        )
    after_ref[...] = after.reshape(count, rows, D)


def dense_forward(core, inputs, pieces, vectors, up_bias, weights):
    windows, rows, _ = inputs.shape
    count = max(1, 256 // rows)
    shapes = [
        jax.ShapeDtypeStruct((windows, rows, D), jnp.bfloat16),
        jax.ShapeDtypeStruct((windows, rows, D), jnp.float32),
        jax.ShapeDtypeStruct((windows, rows, D), jnp.bfloat16),
        jax.ShapeDtypeStruct((windows, rows, FF), jnp.bfloat16),
        jax.ShapeDtypeStruct((windows, rows, FF), jnp.bfloat16),
        jax.ShapeDtypeStruct((windows, rows, D), jnp.float32),
    ]
    lower, upper, w_up = weights
    return pl.pallas_call(
        functools.partial(dense_kernel, count=count, rows=rows),
        grid=(windows // count,),
        in_specs=[pl.BlockSpec(memory_space=pltpu.SMEM), step_block(inputs, count)]
        + [step_block(piece, count) for piece in pieces]
        + [whole_block(vectors), whole_block(up_bias)]
        + [unit_rows(*OUT_ROWS), up_half(0), up_half(1), unit_rows(*DOWN_ROWS)],
        out_specs=[step_block(shape, count) for shape in shapes],
        out_shape=shapes,
        compiler_params=pltpu.CompilerParams(vmem_limit_bytes=60 * 2**20),
        cost_estimate=pl.CostEstimate(
            flops=(2 * windows * rows * D * (D + 2 * FF)) // 16,
            bytes_accessed=(2 * D * (D + 2 * FF) + 26 * windows * rows * D) // 16,
            transcendentals=2 * windows * rows * FF // 16,
        ),
    )(core, inputs, *pieces, vectors, up_bias, lower, w_up, w_up, upper)


def shifted(rows, first, last):
    count = rows.shape[0]
    place = lax.broadcasted_iota(jnp.int32, rows.shape, 0)
    earlier = jnp.where(place == 0, first, pltpu.roll(rows, 1, 0))
    later = jnp.where(place == count - 1, last, pltpu.roll(rows, count - 1, 0))
    return (earlier, later)


def point_kernel(
    after_ref,
    skip_ref,
    upstream_ref,
    first_ref,
    last_ref,
    gain_ref,
    vectors_ref,
    w_ref,
    out_ref,
    grad_conv_ref,
    grad_w_ref,
    gain_rows_ref,
    sums_ref,
    doubled,
    summed,
    grad_w,
    *,
    rows,
):
    step = pl.program_id(0)

    @pl.when(step == 0)
    def _():
        grad_w[...] = jnp.zeros_like(grad_w)
        sums_ref[...] = jnp.zeros_like(sums_ref)

    for number in range(D // LANES):
        span = slice(number * LANES, (number + 1) * LANES)
        after = after_ref[0, :, span]
        doubled[number, pl.ds(0, rows, stride=2), :] = after
        doubled[number, pl.ds(1, rows, stride=2), :] = after
        summed[:, span] = doubled[number] + skip_ref[0, :, span].astype(jnp.float32)
    low = summed[...].astype(jnp.bfloat16).astype(jnp.float32)
    earlier, later = shifted(
        low, first_ref[0].astype(jnp.float32), last_ref[0].astype(jnp.float32)
    )
    conv = (
        vectors_ref[7:8, :] * earlier + vectors_ref[8:9, :] * low + vectors_ref[9:10, :] * later
    ).astype(jnp.bfloat16)
    conv_t = conv.T
    grad_conv = jnp.zeros((2 * rows, D), jnp.float32)
    for number in range(D // CHUNK):
        span = slice(number * CHUNK, (number + 1) * CHUNK)
        weight = w_ref[:, :, :, span].reshape(D, CHUNK)
        gain = gain_ref[0, :, span]
        upstream = upstream_ref[0, :, span].astype(jnp.float32)
        pointed = (
            jnp.dot(conv, weight, preferred_element_type=jnp.float32) + vectors_ref[6:7, span]
        )
        out_ref[0, :, span] = (summed[:, span] + gain * pointed).astype(jnp.bfloat16)
        gain_rows_ref[0, :, span] = jnp.sum(upstream * pointed, axis=0, keepdims=True)
        grad_point = (gain * upstream).astype(jnp.bfloat16)
        sums_ref[0:1, span] = sums_ref[0:1, span] + jnp.sum(
            grad_point.astype(jnp.float32), axis=0, keepdims=True
        )
        grad_conv = grad_conv + times_transposed(grad_point, weight)
        grad_w[:, span] = grad_w[:, span] + jnp.dot(
            conv_t, grad_point, preferred_element_type=jnp.float32
        )
    grad_low = grad_conv.astype(jnp.bfloat16)
    grad_conv_ref[0] = grad_low
    grad_wide = grad_low.astype(jnp.float32)
    for number, rows_here in enumerate((earlier, low, later)):
        sums_ref[number + 1 : number + 2, :] = sums_ref[number + 1 : number + 2, :] + jnp.sum(
            grad_wide * rows_here, axis=0, keepdims=True
        )

    @pl.when(step == pl.num_programs(0) - 1)
    def _():
        grad_w_ref[...] = grad_w[...].astype(jnp.bfloat16).reshape(POINT[0])


def point_layer(after, skip, upstream, first, last, gains, vectors, weights):
    windows, rows, _ = after.shape
    shapes = [
        jax.ShapeDtypeStruct((windows, 2 * rows, D), jnp.bfloat16),
        jax.ShapeDtypeStruct((windows, 2 * rows, D), jnp.bfloat16),
        jax.ShapeDtypeStruct((UNITS, 2, UNIT, D), jnp.bfloat16),
        jax.ShapeDtypeStruct((windows, 1, D), jnp.float32),
        jax.ShapeDtypeStruct((8, D), jnp.float32),
    ]
    moving = (after, skip, upstream, first, last, gains)
    return pl.pallas_call(
        functools.partial(point_kernel, rows=rows),
        grid=(windows,),
        in_specs=[step_block(array, 1) for array in moving]
        + [whole_block(vectors), unit_rows(*POINT_ROWS)],
        out_specs=[
            step_block(shapes[0], 1),
            step_block(shapes[1], 1),
            weight_block(POINT),
            step_block(shapes[3], 1),
            whole_block(shapes[4]),
        ],
        out_shape=shapes,
        scratch_shapes=[
            pltpu.VMEM((D // LANES, 2 * rows, LANES), jnp.float32),
            pltpu.VMEM((2 * rows, D), jnp.float32),
            pltpu.VMEM((D, D), jnp.float32),
        ],
        compiler_params=pltpu.CompilerParams(vmem_limit_bytes=60 * 2**20),
        cost_estimate=pl.CostEstimate(
            flops=(12 * windows * rows * D * D) // 16,
            bytes_accessed=(4 * D * D + 20 * windows * rows * D) // 16,
            transcendentals=0,
        ),
    )(*moving, vectors, weights[1])


def dense_back_kernel(
    core_ref,
    upstream_ref,
    grad_conv_ref,
    first_ref,
    last_ref,
    slope_ref,
    hidden_ref,
    vectors_ref,
    w_out_ref,
    w_left_ref,
    w_right_ref,
    w_down_ref,
    skip_grad_ref,
    grad_mid_ref,
    grad_down_ref,
    grad_before_ref,
    grad_att_ref,
    own_a,
    own_b,
    other_a,
    other_b,
    sums_ref,
    up_sums_ref,
    doubled,
    *,
    count,
    rows,
):
    core = core_ref[0]
    total = count * rows
    width = own_a.shape[2]

    @pl.when(pl.program_id(0) == 0)
    def _():
        sums_ref[...] = jnp.zeros_like(sums_ref)
        up_sums_ref[...] = jnp.zeros_like(up_sums_ref)

    grads = []
    for window in range(count):
        here = grad_conv_ref[window].astype(jnp.float32)
        earlier, later = shifted(
            here, first_ref[window].astype(jnp.float32), last_ref[window].astype(jnp.float32)
        )
        skip_grad = (
            upstream_ref[window].astype(jnp.float32)
            + vectors_ref[7:8, :] * later
            + vectors_ref[8:9, :] * here
            + vectors_ref[9:10, :] * earlier
        )
        skip_grad_ref[window] = skip_grad
        for number in range(D // LANES):
            doubled[number] = skip_grad[:, number * LANES : (number + 1) * LANES]
        grads.append(
            jnp.concatenate(
                [
                    doubled[number, pl.ds(0, rows, stride=2), :]
                    + doubled[number, pl.ds(1, rows, stride=2), :]
                    for number in range(D // LANES)
                ],
                axis=1,
            )
        )
    grad = jnp.concatenate(grads, axis=0)
    low = grad.astype(jnp.bfloat16)
    grad_down_ref[...] = low.reshape(count, rows, D)
    sums_ref[0:1, :] = sums_ref[0:1, :] + jnp.sum(
        low.astype(jnp.float32), axis=0, keepdims=True
    )
    grad_norm = jnp.zeros((total, D), jnp.float32)
    for number in range(FF // WIDE):
        span = slice(number * WIDE, (number + 1) * WIDE)
        half = (w_left_ref, w_right_ref)[number * WIDE // D]
        start = number * WIDE % D
        units = slice(number * WIDE // 32, (number + 1) * WIDE // 32)
        slope = slope_ref[:, :, span].reshape(total, WIDE).astype(jnp.float32)
        grad_active = times_transposed(low, w_down_ref[units].reshape(WIDE, D))
        grad_before = (grad_active * slope).astype(jnp.bfloat16)
        grad_before_ref[:, :, span] = grad_before.reshape(count, rows, WIDE)
        up_sums_ref[0:1, span] = up_sums_ref[0:1, span] + jnp.sum(
            grad_before.astype(jnp.float32), axis=0, keepdims=True
        )
        grad_norm = grad_norm + times_transposed(
            grad_before, half[:, 0, :, start : start + WIDE].reshape(D, WIDE)
        )
    hidden = hidden_ref[...].reshape(total, D)
    gain = vectors_ref[2:3, :]
    _, stats, inverse = layer_stats(hidden, gain, vectors_ref[3:4, :])
    sums_ref[1:2, :] = sums_ref[1:2, :] + jnp.sum(grad_norm * stats, axis=0, keepdims=True)
    sums_ref[2:3, :] = sums_ref[2:3, :] + jnp.sum(grad_norm, axis=0, keepdims=True)
    mid = grad + norm_back(grad_norm, stats, inverse, gain)
    grad_mid_ref[...] = mid.reshape(count, rows, D)
    mid_low = mid.astype(jnp.bfloat16)
    grad_att_ref[...] = mid_low.reshape(count, rows, D)
    sums_ref[3:4, :] = sums_ref[3:4, :] + jnp.sum(
        mid_low.astype(jnp.float32), axis=0, keepdims=True
    )
    for number, piece in enumerate((own_a, own_b, other_a, other_b)):
        group = core if number < 2 else 1 - core
        unit = group * 24 + (number % 2) * 12
        piece[...] = (
            times_transposed(mid_low, w_out_ref[pl.ds(unit, 12)].reshape(width, D))
            .astype(jnp.bfloat16)
            .reshape(count, rows, width)
        )


def dense_backward(
    core, upstream, grad_conv, first, last, slope, hidden, vectors, weights
):
    windows, rows, _ = hidden.shape
    count = max(1, 256 // rows)
    width = H * VD // 4
    shapes = (
        [
            jax.ShapeDtypeStruct((windows, 2 * rows, D), jnp.float32),
            jax.ShapeDtypeStruct((windows, rows, D), jnp.float32),
            jax.ShapeDtypeStruct((windows, rows, D), jnp.bfloat16),
            jax.ShapeDtypeStruct((windows, rows, FF), jnp.bfloat16),
            jax.ShapeDtypeStruct((windows, rows, D), jnp.bfloat16),
        ]
        + [jax.ShapeDtypeStruct((windows, rows, width), jnp.bfloat16)] * 4
        + [jax.ShapeDtypeStruct((8, D), jnp.float32), jax.ShapeDtypeStruct((8, FF), jnp.float32)]
    )
    moving = (upstream, grad_conv, first, last, slope, hidden)
    lower, upper, w_up = weights
    return pl.pallas_call(
        functools.partial(dense_back_kernel, count=count, rows=rows),
        grid=(windows // count,),
        in_specs=[pl.BlockSpec(memory_space=pltpu.SMEM)]
        + [step_block(array, count) for array in moving]
        + [whole_block(vectors)]
        + [unit_rows(*OUT_ROWS), up_half(0), up_half(1), unit_rows(*DOWN_ROWS)],
        out_specs=[step_block(shape, count) for shape in shapes[:9]]
        + [whole_block(shape) for shape in shapes[9:]],
        out_shape=shapes,
        scratch_shapes=[pltpu.VMEM((D // LANES, 2 * rows, LANES), jnp.float32)],
        compiler_params=pltpu.CompilerParams(vmem_limit_bytes=62 * 2**20),
        cost_estimate=pl.CostEstimate(
            flops=(2 * windows * rows * D * (D + 2 * FF)) // 16,
            bytes_accessed=(2 * D * (D + 2 * FF) + 40 * windows * rows * D) // 16,
            transcendentals=0,
        ),
    )(core, *moving, vectors, lower, w_up, w_up, upper)


def weight_grad_kernel(left_ref, right_ref, *refs):
    out_ref = refs[-1]
    total = left_ref.shape[0] * left_ref.shape[1]
    left = left_ref[...].reshape(total, left_ref.shape[2])
    right = right_ref[...].reshape(total, D)
    out_ref[...] = (
        jnp.dot(left.T, right, preferred_element_type=jnp.float32)
        .astype(jnp.bfloat16)
        .reshape(out_ref.shape)
    )


def weight_grad(left, right, held, place):
    windows, rows, depth = left.shape
    halves = right.shape[2] // D
    step = D // 4
    count = step // UNIT // (2 // halves)
    first = place[0][0] * place[1][0] // count
    return pl.pallas_call(
        weight_grad_kernel,
        grid=(halves, depth // step),
        in_specs=[
            pl.BlockSpec((windows, rows, step), lambda h, m: (0, 0, m)),
            pl.BlockSpec((windows, rows, D), lambda h, m: (0, 0, h)),
            pl.BlockSpec(memory_space=pl.ANY),
        ],
        out_specs=pl.BlockSpec(
            (count, 2 // halves, UNIT, D), lambda h, m: (first + m, h, 0, 0)
        ),
        out_shape=jax.ShapeDtypeStruct(held.shape, held.dtype),
        input_output_aliases={2: 0},
        compiler_params=pltpu.CompilerParams(vmem_limit_bytes=48 * 2**20),
        cost_estimate=pl.CostEstimate(
            flops=(2 * windows * rows * depth * right.shape[2]) // 16,
            bytes_accessed=(2 * (windows * rows * (depth + right.shape[2]) + depth * right.shape[2])) // 16,
            transcendentals=0,
        ),
    )(left, right, held)


def ordered(own, other, is_first, axis):
    return jnp.concatenate(
        [jnp.where(is_first, own, other), jnp.where(is_first, other, own)], axis=axis
    )


class Places:
    def __init__(self, windows, local_rows):
        self.dp = lax.axis_size("dp")
        self.seq = lax.axis_size("seq")
        self.windows = windows
        self.rows = local_rows
        self.length = local_rows * self.seq
        self.group = self.seq // (2 * windows)
        self.heads = H // (2 * self.group)
        self.core = lax.axis_index("dp") % 2
        self.is_first = self.core == 0
        self.place = lax.axis_index("seq") % self.group
        self.part = self.rows // (2 * self.group)
        self.head_start = (self.core * self.group + self.place) * self.heads

    def swap(self, array):
        return lax.ppermute(array, "dp", [(i, i ^ 1) for i in range(self.dp)])

    def rows_to_windows(self, own):
        kept, sent = own
        return ordered(kept, self.swap(sent), self.is_first, 0)

    def halves(self, array, axis):
        size = array.shape[axis] // 2
        kept = lax.dynamic_slice_in_dim(array, self.core * size, size, axis)
        sent = lax.dynamic_slice_in_dim(array, (1 - self.core) * size, size, axis)
        return (kept, sent)

    def exchange(self, array):
        return lax.all_to_all(array, "seq", split_axis=0, concat_axis=0, tiled=True)

    def inputs_to_windows(self, inputs):
        both = self.rows_to_windows(self.halves(inputs, 1))
        return both.reshape(self.seq, self.part, inputs.shape[2])

    def gather_rows(self, array):
        features = array.shape[2]
        array = array[:, None]
        if self.group > 1:
            hops = [
                (i, i - i % self.group + (i + 1) % self.group) for i in range(self.seq)
            ]
            pieces = [array]
            for _ in range(self.group - 1):
                pieces.append(lax.ppermute(pieces[-1], "seq", hops))
            pieces = jnp.concatenate(pieces, axis=1)
            order = (self.place - jnp.arange(self.group)) % self.group
            array = jnp.take(pieces, order, axis=1)
        array = ordered(
            array[:, None], self.swap(array)[:, None], self.is_first, 1
        )
        return array.reshape(self.length, features)

    def sum_rows(self, partial):
        features = partial.shape[1]
        partial = partial.reshape(self.seq, 2, self.group * self.part, features)
        kept, sent = self.halves(partial, 1)
        total = kept[:, 0].astype(jnp.float32) + self.swap(
            sent[:, 0].astype(jnp.bfloat16)
        ).astype(jnp.float32)
        if self.group > 1:
            total = lax.psum_scatter(
                total.reshape(self.seq, self.group, self.part, features),
                "seq",
                scatter_dimension=1,
                axis_index_groups=[
                    list(range(i, i + self.group)) for i in range(0, self.seq, self.group)
                ],
                tiled=True,
            )
            total = total[:, 0]
        return total.astype(jnp.bfloat16)

    def sums_to_rows(self, array):
        features = array.shape[2]
        back = array.reshape(2 * self.windows, self.group * self.part, features)
        kept, sent = self.halves(back, 0)
        return ordered(kept, self.swap(sent), self.is_first, 1)

    def heads_to_rows(self, chunk):
        count = chunk.shape[1]
        back = self.exchange(chunk.reshape(self.seq, self.rows, count))
        kept, sent = self.halves(
            back.reshape(2 * self.windows, self.group, self.rows, count), 0
        )
        return (kept, self.swap(sent))

    def rows_to_heads(self, kept, sent):
        count = kept.shape[3]
        both = self.rows_to_windows((kept, sent))
        back = self.exchange(both.reshape(self.seq, self.rows, count))
        return back.reshape(self.length, count)


def bias_tables(special, at):
    length, own = (at.length, at.heads)
    pos_low = special[: F * H].reshape(F, H)
    pos_basis = position_basis(length)
    own_pos = lax.dynamic_slice_in_dim(pos_low, at.head_start, own, 1)
    tables = jnp.dot(own_pos.T, pos_basis.T, precision=highest)
    tables = jnp.roll(jnp.pad(tables, ((0, 0), (0, 1))), 1 - BLOCK, axis=1)
    tables = jnp.broadcast_to(tables[:, None, :], (own, 8, 2 * length))
    return (pos_basis, tables)


def gather_weights(params, sent, at):
    devices = lax.axis_size(("dp", "seq"))
    index = lax.axis_index(("dp", "seq"))
    dp, seq = lax.axis_size("dp"), lax.axis_size("seq")
    shard = params.shape[0]
    own_rows = ROWS // devices
    extra = shard - own_rows * D
    rest = extra * devices
    tail = params[shard - TAIL :].astype(jnp.bfloat16)
    before = lax.ppermute(tail, ("dp", "seq"), [(i, i + 1) for i in range(devices - 1)])
    joined = jnp.concatenate([before.astype(jnp.float32), params])
    piece = lax.dynamic_slice_in_dim(joined, TAIL - extra * index, own_rows * D)
    piece = piece.astype(jnp.bfloat16).reshape(own_rows, D)
    special = jnp.where(index == devices - 1, tail, jnp.zeros_like(tail))
    for axis, bit in axis_bits("dp"):
        special = special + partner(special, axis, bit)
    special = jnp.broadcast_to(special.reshape(1, TAIL // D, D), (seq, TAIL // D, D))
    special = lax.all_to_all(special, "seq", split_axis=0, concat_axis=0, tiled=True)[seq - 1]
    special, sent = lax.optimization_barrier((special, sent))
    ready = lax.all_to_all(sent, "seq", split_axis=0, concat_axis=0, tiled=True)
    special = special.astype(jnp.float32).reshape(-1)[TAIL - rest :]
    pos_basis, tables = bias_tables(special, at)
    if own_rows % UNIT == 0:
        here = piece.reshape(own_rows // UNIT, UNIT, D)
        other = jnp.swapaxes(piece.reshape(own_rows // UNIT, 8, 2, D), 1, 2).reshape(here.shape)
        row = own_rows * index + UNIT * jnp.arange(own_rows // UNIT)
        inside = (row >= UP_ROWS[0]) & (row < UP_ROWS[0] + UP_ROWS[1])
        piece = jnp.where(inside[:, None, None], other, here).reshape(piece.shape)
    half = own_rows // 2
    if dp == 2 and half % 8 == 0:
        second = lax.axis_index("dp") == 1
        given = jnp.where(second, piece[:half], piece[half:])
        taken = partner(given, "dp", 0)
        low = jnp.where(second, taken, piece[:half])
        high = jnp.where(second, piece[half:], taken)
        lower = lax.all_gather(low, ("seq", "dp"), axis=0, tiled=True)
        high, lower, ready, tables = lax.optimization_barrier((high, lower, ready, tables))
        upper = lax.all_gather(high, ("seq", "dp"), axis=0, tiled=True)
    else:
        everything = lax.all_gather(piece, ("dp", "seq"), axis=0, tiled=True)
        lower, upper = (everything[: ROWS // 2], everything[ROWS // 2 :])
    if own_rows % UNIT == 0:
        w_up = up_units(lower.reshape(-1, UNIT, D), upper.reshape(-1, UNIT, D))
    else:
        w_up = jnp.concatenate([lower[UP_ROWS[0] :], upper[: UP_ROWS[0] + UP_ROWS[1] - ROWS // 2]])
        w_up = jnp.swapaxes(w_up.reshape(96, UNIT, 2, D), 1, 2)
    views = [array.reshape(-1, 2, UNIT, D) for array in (lower, upper)]
    return (lower, (*views, w_up), special, ready, pos_basis, tables)


def axis_bits(axis):
    return [(axis, bit) for bit in range(lax.axis_size(axis).bit_length() - 2, -1, -1)]


def partner(array, axis, bit):
    pairs = [(i, i ^ (1 << bit)) for i in range(lax.axis_size(axis))]
    return lax.ppermute(array, axis, pairs)


def turned(number):
    along = axis_bits("seq")[::-1]
    return (along, along[1:2] + along[:1] + along[2:], along[2:] + along[:2])[number % 3]


def halves_apart(rows, first, outer, inner):
    units = rows.shape[0] // (2 * UNIT)
    here = rows.reshape(units, 2 * UNIT, D)
    other = jnp.swapaxes(rows.reshape(units, outer, inner, D), 1, 2).reshape(here.shape)
    inside = first + 2 * UNIT * jnp.arange(units) < 2 * D
    return jnp.where(inside[:, None, None], other, here).reshape(rows.shape)


class Sums:
    def __init__(self, rows):
        self.bits = axis_bits("dp") + axis_bits("seq")
        self.states = [rows.reshape((2,) * len(self.bits) + (-1, D))]
        self.left = [list(self.bits)]
        self.orders = [axis_bits("dp")[::-1]]
        self.steps = len(self.bits)

    def send(self):
        self.steps -= 1
        if not self.orders[0]:
            band = D // 3
            self.states = [self.states[0][..., k * band : (k + 1) * band] for k in range(3)]
            self.left = [list(self.left[0]) for _ in range(3)]
            self.orders = [turned(k) for k in range(3)]
        for k, state in enumerate(self.states):
            axis, bit = self.orders[k][0]
            self.orders[k] = self.orders[k][1:]
            dim = self.left[k].index((axis, bit))
            self.left[k].pop(dim)
            mine = (lax.axis_index(axis) >> bit) & 1
            sent = lax.dynamic_index_in_dim(state, 1 - mine, dim, False)
            kept = lax.dynamic_index_in_dim(state, mine, dim, False)
            self.states[k] = (kept, sent, axis, bit)

    def before(self, array):
        sent, array = lax.optimization_barrier(([state[1] for state in self.states], array))
        self.states = [
            (kept, there, axis, bit)
            for (kept, _, axis, bit), there in zip(self.states, sent, strict=True)
        ]
        return array

    def move(self):
        self.states = [
            (kept, partner(sent, axis, bit), axis, bit) for kept, sent, axis, bit in self.states
        ]

    def add(self):
        self.states = [
            (kept.astype(jnp.float32) + other.astype(jnp.float32)).astype(jnp.bfloat16)
            for kept, other, _, _ in self.states
        ]

    def finish(self, left=0):
        while self.steps > left:
            self.send()
            self.move()
            self.add()
        return jnp.concatenate(self.states, axis=1) if left == 0 else None


PARTS = ((4096, 6144), (2560, 1536), (10240, 1536))
QKV_PARTS = ((0, 2560),)


def moves(parts, more):
    devices = lax.axis_size(("dp", "seq"))
    own_rows = ROWS // devices
    count = sum(rows for _, rows in parts) // devices
    found, start = ([], 0)
    for first, rows in parts:
        for t in range(devices):
            low, high = (max(count * t, start), min(count * (t + 1), start + rows))
            if low >= high:
                continue
            row = first + low - start
            for i in range(devices):
                if row < own_rows * (i + 1) + more and row + high - low > own_rows * i:
                    found.append((i, t, high - low, row - own_rows * i, low - count * t))
        start += rows
    rounds = []
    for move in found:
        for held in rounds:
            if all(move[0] != other[0] and move[1] != other[1] for other in held):
                held.append(move)
                break
        else:
            rounds.append([move])
    return (rounds, count)


def per_device(values):
    index = lax.axis_index(("dp", "seq"))
    result = jnp.zeros((), jnp.int32)
    for place, value in values:
        if value != 0:
            result = jnp.where(index == place, value, result)
    return result


def to_owners(buffer, share, parts):
    rounds, most = moves(parts, TAIL // D)
    starts = [value for held in rounds for move in held for value in move[2:]]
    size = math.gcd(UNIT, MARGIN, most, buffer.shape[0], *starts)
    blocks = most // size
    share = jnp.pad(share.reshape(blocks, size, D), ((0, blocks), (0, 0), (0, 0)))
    buffer = buffer.reshape(-1, size, D)
    arrived = []
    for held in rounds:
        start = per_device([(t, offset // size) for _, t, _, _, offset in held])
        arrived.append(
            lax.ppermute(
                lax.dynamic_slice_in_dim(share, start, blocks, 0),
                ("dp", "seq"),
                [(t, i) for i, t, _, _, _ in held],
            )
        )
    for held, moved in zip(rounds, arrived, strict=True):
        place = per_device([(i, (MARGIN + low) // size) for i, _, _, low, _ in held])
        count = per_device([(i, rows // size) for i, _, rows, _, _ in held])
        inside = jnp.arange(blocks) < count
        moved = jnp.where(inside[:, None, None], moved, jnp.zeros_like(moved))
        there = lax.dynamic_slice_in_dim(buffer, place, blocks, 0)
        buffer = lax.dynamic_update_slice_in_dim(buffer, there + moved, place, 0)
    return buffer.reshape(-1, D)


def own_entries(buffer, special):
    devices = lax.axis_size(("dp", "seq"))
    index = lax.axis_index(("dp", "seq"))
    own_rows = ROWS // devices
    rest = special.shape[0]
    extra = rest // devices
    held = buffer[MARGIN : MARGIN + own_rows + TAIL // D].astype(jnp.float32)
    after = held[own_rows:].reshape(-1)
    after = jnp.where(index == devices - 1, jnp.pad(special, (0, TAIL - rest)), after)
    joined = jnp.concatenate([held[:own_rows].reshape(-1), after])
    return lax.dynamic_slice_in_dim(joined, extra * index, own_rows * D + extra)


def body(block_input, skip_input, species, cotangent, params, first_moment, second_moment):
    windows, local_rows, _ = block_input.shape
    at = Places(windows, local_rows)
    length = at.length
    own = at.heads
    scale = 1.0 / math.sqrt(KD)
    f32, bf16 = jnp.float32, jnp.bfloat16

    early, weights, special, moved, pos_basis, tables = gather_weights(
        params, at.inputs_to_windows(block_input), at
    )
    up_bias = special[F * H : F * H + FF]
    vectors = special[F * H + FF :].reshape(12, D)

    def columns(matrix, width):
        return lax.dynamic_slice_in_dim(matrix, at.head_start * width, own * width, 1)

    w_own = jnp.concatenate(
        [
            columns(early[:512].reshape(D, H * KD), KD) * jnp.asarray(scale, bf16),
            columns(early[512:1024].reshape(D, H * KD), KD),
            columns(early[1024:2560].reshape(D, H * VD), VD),
        ],
        axis=1,
    )
    low_part, _, _ = layer_stats(moved.astype(f32), vectors[0], vectors[1])
    low_all = at.gather_rows(low_part.astype(bf16))
    projected = jnp.einsum("rd,dk->kr", low_all, w_own, preferred_element_type=f32).astype(bf16)
    queries, keys, values = (
        projected[: own * KD],
        projected[own * KD : 2 * own * KD],
        projected[2 * own * KD :],
    )

    operands, saved, pieces = ([], [], ([], []))
    for pair in range(own // PAIR):
        narrow = slice(pair * PAIR * KD, (pair + 1) * PAIR * KD)
        wide = slice(pair * PAIR * VD, (pair + 1) * PAIR * VD)
        given = (
            tables[pair * PAIR : (pair + 1) * PAIR],
            queries[narrow],
            keys[narrow],
            values[wide],
        )
        result, log_total = attention_forward(*given)
        operands.append(given)
        saved.append((result, log_total))
        for held, part in zip(pieces, at.heads_to_rows(result), strict=True):
            held.append(part)
    pairs = own // PAIR
    pieces = [
        held[pair][:, place] for held in pieces for place in range(at.group) for pair in range(pairs)
    ]

    core = jnp.asarray(at.core, jnp.int32).reshape(1)
    heads, hidden_one, low_two, activated, slope, hidden_two = dense_forward(
        core, block_input, pieces, vectors, up_bias[None], weights
    )
    ends = [
        (hidden_two[:, row : row + 1] + skip_input[:, up : up + 1].astype(f32)).astype(bf16)
        for row, up in ((0, 0), (local_rows - 1, 2 * local_rows - 1))
    ]
    first, last = edge_rows(ends)
    is_mouse = (species == 1).astype(f32)[:, None]
    species_gain = (1.0 - is_mouse) * vectors[10] + is_mouse * vectors[11]
    block_out, grad_conv, dense_grads, gain_rows, point_sums = point_layer(
        hidden_two,
        skip_input,
        cotangent,
        first,
        last,
        species_gain[:, None, :],
        vectors,
        weights,
    )
    gain_rows = gain_rows[:, 0]
    grad_human = jnp.sum((1.0 - is_mouse) * gain_rows, axis=0)
    grad_mouse = jnp.sum(is_mouse * gain_rows, axis=0)
    first, last = edge_rows([grad_conv[:, :1], grad_conv[:, 2 * local_rows - 1 :]])
    (
        skip_grad,
        grad_mid,
        grad_down_low,
        grad_before,
        grad_attn_low,
        *grad_pieces,
        dense_sums,
        up_sums,
    ) = dense_backward(
        core,
        cotangent,
        grad_conv,
        first,
        last,
        slope,
        hidden_one,
        vectors,
        weights,
    )
    grad_pieces = [
        jnp.stack(
            [
                grad_pieces[2 * group + place * pairs + pair]
                for place in range(at.group)
            ],
            axis=1,
        )
        for group in range(2)
        for pair in range(pairs)
    ]

    middle = jnp.concatenate(
        [
            up_sums[0],
            dense_sums[1],
            dense_sums[2],
            dense_sums[3],
            dense_sums[0],
            point_sums[:4].reshape(-1),
            grad_human,
            grad_mouse,
        ]
    )
    devices = lax.axis_size(("dp", "seq"))
    chunks = [at.rows_to_heads(grad_pieces[pair], grad_pieces[pairs + pair]) for pair in range(pairs)]
    dense_grads = weight_grad(activated, grad_down_low, dense_grads, DOWN)
    dense_grads = weight_grad(low_two, grad_before, dense_grads, LEFT)
    dense_grads = weight_grad(heads, grad_attn_low, dense_grads, OUT).reshape(-1, D)
    even = dense_grads.shape[0] // devices % (2 * UNIT) == 0
    if not even:
        dense_grads = halves_apart(dense_grads, 0, 2, UNIT)
    dense_grads, chunks[0] = lax.optimization_barrier((dense_grads, chunks[0]))
    dense = lax.psum_scatter(dense_grads, ("dp", "seq"), scatter_dimension=0, tiled=True)

    dq, dk, dv, dt = ([], [], [], [])
    for pair in range(pairs):
        result, log_total = saved[pair]
        grads = attention_backward(*operands[pair], result, chunks[pair], log_total)
        if pair + 1 < pairs:
            grads, chunks[pair + 1] = lax.optimization_barrier((grads, chunks[pair + 1]))
        for piece, held in zip(grads, (dq, dk, dv, dt), strict=True):
            held.append(piece)
    grad_own = jnp.concatenate(dq + dk + dv, axis=1)
    partial = jnp.einsum("rk,dk->rd", grad_own, w_own, preferred_element_type=f32).astype(bf16)
    partial, grad_own = lax.optimization_barrier((partial, grad_own))
    back = at.exchange(at.sum_rows(partial))
    grad_w_own = jnp.einsum("rd,rk->dk", low_all, grad_own, preferred_element_type=f32)
    grad_w_query = grad_w_own[:, : own * KD] * scale
    grad_w_key = grad_w_own[:, own * KD : 2 * own * KD]
    grad_w_value = grad_w_own[:, 2 * own * KD :]

    def all_columns(matrix, width):
        whole = jnp.zeros((D, H * width), bf16)
        return lax.dynamic_update_slice_in_dim(
            whole, matrix.astype(bf16), at.head_start * width, 1
        ).reshape(-1, D)

    first_rows = jnp.concatenate(
        [
            all_columns(grad_w_query, KD),
            all_columns(grad_w_key, KD),
            all_columns(grad_w_value, VD),
        ],
        axis=0,
    )
    first_sums = Sums(first_rows)
    first_sums.finish(2)
    first_sums.states, back = lax.optimization_barrier((first_sums.states, back))
    grad_norm_one = at.sums_to_rows(back).astype(f32)
    _, stats_one, inverse_one = layer_stats(block_input.astype(f32), vectors[0], vectors[1])
    input_grad = grad_mid + norm_back(grad_norm_one, stats_one, inverse_one, vectors[0])
    grad_gain_one = jnp.sum(grad_norm_one * stats_one, axis=(0, 1))
    grad_bias_one = jnp.sum(grad_norm_one, axis=(0, 1))
    grad_tables = jnp.roll(jnp.concatenate(dt, axis=0), BLOCK - 1, axis=1)[:, : 2 * length - 1]
    grad_pos = jnp.dot(pos_basis.T, grad_tables.T, precision=highest)
    grad_pos = lax.dynamic_update_slice_in_dim(
        jnp.zeros((F, H), f32), grad_pos, at.head_start, 1
    )
    late = jnp.concatenate([grad_pos.reshape(-1), grad_gain_one, grad_bias_one])
    summed = jnp.concatenate([late, middle])
    for axis, bit in axis_bits("dp") + axis_bits("seq"):
        summed = summed + partner(summed, axis, bit)
    late, middle = (summed[: late.shape[0]], summed[late.shape[0] :])
    special_grads = jnp.concatenate(
        [late[: F * H], middle[:FF], late[F * H :], middle[FF:]]
    )
    share = dense
    if even:
        share = halves_apart(share, lax.axis_index(("dp", "seq")) * share.shape[0], 2, UNIT)
    buffer = jnp.zeros((ROWS // devices + TAIL // D + 2 * MARGIN, D), bf16)
    buffer = to_owners(buffer, share, PARTS)
    buffer = to_owners(buffer, first_sums.finish(), QKV_PARTS)
    reduced = own_entries(buffer, special_grads)
    shard_len = params.shape[0]
    position = lax.axis_index(("dp", "seq")) * shard_len + jnp.arange(shard_len)
    param_new, first_new, second_new = adam_update(
        params, first_moment, second_moment, reduced, position
    )
    return (
        block_out,
        input_grad,
        skip_grad,
        param_new,
        first_new,
        second_new,
        param_new.astype(bf16),
    )


def solution(mesh):
    return jax.shard_map(
        body,
        mesh=mesh,
        in_specs=(
            P("dp", "seq", None),
            P("dp", "seq", None),
            P("dp"),
            P("dp", "seq", None),
            P(("dp", "seq")),
            P(("dp", "seq")),
            P(("dp", "seq")),
        ),
        out_specs=(
            P("dp", "seq", None),
            P("dp", "seq", None),
            P("dp", "seq", None),
            P(("dp", "seq")),
            P(("dp", "seq")),
            P(("dp", "seq")),
            P(("dp", "seq")),
        ),
        check_vma=False,
    )
```

```python
import functools
import math

import jax
import jax.numpy as jnp
from jax import lax
from jax.experimental import pallas as pl
from jax.experimental.pallas import tpu as pltpu
from jax.sharding import PartitionSpec as P

D = 1536
H = 8
KD = 64
VD = 192
FF = 3072
F = 192
STEP = 10
BLOCK = 256
PAIR = 2
CHUNK = 512
WIDE = 768
LANES = 128
ROWS = 11776
QKV_ROWS = 2560
TAIL = 24576
MARGIN = 288
UNIT = 16
UNITS = 288


eps_norm = 1e-05
beta_one = 0.5
beta_two = 0.5
adam_eps = 1e-08
decay_rate = 0.01
highest = lax.Precision.HIGHEST


def edge_rows(array):
    devices = lax.axis_size("seq")
    up = [(i, i + 1) for i in range(devices - 1)]
    first = lax.ppermute(array[1], "seq", up)
    last = lax.ppermute(array[0], "seq", [(j, i) for i, j in up])
    return (first, last)


def segment_ends():
    counts = [
        D * H * KD,
        D * H * KD,
        D * H * VD,
        H * VD * D,
        D * FF,
        FF * D,
        D * D,
        F * H,
        FF,
        12 * D,
    ]
    limits = []
    running = 0
    for amount in counts:
        running = running + amount
        limits.append(running)
    return limits


def rate_at(position):
    limits = segment_ends()
    step_rates = [
        2.0 / math.sqrt(D),
        2.0 / math.sqrt(D),
        2.0 / math.sqrt(D),
        8.0 / math.sqrt(H * VD),
        2.0 / math.sqrt(D),
        2.0 / math.sqrt(FF),
        2.0 / math.sqrt(D),
        3.0 / math.sqrt(F),
        0.4,
        0.4,
    ]
    result = jnp.full(position.shape, step_rates[-1], jnp.float32)
    for segment in range(len(limits) - 2, -1, -1):
        result = jnp.where(position < limits[segment], step_rates[segment], result)
    return result


def adam_update(param_old, first_old, second_old, gradient, position):
    step_rate = rate_at(position)
    first_new = beta_one * first_old + (1.0 - beta_one) * gradient
    second_new = beta_two * second_old + (1.0 - beta_two) * gradient * gradient
    first_hat = first_new / (1.0 - beta_one**STEP)
    second_hat = second_new / (1.0 - beta_two**STEP)
    param_new = param_old - step_rate * (
        first_hat / (jnp.sqrt(second_hat) + adam_eps) + decay_rate * param_old
    )
    return (param_new, first_new, second_new)


def position_basis(length):
    offsets = jnp.arange(2 * length - 1).astype(jnp.float32) - (length - 1)
    halves = F // 2
    ladder = jnp.arange(halves).astype(jnp.float32) / max(halves - 1, 1)
    lifetimes = jnp.exp(ladder * math.log(length))
    decays = jnp.exp(-jnp.abs(offsets)[:, None] * (math.log(2.0) / lifetimes)[None, :])
    return jnp.concatenate([decays, jnp.sign(offsets)[:, None] * decays], axis=1)


def layer_stats(inputs, norm_gain, norm_bias):
    centered = inputs - jnp.mean(inputs, axis=-1, keepdims=True)
    inverse = lax.rsqrt(jnp.mean(centered * centered, axis=-1, keepdims=True) + eps_norm)
    normed = centered * inverse
    return (normed * norm_gain + norm_bias, normed, inverse)


def norm_back(upstream, normed, inverse, norm_gain):
    scaled = upstream * norm_gain
    return inverse * (
        scaled
        - jnp.mean(scaled, axis=-1, keepdims=True)
        - normed * jnp.mean(scaled * normed, axis=-1, keepdims=True)
    )


def spread_rows(first_row, bands):
    start = pltpu.roll(first_row, 0, 1, stride=1, stride_axis=0)
    bands[0:8, :] = start
    height = 8
    while height < BLOCK:
        bands[height : 2 * height, :] = pltpu.roll(bands[0:height, :], height, 1)
        height *= 2


def collect_rows(bands, width):
    height = BLOCK // 2
    while height >= 8:
        bands[0:height, :] = bands[0:height, :] + pltpu.roll(
            bands[height : 2 * height, :], width - height, 1
        )
        height //= 2
    total = bands[0:1, :]
    for row in range(1, 8):
        total = total + pltpu.roll(bands[row : row + 1, :], width - row, 1)
    return total


def forward_kernel(
    table_ref, q_ref, k_ref, v_ref, out_ref, lse_ref, bands, key_rows, scores, *, blocks
):
    block = pl.program_id(0)

    @pl.when(block == 0)
    def _():
        for head in range(PAIR):
            spread_rows(table_ref[head], bands.at[head])
            key_rows[head] = k_ref[head * KD : (head + 1) * KD, :].T

    results = []
    for head in range(PAIR):
        queries = q_ref[head * KD : (head + 1) * KD, :]
        top = jnp.full((1, BLOCK), -jnp.inf, jnp.float32)
        for j in range(blocks):
            at = pl.multiple_of((block - j + blocks - 1) * BLOCK, BLOCK)
            span = slice(j * BLOCK, (j + 1) * BLOCK)
            part = (
                jnp.dot(key_rows[head, span, :], queries, preferred_element_type=jnp.float32)
                + bands[head, :, pl.ds(at, BLOCK)]
            )
            scores[span, :] = part
            top = jnp.maximum(top, jnp.max(part, axis=0, keepdims=True))
        total = jnp.zeros((1, BLOCK), jnp.float32)
        result = jnp.zeros((VD, BLOCK), jnp.float32)
        for j in range(blocks):
            span = slice(j * BLOCK, (j + 1) * BLOCK)
            grown = jnp.exp(scores[span, :] - top)
            total = total + jnp.sum(grown, axis=0, keepdims=True)
            result = result + jnp.dot(
                v_ref[head * VD : (head + 1) * VD, span],
                grown.astype(jnp.bfloat16),
                preferred_element_type=jnp.float32,
            )
        results.append(result * (1.0 / total))
        lse_ref[head : head + 1, :] = top + jnp.log(total)
    out_ref[...] = jnp.concatenate(results, axis=0).T.astype(jnp.bfloat16)


def attention_forward(tables, queries, keys, values):
    length = keys.shape[1]
    blocks = length // BLOCK
    return pl.pallas_call(
        functools.partial(forward_kernel, blocks=blocks),
        grid=(blocks,),
        in_specs=[
            pl.BlockSpec((PAIR, 8, 2 * length), lambda i: (0, 0, 0)),
            pl.BlockSpec((PAIR * KD, BLOCK), lambda i: (0, i)),
            pl.BlockSpec((PAIR * KD, length), lambda i: (0, 0)),
            pl.BlockSpec((PAIR * VD, length), lambda i: (0, 0)),
        ],
        out_specs=[
            pl.BlockSpec((BLOCK, PAIR * VD), lambda i: (i, 0)),
            pl.BlockSpec((PAIR, BLOCK), lambda i: (0, i)),
        ],
        out_shape=[
            jax.ShapeDtypeStruct((length, PAIR * VD), jnp.bfloat16),
            jax.ShapeDtypeStruct((PAIR, length), jnp.float32),
        ],
        scratch_shapes=[
            pltpu.VMEM((PAIR, BLOCK, 2 * length), jnp.float32),
            pltpu.VMEM((PAIR, length, KD), jnp.bfloat16),
            pltpu.VMEM((length, BLOCK), jnp.float32),
        ],
        compiler_params=pltpu.CompilerParams(vmem_limit_bytes=48 * 2**20),
        cost_estimate=pl.CostEstimate(
            flops=(4 * PAIR * length * length * 256) // 16,
            bytes_accessed=(8 * PAIR * length * (KD + VD)) // 16,
            transcendentals=PAIR * length * length // 16,
        ),
    )(tables, queries, keys, values)


def backward_kernel(
    table_ref,
    q_ref,
    k_ref,
    v_ref,
    out_ref,
    grad_ref,
    lse_ref,
    dq_ref,
    dk_ref,
    dv_ref,
    dt_ref,
    bands,
    grad_bands,
    key_rows,
    value_rows,
    dk_sum,
    dv_sum,
    *,
    blocks,
):
    block = pl.program_id(0)

    @pl.when(block == 0)
    def _():
        for head in range(PAIR):
            spread_rows(table_ref[head], bands.at[head])
            key_rows[head] = k_ref[head * KD : (head + 1) * KD, :].T
            value_rows[head] = v_ref[head * VD : (head + 1) * VD, :].T
        grad_bands[...] = jnp.zeros_like(grad_bands)
        dk_sum[...] = jnp.zeros_like(dk_sum)
        dv_sum[...] = jnp.zeros_like(dv_sum)

    grad_t = grad_ref[...].T
    out_t = out_ref[...].T
    products = grad_t.astype(jnp.float32) * out_t.astype(jnp.float32)
    results = []
    for head in range(PAIR):
        wide = slice(head * VD, (head + 1) * VD)
        delta = jnp.sum(products[wide, :], axis=0, keepdims=True)
        grad_here = grad_t[wide, :]
        grad_rows = grad_here.T
        queries = q_ref[head * KD : (head + 1) * KD, :]
        query_rows = queries.T
        lse = lse_ref[head : head + 1, :]
        dq = jnp.zeros((KD, BLOCK), jnp.float32)
        for j in range(blocks):
            span = slice(j * BLOCK, (j + 1) * BLOCK)
            at = pl.multiple_of((block - j + blocks - 1) * BLOCK, BLOCK)
            part = (
                jnp.dot(key_rows[head, span, :], queries, preferred_element_type=jnp.float32)
                + bands[head, :, pl.ds(at, BLOCK)]
            )
            soft = jnp.exp(part - lse)
            grad_soft = jnp.dot(
                value_rows[head, span, :], grad_here, preferred_element_type=jnp.float32
            )
            grad_scores = soft * (grad_soft - delta)
            grad_bands[head, :, pl.ds(at, BLOCK)] = (
                grad_bands[head, :, pl.ds(at, BLOCK)] + grad_scores
            )
            low = grad_scores.astype(jnp.bfloat16)
            dv_sum[head, span, :] = dv_sum[head, span, :] + jnp.dot(
                soft.astype(jnp.bfloat16), grad_rows, preferred_element_type=jnp.float32
            )
            dk_sum[head, span, :] = dk_sum[head, span, :] + jnp.dot(
                low, query_rows, preferred_element_type=jnp.float32
            )
            dq = dq + jnp.dot(
                k_ref[head * KD : (head + 1) * KD, span], low, preferred_element_type=jnp.float32
            )
        results.append(dq)
    dq_ref[...] = jnp.concatenate(results, axis=0).T.astype(jnp.bfloat16)

    @pl.when(block == blocks - 1)
    def _():
        dk_ref[...] = jnp.concatenate(
            [dk_sum[head] for head in range(PAIR)], axis=1
        ).astype(jnp.bfloat16)
        dv_ref[...] = jnp.concatenate(
            [dv_sum[head] for head in range(PAIR)], axis=1
        ).astype(jnp.bfloat16)
        for head in range(PAIR):
            dt_ref[head : head + 1, :] = collect_rows(
                grad_bands.at[head], grad_bands.shape[2]
            )


def attention_backward(tables, queries, keys, values, heads, grad_heads, lse):
    length = keys.shape[1]
    blocks = length // BLOCK
    return pl.pallas_call(
        functools.partial(backward_kernel, blocks=blocks),
        grid=(blocks,),
        in_specs=[
            pl.BlockSpec((PAIR, 8, 2 * length), lambda i: (0, 0, 0)),
            pl.BlockSpec((PAIR * KD, BLOCK), lambda i: (0, i)),
            pl.BlockSpec((PAIR * KD, length), lambda i: (0, 0)),
            pl.BlockSpec((PAIR * VD, length), lambda i: (0, 0)),
            pl.BlockSpec((BLOCK, PAIR * VD), lambda i: (i, 0)),
            pl.BlockSpec((BLOCK, PAIR * VD), lambda i: (i, 0)),
            pl.BlockSpec((PAIR, BLOCK), lambda i: (0, i)),
        ],
        out_specs=[
            pl.BlockSpec((BLOCK, PAIR * KD), lambda i: (i, 0)),
            pl.BlockSpec((length, PAIR * KD), lambda i: (0, 0)),
            pl.BlockSpec((length, PAIR * VD), lambda i: (0, 0)),
            pl.BlockSpec((PAIR, 2 * length), lambda i: (0, 0)),
        ],
        out_shape=[
            jax.ShapeDtypeStruct((length, PAIR * KD), jnp.bfloat16),
            jax.ShapeDtypeStruct((length, PAIR * KD), jnp.bfloat16),
            jax.ShapeDtypeStruct((length, PAIR * VD), jnp.bfloat16),
            jax.ShapeDtypeStruct((PAIR, 2 * length), jnp.float32),
        ],
        scratch_shapes=[
            pltpu.VMEM((PAIR, BLOCK, 2 * length), jnp.float32),
            pltpu.VMEM((PAIR, BLOCK, 2 * length), jnp.float32),
            pltpu.VMEM((PAIR, length, KD), jnp.bfloat16),
            pltpu.VMEM((PAIR, length, VD), jnp.bfloat16),
            pltpu.VMEM((PAIR, length, KD), jnp.float32),
            pltpu.VMEM((PAIR, length, VD), jnp.float32),
        ],
        compiler_params=pltpu.CompilerParams(vmem_limit_bytes=56 * 2**20),
        cost_estimate=pl.CostEstimate(
            flops=(10 * PAIR * length * length * 256) // 16,
            bytes_accessed=(16 * PAIR * length * (KD + VD)) // 16,
            transcendentals=PAIR * length * length // 16,
        ),
    )(tables, queries, keys, values, heads, grad_heads, lse)


def whole_block(array):
    zeros = (0,) * array.ndim
    return pl.BlockSpec(array.shape, lambda i: zeros, pipeline_mode=pl.Buffered(1))


LEFT, DOWN = ((96, 1, UNIT, D), (0, 0)), ((96, 2, UNIT, D), (1, 0))
OUT, POINT = ((48, 2, UNIT, D), (4, 0)), ((48, 2, UNIT, D), (5, 0))


def weight_block(weight):
    shape, place = weight
    return pl.BlockSpec(shape, lambda *i: place + (0, 0), pipeline_mode=pl.Buffered(1))


def up_half(half):
    return pl.BlockSpec(
        (96, 1, UNIT, D), lambda i: (0, half, 0, 0), pipeline_mode=pl.Buffered(1)
    )


def unit_rows(first, rows):
    first, units = (first // (2 * UNIT), rows // (2 * UNIT))
    return pl.BlockSpec(
        (pl.Element(units), pl.Element(2), pl.Element(UNIT), pl.Element(D)),
        lambda i: (first, 0, 0, 0),
        pipeline_mode=pl.Buffered(1),
    )


def own_weights_kernel(start_ref, q_ref, k_ref, v_a, v_b, v_c, out_ref, apart, *, own):
    start = start_ref[0]
    rows, narrow = (q_ref.shape[0], own * KD)
    for number, (ref, scale) in enumerate(((q_ref, 1.0 / math.sqrt(KD)), (k_ref, 1.0))):
        for third in range(3):
            at = pl.multiple_of(third * (H * KD) + start * KD, LANES)
            part = ref[:, pl.ds(at, narrow)].astype(jnp.float32) * scale
            for lanes in range(narrow // LANES):
                apart[lanes, pl.ds(third, rows, stride=3), :] = part[
                    :, lanes * LANES : (lanes + 1) * LANES
                ]
        for lanes in range(narrow // LANES):
            place = number * narrow + lanes * LANES
            out_ref[:, place : place + LANES] = apart[lanes].astype(jnp.bfloat16)
    at = pl.multiple_of(start * VD, LANES)
    for number, ref in enumerate((v_a, v_b, v_c)):
        out_ref[number * rows : (number + 1) * rows, 2 * narrow :] = ref[:, pl.ds(at, own * VD)]


def own_weights(rows, start, own):
    steps, narrow = (4, H * KD // 4)
    out = jax.ShapeDtypeStruct((D, own * (2 * KD + VD)), jnp.bfloat16)
    return pl.pallas_call(
        functools.partial(own_weights_kernel, own=own),
        grid=(steps,),
        in_specs=[
            pl.BlockSpec(memory_space=pltpu.SMEM),
            pl.BlockSpec((narrow, D), lambda i: (i, 0)),
            pl.BlockSpec((narrow, D), lambda i: (steps + i, 0)),
            pl.BlockSpec((narrow, D), lambda i: (2 * steps + 3 * i, 0)),
            pl.BlockSpec((narrow, D), lambda i: (2 * steps + 3 * i + 1, 0)),
            pl.BlockSpec((narrow, D), lambda i: (2 * steps + 3 * i + 2, 0)),
        ],
        out_specs=pl.BlockSpec((D // steps, out.shape[1]), lambda i: (i, 0)),
        out_shape=out,
        scratch_shapes=[pltpu.VMEM((own * KD // LANES, D // steps, LANES), jnp.float32)],
        compiler_params=pltpu.CompilerParams(vmem_limit_bytes=32 * 2**20),
    )(start, *[rows] * 5)


def up_units_kernel(lower_ref, upper_ref, out_ref, *, steps):
    units = out_ref.shape[0]

    def put(rows_ref):
        rows = rows_ref[...].astype(jnp.float32).reshape(units, 2, 2, 8, D)
        out_ref[...] = (
            jnp.swapaxes(rows, 1, 2).reshape(units, 2, UNIT, D).astype(jnp.bfloat16)
        )

    pl.when(pl.program_id(0) < steps)(lambda: put(lower_ref))
    pl.when(pl.program_id(0) >= steps)(lambda: put(upper_ref))


def up_units(lower, upper):
    units = 8
    start = UP_ROWS[0] // UNIT // (2 * units)
    steps = lower.shape[0] // (2 * units) - start
    return pl.pallas_call(
        functools.partial(up_units_kernel, steps=steps),
        grid=(96 // units,),
        in_specs=[
            pl.BlockSpec(
                (2 * units, UNIT, D), lambda i: (start + jnp.minimum(i, steps - 1), 0, 0)
            ),
            pl.BlockSpec((2 * units, UNIT, D), lambda i: (jnp.maximum(i - steps, 0), 0, 0)),
        ],
        out_specs=pl.BlockSpec((units, 2, UNIT, D), lambda i: (i, 0, 0, 0)),
        out_shape=jax.ShapeDtypeStruct((96, 2, UNIT, D), jnp.bfloat16),
        compiler_params=pltpu.CompilerParams(vmem_limit_bytes=32 * 2**20),
    )(lower, upper)


OUT_ROWS, UP_ROWS, DOWN_ROWS, POINT_ROWS = (2560, D), (4096, FF), (1280, FF), (4352, D)


def step_block(array, count):
    shape = (count,) + array.shape[1:]
    rest = (0,) * (array.ndim - 1)
    return pl.BlockSpec(shape, lambda i: (i,) + rest)


def times_transposed(left, right):
    return lax.dot_general(
        left, right, (((1,), (1,)), ((), ())), preferred_element_type=jnp.float32
    )


def dense_kernel(
    core_ref,
    inputs_ref,
    own_a,
    own_b,
    other_a,
    other_b,
    vectors_ref,
    up_bias_ref,
    w_out_ref,
    w_left_ref,
    w_right_ref,
    w_down_ref,
    heads_ref,
    hidden_ref,
    low_ref,
    active_ref,
    slope_ref,
    after_ref,
    *,
    count,
    rows,
):
    core = core_ref[0]
    total = count * rows
    width = own_a.shape[2]
    hidden = inputs_ref[...].reshape(total, D).astype(jnp.float32) + vectors_ref[4:5, :]
    for number, piece in enumerate((own_a, own_b, other_a, other_b)):
        group = core if number < 2 else 1 - core
        at = pl.multiple_of(group * (2 * width) + (number % 2) * width, 128)
        unit = group * 24 + (number % 2) * 12
        held = piece[...]
        heads_ref[:, :, pl.ds(at, width)] = held
        hidden = hidden + jnp.dot(
            held.reshape(total, width),
            w_out_ref[pl.ds(unit, 12)].reshape(width, D),
            preferred_element_type=jnp.float32,
        )
    hidden_ref[...] = hidden.reshape(count, rows, D)
    normed, _, _ = layer_stats(hidden, vectors_ref[2:3, :], vectors_ref[3:4, :])
    low = normed.astype(jnp.bfloat16)
    low_ref[...] = low.reshape(count, rows, D)
    after = hidden + vectors_ref[5:6, :]
    for number in range(FF // WIDE):
        span = slice(number * WIDE, (number + 1) * WIDE)
        half = (w_left_ref, w_right_ref)[number * WIDE // D]
        start = number * WIDE % D
        units = slice(number * WIDE // 32, (number + 1) * WIDE // 32)
        before = (
            jnp.dot(
                low,
                half[:, 0, :, start : start + WIDE].reshape(D, WIDE),
                preferred_element_type=jnp.float32,
            )
            + up_bias_ref[:, span]
        )
        phi = 0.5 * (1.0 + lax.erf(before * (1.0 / math.sqrt(2.0))))
        slope = phi + before * jnp.exp(-0.5 * before * before) * (1.0 / math.sqrt(2.0 * math.pi))
        active = (before * phi).astype(jnp.bfloat16)
        active_ref[:, :, span] = active.reshape(count, rows, WIDE)
        slope_ref[:, :, span] = slope.astype(jnp.bfloat16).reshape(count, rows, WIDE)
        after = after + jnp.dot(
            active, w_down_ref[units].reshape(WIDE, D), preferred_element_type=jnp.float32
        )
    after_ref[...] = after.reshape(count, rows, D)


def dense_forward(core, inputs, pieces, vectors, up_bias, weights):
    windows, rows, _ = inputs.shape
    count = max(1, 256 // rows)
    shapes = [
        jax.ShapeDtypeStruct((windows, rows, D), jnp.bfloat16),
        jax.ShapeDtypeStruct((windows, rows, D), jnp.float32),
        jax.ShapeDtypeStruct((windows, rows, D), jnp.bfloat16),
        jax.ShapeDtypeStruct((windows, rows, FF), jnp.bfloat16),
        jax.ShapeDtypeStruct((windows, rows, FF), jnp.bfloat16),
        jax.ShapeDtypeStruct((windows, rows, D), jnp.float32),
    ]
    lower, upper, w_up = weights
    return pl.pallas_call(
        functools.partial(dense_kernel, count=count, rows=rows),
        grid=(windows // count,),
        in_specs=[pl.BlockSpec(memory_space=pltpu.SMEM), step_block(inputs, count)]
        + [step_block(piece, count) for piece in pieces]
        + [whole_block(vectors), whole_block(up_bias)]
        + [unit_rows(*OUT_ROWS), up_half(0), up_half(1), unit_rows(*DOWN_ROWS)],
        out_specs=[step_block(shape, count) for shape in shapes],
        out_shape=shapes,
        compiler_params=pltpu.CompilerParams(vmem_limit_bytes=60 * 2**20),
        cost_estimate=pl.CostEstimate(
            flops=(2 * windows * rows * D * (D + 2 * FF)) // 16,
            bytes_accessed=(2 * D * (D + 2 * FF) + 26 * windows * rows * D) // 16,
            transcendentals=2 * windows * rows * FF // 16,
        ),
    )(core, inputs, *pieces, vectors, up_bias, lower, w_up, w_up, upper)


def shifted(rows, first, last):
    count = rows.shape[0]
    place = lax.broadcasted_iota(jnp.int32, rows.shape, 0)
    earlier = jnp.where(place == 0, first, pltpu.roll(rows, 1, 0))
    later = jnp.where(place == count - 1, last, pltpu.roll(rows, count - 1, 0))
    return (earlier, later)


def point_kernel(
    after_ref,
    skip_ref,
    upstream_ref,
    first_ref,
    last_ref,
    gain_ref,
    vectors_ref,
    w_ref,
    out_ref,
    grad_conv_ref,
    grad_w_ref,
    gain_rows_ref,
    sums_ref,
    doubled,
    summed,
    grad_w,
    *,
    rows,
):
    step = pl.program_id(0)

    @pl.when(step == 0)
    def _():
        grad_w[...] = jnp.zeros_like(grad_w)
        sums_ref[...] = jnp.zeros_like(sums_ref)

    for number in range(D // LANES):
        span = slice(number * LANES, (number + 1) * LANES)
        after = after_ref[0, :, span]
        doubled[number, pl.ds(0, rows, stride=2), :] = after
        doubled[number, pl.ds(1, rows, stride=2), :] = after
        summed[:, span] = doubled[number] + skip_ref[0, :, span].astype(jnp.float32)
    low = summed[...].astype(jnp.bfloat16).astype(jnp.float32)
    earlier, later = shifted(
        low, first_ref[0].astype(jnp.float32), last_ref[0].astype(jnp.float32)
    )
    conv = (
        vectors_ref[7:8, :] * earlier + vectors_ref[8:9, :] * low + vectors_ref[9:10, :] * later
    ).astype(jnp.bfloat16)
    conv_t = conv.T
    grad_conv = jnp.zeros((2 * rows, D), jnp.float32)
    for number in range(D // CHUNK):
        span = slice(number * CHUNK, (number + 1) * CHUNK)
        weight = w_ref[:, :, :, span].reshape(D, CHUNK)
        gain = gain_ref[0, :, span]
        upstream = upstream_ref[0, :, span].astype(jnp.float32)
        pointed = (
            jnp.dot(conv, weight, preferred_element_type=jnp.float32) + vectors_ref[6:7, span]
        )
        out_ref[0, :, span] = (summed[:, span] + gain * pointed).astype(jnp.bfloat16)
        gain_rows_ref[0, :, span] = jnp.sum(upstream * pointed, axis=0, keepdims=True)
        grad_point = (gain * upstream).astype(jnp.bfloat16)
        sums_ref[0:1, span] = sums_ref[0:1, span] + jnp.sum(
            grad_point.astype(jnp.float32), axis=0, keepdims=True
        )
        grad_conv = grad_conv + times_transposed(grad_point, weight)
        grad_w[:, span] = grad_w[:, span] + jnp.dot(
            conv_t, grad_point, preferred_element_type=jnp.float32
        )
    grad_low = grad_conv.astype(jnp.bfloat16)
    grad_conv_ref[0] = grad_low
    grad_wide = grad_low.astype(jnp.float32)
    for number, rows_here in enumerate((earlier, low, later)):
        sums_ref[number + 1 : number + 2, :] = sums_ref[number + 1 : number + 2, :] + jnp.sum(
            grad_wide * rows_here, axis=0, keepdims=True
        )

    @pl.when(step == pl.num_programs(0) - 1)
    def _():
        grad_w_ref[...] = grad_w[...].astype(jnp.bfloat16).reshape(POINT[0])


def point_layer(after, skip, upstream, first, last, gains, vectors, weights):
    windows, rows, _ = after.shape
    shapes = [
        jax.ShapeDtypeStruct((windows, 2 * rows, D), jnp.bfloat16),
        jax.ShapeDtypeStruct((windows, 2 * rows, D), jnp.bfloat16),
        jax.ShapeDtypeStruct((UNITS, 2, UNIT, D), jnp.bfloat16),
        jax.ShapeDtypeStruct((windows, 1, D), jnp.float32),
        jax.ShapeDtypeStruct((8, D), jnp.float32),
    ]
    moving = (after, skip, upstream, first, last, gains)
    return pl.pallas_call(
        functools.partial(point_kernel, rows=rows),
        grid=(windows,),
        in_specs=[step_block(array, 1) for array in moving]
        + [whole_block(vectors), unit_rows(*POINT_ROWS)],
        out_specs=[
            step_block(shapes[0], 1),
            step_block(shapes[1], 1),
            weight_block(POINT),
            step_block(shapes[3], 1),
            whole_block(shapes[4]),
        ],
        out_shape=shapes,
        scratch_shapes=[
            pltpu.VMEM((D // LANES, 2 * rows, LANES), jnp.float32),
            pltpu.VMEM((2 * rows, D), jnp.float32),
            pltpu.VMEM((D, D), jnp.float32),
        ],
        compiler_params=pltpu.CompilerParams(vmem_limit_bytes=60 * 2**20),
        cost_estimate=pl.CostEstimate(
            flops=(12 * windows * rows * D * D) // 16,
            bytes_accessed=(4 * D * D + 20 * windows * rows * D) // 16,
            transcendentals=0,
        ),
    )(*moving, vectors, weights[1])


def dense_back_kernel(
    core_ref,
    upstream_ref,
    grad_conv_ref,
    first_ref,
    last_ref,
    slope_ref,
    hidden_ref,
    vectors_ref,
    w_out_ref,
    w_left_ref,
    w_right_ref,
    w_down_ref,
    skip_grad_ref,
    grad_mid_ref,
    grad_down_ref,
    grad_before_ref,
    grad_att_ref,
    own_a,
    own_b,
    other_a,
    other_b,
    sums_ref,
    up_sums_ref,
    doubled,
    *,
    count,
    rows,
):
    core = core_ref[0]
    total = count * rows
    width = own_a.shape[2]

    @pl.when(pl.program_id(0) == 0)
    def _():
        sums_ref[...] = jnp.zeros_like(sums_ref)
        up_sums_ref[...] = jnp.zeros_like(up_sums_ref)

    grads = []
    for window in range(count):
        here = grad_conv_ref[window].astype(jnp.float32)
        earlier, later = shifted(
            here, first_ref[window].astype(jnp.float32), last_ref[window].astype(jnp.float32)
        )
        skip_grad = (
            upstream_ref[window].astype(jnp.float32)
            + vectors_ref[7:8, :] * later
            + vectors_ref[8:9, :] * here
            + vectors_ref[9:10, :] * earlier
        )
        skip_grad_ref[window] = skip_grad
        for number in range(D // LANES):
            doubled[number] = skip_grad[:, number * LANES : (number + 1) * LANES]
        grads.append(
            jnp.concatenate(
                [
                    doubled[number, pl.ds(0, rows, stride=2), :]
                    + doubled[number, pl.ds(1, rows, stride=2), :]
                    for number in range(D // LANES)
                ],
                axis=1,
            )
        )
    grad = jnp.concatenate(grads, axis=0)
    low = grad.astype(jnp.bfloat16)
    grad_down_ref[...] = low.reshape(count, rows, D)
    sums_ref[0:1, :] = sums_ref[0:1, :] + jnp.sum(
        low.astype(jnp.float32), axis=0, keepdims=True
    )
    grad_norm = jnp.zeros((total, D), jnp.float32)
    for number in range(FF // WIDE):
        span = slice(number * WIDE, (number + 1) * WIDE)
        half = (w_left_ref, w_right_ref)[number * WIDE // D]
        start = number * WIDE % D
        units = slice(number * WIDE // 32, (number + 1) * WIDE // 32)
        slope = slope_ref[:, :, span].reshape(total, WIDE).astype(jnp.float32)
        grad_active = times_transposed(low, w_down_ref[units].reshape(WIDE, D))
        grad_before = (grad_active * slope).astype(jnp.bfloat16)
        grad_before_ref[:, :, span] = grad_before.reshape(count, rows, WIDE)
        up_sums_ref[0:1, span] = up_sums_ref[0:1, span] + jnp.sum(
            grad_before.astype(jnp.float32), axis=0, keepdims=True
        )
        grad_norm = grad_norm + times_transposed(
            grad_before, half[:, 0, :, start : start + WIDE].reshape(D, WIDE)
        )
    hidden = hidden_ref[...].reshape(total, D)
    gain = vectors_ref[2:3, :]
    _, stats, inverse = layer_stats(hidden, gain, vectors_ref[3:4, :])
    sums_ref[1:2, :] = sums_ref[1:2, :] + jnp.sum(grad_norm * stats, axis=0, keepdims=True)
    sums_ref[2:3, :] = sums_ref[2:3, :] + jnp.sum(grad_norm, axis=0, keepdims=True)
    mid = grad + norm_back(grad_norm, stats, inverse, gain)
    grad_mid_ref[...] = mid.reshape(count, rows, D)
    mid_low = mid.astype(jnp.bfloat16)
    grad_att_ref[...] = mid_low.reshape(count, rows, D)
    sums_ref[3:4, :] = sums_ref[3:4, :] + jnp.sum(
        mid_low.astype(jnp.float32), axis=0, keepdims=True
    )
    for number, piece in enumerate((own_a, own_b, other_a, other_b)):
        group = core if number < 2 else 1 - core
        unit = group * 24 + (number % 2) * 12
        piece[...] = (
            times_transposed(mid_low, w_out_ref[pl.ds(unit, 12)].reshape(width, D))
            .astype(jnp.bfloat16)
            .reshape(count, rows, width)
        )


def dense_backward(
    core, upstream, grad_conv, first, last, slope, hidden, vectors, weights
):
    windows, rows, _ = hidden.shape
    count = max(1, 256 // rows)
    width = H * VD // 4
    shapes = (
        [
            jax.ShapeDtypeStruct((windows, 2 * rows, D), jnp.float32),
            jax.ShapeDtypeStruct((windows, rows, D), jnp.float32),
            jax.ShapeDtypeStruct((windows, rows, D), jnp.bfloat16),
            jax.ShapeDtypeStruct((windows, rows, FF), jnp.bfloat16),
            jax.ShapeDtypeStruct((windows, rows, D), jnp.bfloat16),
        ]
        + [jax.ShapeDtypeStruct((windows, rows, width), jnp.bfloat16)] * 4
        + [jax.ShapeDtypeStruct((8, D), jnp.float32), jax.ShapeDtypeStruct((8, FF), jnp.float32)]
    )
    moving = (upstream, grad_conv, first, last, slope, hidden)
    lower, upper, w_up = weights
    return pl.pallas_call(
        functools.partial(dense_back_kernel, count=count, rows=rows),
        grid=(windows // count,),
        in_specs=[pl.BlockSpec(memory_space=pltpu.SMEM)]
        + [step_block(array, count) for array in moving]
        + [whole_block(vectors)]
        + [unit_rows(*OUT_ROWS), up_half(0), up_half(1), unit_rows(*DOWN_ROWS)],
        out_specs=[step_block(shape, count) for shape in shapes[:9]]
        + [whole_block(shape) for shape in shapes[9:]],
        out_shape=shapes,
        scratch_shapes=[pltpu.VMEM((D // LANES, 2 * rows, LANES), jnp.float32)],
        compiler_params=pltpu.CompilerParams(vmem_limit_bytes=62 * 2**20),
        cost_estimate=pl.CostEstimate(
            flops=(2 * windows * rows * D * (D + 2 * FF)) // 16,
            bytes_accessed=(2 * D * (D + 2 * FF) + 40 * windows * rows * D) // 16,
            transcendentals=0,
        ),
    )(core, *moving, vectors, lower, w_up, w_up, upper)


def weight_grad_kernel(left_ref, right_ref, *refs):
    out_ref = refs[-1]
    total = left_ref.shape[0] * left_ref.shape[1]
    left = left_ref[...].reshape(total, left_ref.shape[2])
    right = right_ref[...].reshape(total, D)
    out_ref[...] = (
        jnp.dot(left.T, right, preferred_element_type=jnp.float32)
        .astype(jnp.bfloat16)
        .reshape(out_ref.shape)
    )


def weight_grad(left, right, held, place):
    windows, rows, depth = left.shape
    halves = right.shape[2] // D
    step = D // 4
    count = step // UNIT // (2 // halves)
    first = place[0][0] * place[1][0] // count
    return pl.pallas_call(
        weight_grad_kernel,
        grid=(halves, depth // step),
        in_specs=[
            pl.BlockSpec((windows, rows, step), lambda h, m: (0, 0, m)),
            pl.BlockSpec((windows, rows, D), lambda h, m: (0, 0, h)),
            pl.BlockSpec(memory_space=pl.ANY),
        ],
        out_specs=pl.BlockSpec(
            (count, 2 // halves, UNIT, D), lambda h, m: (first + m, h, 0, 0)
        ),
        out_shape=jax.ShapeDtypeStruct(held.shape, held.dtype),
        input_output_aliases={2: 0},
        compiler_params=pltpu.CompilerParams(vmem_limit_bytes=48 * 2**20),
        cost_estimate=pl.CostEstimate(
            flops=(2 * windows * rows * depth * right.shape[2]) // 16,
            bytes_accessed=(2 * (windows * rows * (depth + right.shape[2]) + depth * right.shape[2])) // 16,
            transcendentals=0,
        ),
    )(left, right, held)


def ordered(own, other, is_first, axis):
    return jnp.concatenate(
        [jnp.where(is_first, own, other), jnp.where(is_first, other, own)], axis=axis
    )


class Places:
    def __init__(self, windows, local_rows):
        self.dp = lax.axis_size("dp")
        self.seq = lax.axis_size("seq")
        self.windows = windows
        self.rows = local_rows
        self.length = local_rows * self.seq
        self.group = self.seq // (2 * windows)
        self.heads = H // (2 * self.group)
        self.core = lax.axis_index("dp") % 2
        self.is_first = self.core == 0
        self.place = lax.axis_index("seq") % self.group
        self.part = self.rows // (2 * self.group)
        self.head_start = (self.core * self.group + self.place) * self.heads

    def swap(self, array):
        return lax.ppermute(array, "dp", [(i, i ^ 1) for i in range(self.dp)])

    def rows_to_windows(self, own):
        kept, sent = own
        return ordered(kept, self.swap(sent), self.is_first, 0)

    def halves(self, array, axis):
        size = array.shape[axis] // 2
        kept = lax.dynamic_slice_in_dim(array, self.core * size, size, axis)
        sent = lax.dynamic_slice_in_dim(array, (1 - self.core) * size, size, axis)
        return (kept, sent)

    def exchange(self, array):
        return lax.all_to_all(array, "seq", split_axis=0, concat_axis=0, tiled=True)

    def inputs_to_windows(self, inputs):
        both = self.rows_to_windows(self.halves(inputs, 1))
        return both.reshape(self.seq, self.part, inputs.shape[2])

    def gather_rows(self, array):
        features = array.shape[2]
        array = array[:, None]
        if self.group > 1:
            hops = [
                (i, i - i % self.group + (i + 1) % self.group) for i in range(self.seq)
            ]
            pieces = [array]
            for _ in range(self.group - 1):
                pieces.append(lax.ppermute(pieces[-1], "seq", hops))
            pieces = jnp.concatenate(pieces, axis=1)
            order = (self.place - jnp.arange(self.group)) % self.group
            array = jnp.take(pieces, order, axis=1)
        array = ordered(
            array[:, None], self.swap(array)[:, None], self.is_first, 1
        )
        return array.reshape(self.length, features)

    def sum_rows(self, partial):
        features = partial.shape[1]
        partial = partial.reshape(self.seq, 2, self.group * self.part, features)
        kept, sent = self.halves(partial, 1)
        total = kept[:, 0].astype(jnp.float32) + self.swap(
            sent[:, 0].astype(jnp.bfloat16)
        ).astype(jnp.float32)
        if self.group > 1:
            total = lax.psum_scatter(
                total.reshape(self.seq, self.group, self.part, features),
                "seq",
                scatter_dimension=1,
                axis_index_groups=[
                    list(range(i, i + self.group)) for i in range(0, self.seq, self.group)
                ],
                tiled=True,
            )
            total = total[:, 0]
        return total.astype(jnp.bfloat16)

    def sums_to_rows(self, array):
        features = array.shape[2]
        back = array.reshape(2 * self.windows, self.group * self.part, features)
        kept, sent = self.halves(back, 0)
        return ordered(kept, self.swap(sent), self.is_first, 1)

    def heads_to_rows(self, chunk):
        count = chunk.shape[1]
        back = self.exchange(chunk.reshape(self.seq, self.rows, count))
        kept, sent = self.halves(
            back.reshape(2 * self.windows, self.group, self.rows, count), 0
        )
        return (kept, self.swap(sent))

    def rows_to_heads(self, kept, sent):
        count = kept.shape[3]
        both = self.rows_to_windows((kept, sent))
        back = self.exchange(both.reshape(self.seq, self.rows, count))
        return back.reshape(self.length, count)


def normed_rows(moved, special, at):
    vectors = special[F * H + FF :].reshape(12, D)
    low_part, _, _ = layer_stats(moved.astype(jnp.float32), vectors[0], vectors[1])
    return at.gather_rows(low_part.astype(jnp.bfloat16))


def bias_tables(special, at):
    length, own = (at.length, at.heads)
    pos_low = special[: F * H].reshape(F, H)
    pos_basis = position_basis(length)
    own_pos = lax.dynamic_slice_in_dim(pos_low, at.head_start, own, 1)
    tables = jnp.dot(own_pos.T, pos_basis.T, precision=highest)
    tables = jnp.roll(jnp.pad(tables, ((0, 0), (0, 1))), 1 - BLOCK, axis=1)
    tables = jnp.broadcast_to(tables[:, None, :], (own, 8, 2 * length))
    return (pos_basis, tables)


def gather_weights(params, sent, at):
    devices = lax.axis_size(("dp", "seq"))
    index = lax.axis_index(("dp", "seq"))
    dp, seq = lax.axis_size("dp"), lax.axis_size("seq")
    shard = params.shape[0]
    own_rows = ROWS // devices
    extra = shard - own_rows * D
    rest = extra * devices
    tail = params[shard - TAIL :].astype(jnp.bfloat16)
    before = lax.ppermute(tail, ("dp", "seq"), [(i, i + 1) for i in range(devices - 1)])
    joined = jnp.concatenate([before.astype(jnp.float32), params])
    piece = lax.dynamic_slice_in_dim(joined, TAIL - extra * index, own_rows * D)
    piece = piece.astype(jnp.bfloat16).reshape(own_rows, D)
    special = jnp.where(index == devices - 1, tail, jnp.zeros_like(tail))
    for axis, bit in axis_bits("dp"):
        special = special + partner(special, axis, bit)
    special = jnp.broadcast_to(special.reshape(1, TAIL // D, D), (seq, TAIL // D, D))
    special = lax.all_to_all(special, "seq", split_axis=0, concat_axis=0, tiled=True)[seq - 1]
    special, sent = lax.optimization_barrier((special, sent))
    ready = lax.all_to_all(sent, "seq", split_axis=0, concat_axis=0, tiled=True)
    special = special.astype(jnp.float32).reshape(-1)[TAIL - rest :]
    pos_basis, tables = bias_tables(special, at)
    ready = normed_rows(ready, special, at)
    if own_rows % UNIT == 0:
        here = piece.reshape(own_rows // UNIT, UNIT, D)
        other = jnp.swapaxes(piece.reshape(own_rows // UNIT, 8, 2, D), 1, 2).reshape(here.shape)
        row = own_rows * index + UNIT * jnp.arange(own_rows // UNIT)
        inside = (row >= UP_ROWS[0]) & (row < UP_ROWS[0] + UP_ROWS[1])
        piece = jnp.where(inside[:, None, None], other, here).reshape(piece.shape)
    half = own_rows // 2
    if dp == 2 and half % 8 == 0:
        second = lax.axis_index("dp") == 1
        given = jnp.where(second, piece[:half], piece[half:])
        taken = partner(given, "dp", 0)
        low = jnp.where(second, taken, piece[:half])
        high = jnp.where(second, piece[half:], taken)
        lower = lax.all_gather(low, ("seq", "dp"), axis=0, tiled=True)
        high, lower, ready, tables = lax.optimization_barrier((high, lower, ready, tables))
        upper = lax.all_gather(high, ("seq", "dp"), axis=0, tiled=True)
    else:
        everything = lax.all_gather(piece, ("dp", "seq"), axis=0, tiled=True)
        lower, upper = (everything[: ROWS // 2], everything[ROWS // 2 :])
    if own_rows % UNIT == 0:
        w_up = up_units(lower.reshape(-1, UNIT, D), upper.reshape(-1, UNIT, D))
    else:
        w_up = jnp.concatenate([lower[UP_ROWS[0] :], upper[: UP_ROWS[0] + UP_ROWS[1] - ROWS // 2]])
        w_up = jnp.swapaxes(w_up.reshape(96, UNIT, 2, D), 1, 2)
    views = [array.reshape(-1, 2, UNIT, D) for array in (lower, upper)]
    return (lower, (*views, w_up), special, ready, pos_basis, tables)


def axis_bits(axis):
    return [(axis, bit) for bit in range(lax.axis_size(axis).bit_length() - 2, -1, -1)]


def partner(array, axis, bit):
    pairs = [(i, i ^ (1 << bit)) for i in range(lax.axis_size(axis))]
    return lax.ppermute(array, axis, pairs)


def turned(number):
    along = axis_bits("seq")[::-1]
    return (along, along[1:2] + along[:1] + along[2:], along[2:] + along[:2])[number % 3]


def halves_apart(rows, first, outer, inner):
    units = rows.shape[0] // (2 * UNIT)
    here = rows.reshape(units, 2 * UNIT, D)
    other = jnp.swapaxes(rows.reshape(units, outer, inner, D), 1, 2).reshape(here.shape)
    inside = first + 2 * UNIT * jnp.arange(units) < 2 * D
    return jnp.where(inside[:, None, None], other, here).reshape(rows.shape)


class Sums:
    def __init__(self, rows):
        self.bits = axis_bits("dp") + axis_bits("seq")
        self.states = [rows.reshape((2,) * len(self.bits) + (-1, D))]
        self.left = [list(self.bits)]
        self.orders = [axis_bits("dp")[::-1]]
        self.steps = len(self.bits)

    def send(self):
        self.steps -= 1
        if not self.orders[0]:
            band = D // 3
            self.states = [self.states[0][..., k * band : (k + 1) * band] for k in range(3)]
            self.left = [list(self.left[0]) for _ in range(3)]
            self.orders = [turned(k) for k in range(3)]
        for k, state in enumerate(self.states):
            axis, bit = self.orders[k][0]
            self.orders[k] = self.orders[k][1:]
            dim = self.left[k].index((axis, bit))
            self.left[k].pop(dim)
            mine = (lax.axis_index(axis) >> bit) & 1
            sent = lax.dynamic_index_in_dim(state, 1 - mine, dim, False)
            kept = lax.dynamic_index_in_dim(state, mine, dim, False)
            self.states[k] = (kept, sent, axis, bit)

    def before(self, array):
        sent, array = lax.optimization_barrier(([state[1] for state in self.states], array))
        self.states = [
            (kept, there, axis, bit)
            for (kept, _, axis, bit), there in zip(self.states, sent, strict=True)
        ]
        return array

    def move(self):
        self.states = [
            (kept, partner(sent, axis, bit), axis, bit) for kept, sent, axis, bit in self.states
        ]

    def add(self):
        self.states = [
            (kept.astype(jnp.float32) + other.astype(jnp.float32)).astype(jnp.bfloat16)
            for kept, other, _, _ in self.states
        ]

    def finish(self, left=0):
        while self.steps > left:
            self.send()
            self.move()
            self.add()
        return jnp.concatenate(self.states, axis=1) if left == 0 else None


PARTS = ((4096, 6144), (2560, 1536), (10240, 1536))
QKV_PARTS = ((0, 2560),)


def moves(parts, more):
    devices = lax.axis_size(("dp", "seq"))
    own_rows = ROWS // devices
    count = sum(rows for _, rows in parts) // devices
    found, start = ([], 0)
    for first, rows in parts:
        for t in range(devices):
            low, high = (max(count * t, start), min(count * (t + 1), start + rows))
            if low >= high:
                continue
            row = first + low - start
            for i in range(devices):
                if row < own_rows * (i + 1) + more and row + high - low > own_rows * i:
                    found.append((i, t, high - low, row - own_rows * i, low - count * t))
        start += rows
    rounds = []
    for move in found:
        for held in rounds:
            if all(move[0] != other[0] and move[1] != other[1] for other in held):
                held.append(move)
                break
        else:
            rounds.append([move])
    return (rounds, count)


def per_device(values):
    index = lax.axis_index(("dp", "seq"))
    result = jnp.zeros((), jnp.int32)
    for place, value in values:
        if value != 0:
            result = jnp.where(index == place, value, result)
    return result


def to_owners(buffer, share, parts):
    rounds, most = moves(parts, TAIL // D)
    starts = [value for held in rounds for move in held for value in move[2:]]
    size = math.gcd(UNIT, MARGIN, most, buffer.shape[0], *starts)
    blocks = most // size
    share = jnp.pad(share.reshape(blocks, size, D), ((0, blocks), (0, 0), (0, 0)))
    buffer = buffer.reshape(-1, size, D)
    arrived = []
    for held in rounds:
        start = per_device([(t, offset // size) for _, t, _, _, offset in held])
        arrived.append(
            lax.ppermute(
                lax.dynamic_slice_in_dim(share, start, blocks, 0),
                ("dp", "seq"),
                [(t, i) for i, t, _, _, _ in held],
            )
        )
    for held, moved in zip(rounds, arrived, strict=True):
        place = per_device([(i, (MARGIN + low) // size) for i, _, _, low, _ in held])
        count = per_device([(i, rows // size) for i, _, rows, _, _ in held])
        inside = jnp.arange(blocks) < count
        moved = jnp.where(inside[:, None, None], moved, jnp.zeros_like(moved))
        there = lax.dynamic_slice_in_dim(buffer, place, blocks, 0)
        buffer = lax.dynamic_update_slice_in_dim(buffer, there + moved, place, 0)
    return buffer.reshape(-1, D)


def own_entries(buffer, special):
    devices = lax.axis_size(("dp", "seq"))
    index = lax.axis_index(("dp", "seq"))
    own_rows = ROWS // devices
    rest = special.shape[0]
    extra = rest // devices
    held = buffer[MARGIN : MARGIN + own_rows + TAIL // D].astype(jnp.float32)
    after = held[own_rows:].reshape(-1)
    after = jnp.where(index == devices - 1, jnp.pad(special, (0, TAIL - rest)), after)
    joined = jnp.concatenate([held[:own_rows].reshape(-1), after])
    return lax.dynamic_slice_in_dim(joined, extra * index, own_rows * D + extra)


def body(block_input, skip_input, species, cotangent, params, first_moment, second_moment):
    windows, local_rows, _ = block_input.shape
    at = Places(windows, local_rows)
    length = at.length
    own = at.heads
    scale = 1.0 / math.sqrt(KD)
    f32, bf16 = jnp.float32, jnp.bfloat16

    early, weights, special, low_all, pos_basis, tables = gather_weights(
        params, at.inputs_to_windows(block_input), at
    )
    up_bias = special[F * H : F * H + FF]
    vectors = special[F * H + FF :].reshape(12, D)

    w_own = own_weights(early, jnp.asarray(at.head_start, jnp.int32).reshape(1), own)

    projected = jnp.einsum("rd,dk->kr", low_all, w_own, preferred_element_type=f32).astype(bf16)
    queries, keys, values = (
        projected[: own * KD],
        projected[own * KD : 2 * own * KD],
        projected[2 * own * KD :],
    )

    operands, saved, pieces = ([], [], ([], []))
    for pair in range(own // PAIR):
        narrow = slice(pair * PAIR * KD, (pair + 1) * PAIR * KD)
        wide = slice(pair * PAIR * VD, (pair + 1) * PAIR * VD)
        given = (
            tables[pair * PAIR : (pair + 1) * PAIR],
            queries[narrow],
            keys[narrow],
            values[wide],
        )
        result, log_total = attention_forward(*given)
        operands.append(given)
        saved.append((result, log_total))
        for held, part in zip(pieces, at.heads_to_rows(result), strict=True):
            held.append(part)
    pairs = own // PAIR
    pieces = [
        held[pair][:, place] for held in pieces for place in range(at.group) for pair in range(pairs)
    ]

    core = jnp.asarray(at.core, jnp.int32).reshape(1)
    heads, hidden_one, low_two, activated, slope, hidden_two = dense_forward(
        core, block_input, pieces, vectors, up_bias[None], weights
    )
    ends = [
        (hidden_two[:, row : row + 1] + skip_input[:, up : up + 1].astype(f32)).astype(bf16)
        for row, up in ((0, 0), (local_rows - 1, 2 * local_rows - 1))
    ]
    first, last = edge_rows(ends)
    is_mouse = (species == 1).astype(f32)[:, None]
    species_gain = (1.0 - is_mouse) * vectors[10] + is_mouse * vectors[11]
    block_out, grad_conv, dense_grads, gain_rows, point_sums = point_layer(
        hidden_two,
        skip_input,
        cotangent,
        first,
        last,
        species_gain[:, None, :],
        vectors,
        weights,
    )
    gain_rows = gain_rows[:, 0]
    grad_human = jnp.sum((1.0 - is_mouse) * gain_rows, axis=0)
    grad_mouse = jnp.sum(is_mouse * gain_rows, axis=0)
    first, last = edge_rows([grad_conv[:, :1], grad_conv[:, 2 * local_rows - 1 :]])
    (
        skip_grad,
        grad_mid,
        grad_down_low,
        grad_before,
        grad_attn_low,
        *grad_pieces,
        dense_sums,
        up_sums,
    ) = dense_backward(
        core,
        cotangent,
        grad_conv,
        first,
        last,
        slope,
        hidden_one,
        vectors,
        weights,
    )
    grad_pieces = [
        jnp.stack(
            [
                grad_pieces[2 * group + place * pairs + pair]
                for place in range(at.group)
            ],
            axis=1,
        )
        for group in range(2)
        for pair in range(pairs)
    ]

    middle = jnp.concatenate(
        [
            up_sums[0],
            dense_sums[1],
            dense_sums[2],
            dense_sums[3],
            dense_sums[0],
            point_sums[:4].reshape(-1),
            grad_human,
            grad_mouse,
        ]
    )
    devices = lax.axis_size(("dp", "seq"))
    chunks = [at.rows_to_heads(grad_pieces[pair], grad_pieces[pairs + pair]) for pair in range(pairs)]
    dense_grads = weight_grad(activated, grad_down_low, dense_grads, DOWN)
    dense_grads = weight_grad(low_two, grad_before, dense_grads, LEFT)
    dense_grads = weight_grad(heads, grad_attn_low, dense_grads, OUT).reshape(-1, D)
    even = dense_grads.shape[0] // devices % (2 * UNIT) == 0
    if not even:
        dense_grads = halves_apart(dense_grads, 0, 2, UNIT)
    dense_grads, chunks[0] = lax.optimization_barrier((dense_grads, chunks[0]))
    dense = lax.psum_scatter(dense_grads, ("dp", "seq"), scatter_dimension=0, tiled=True)

    dq, dk, dv, dt = ([], [], [], [])
    for pair in range(pairs):
        result, log_total = saved[pair]
        grads = attention_backward(*operands[pair], result, chunks[pair], log_total)
        if pair + 1 < pairs:
            grads, chunks[pair + 1] = lax.optimization_barrier((grads, chunks[pair + 1]))
        for piece, held in zip(grads, (dq, dk, dv, dt), strict=True):
            held.append(piece)
    grad_own = jnp.concatenate(dq + dk + dv, axis=1)
    partial = jnp.einsum("rk,dk->rd", grad_own, w_own, preferred_element_type=f32).astype(bf16)
    partial, grad_own = lax.optimization_barrier((partial, grad_own))
    back = at.exchange(at.sum_rows(partial))
    grad_w_own = jnp.einsum("rd,rk->dk", low_all, grad_own, preferred_element_type=f32)
    grad_w_query = grad_w_own[:, : own * KD] * scale
    grad_w_key = grad_w_own[:, own * KD : 2 * own * KD]
    grad_w_value = grad_w_own[:, 2 * own * KD :]

    def all_columns(matrix, width):
        whole = jnp.zeros((D, H * width), bf16)
        return lax.dynamic_update_slice_in_dim(
            whole, matrix.astype(bf16), at.head_start * width, 1
        ).reshape(-1, D)

    first_rows = jnp.concatenate(
        [
            all_columns(grad_w_query, KD),
            all_columns(grad_w_key, KD),
            all_columns(grad_w_value, VD),
        ],
        axis=0,
    )
    first_sums = Sums(first_rows)
    first_sums.finish(2)
    first_sums.states, back = lax.optimization_barrier((first_sums.states, back))
    grad_norm_one = at.sums_to_rows(back).astype(f32)
    _, stats_one, inverse_one = layer_stats(block_input.astype(f32), vectors[0], vectors[1])
    input_grad = grad_mid + norm_back(grad_norm_one, stats_one, inverse_one, vectors[0])
    grad_gain_one = jnp.sum(grad_norm_one * stats_one, axis=(0, 1))
    grad_bias_one = jnp.sum(grad_norm_one, axis=(0, 1))
    grad_tables = jnp.roll(jnp.concatenate(dt, axis=0), BLOCK - 1, axis=1)[:, : 2 * length - 1]
    grad_pos = jnp.dot(pos_basis.T, grad_tables.T, precision=highest)
    grad_pos = lax.dynamic_update_slice_in_dim(
        jnp.zeros((F, H), f32), grad_pos, at.head_start, 1
    )
    late = jnp.concatenate([grad_pos.reshape(-1), grad_gain_one, grad_bias_one])
    summed = jnp.concatenate([late, middle])
    for axis, bit in axis_bits("dp") + axis_bits("seq"):
        summed = summed + partner(summed, axis, bit)
    late, middle = (summed[: late.shape[0]], summed[late.shape[0] :])
    special_grads = jnp.concatenate(
        [late[: F * H], middle[:FF], late[F * H :], middle[FF:]]
    )
    buffer = jnp.zeros((ROWS // devices + TAIL // D + 2 * MARGIN, D), bf16)
    buffer = to_owners(buffer, first_sums.finish(), QKV_PARTS)
    share, buffer, special_grads = lax.optimization_barrier((dense, buffer, special_grads))
    if even:
        share = halves_apart(share, lax.axis_index(("dp", "seq")) * share.shape[0], 2, UNIT)
    buffer = to_owners(buffer, share, PARTS)
    reduced = own_entries(buffer, special_grads)
    shard_len = params.shape[0]
    position = lax.axis_index(("dp", "seq")) * shard_len + jnp.arange(shard_len)
    param_new, first_new, second_new = adam_update(
        params, first_moment, second_moment, reduced, position
    )
    return (
        block_out,
        input_grad,
        skip_grad,
        param_new,
        first_new,
        second_new,
        param_new.astype(bf16),
    )


def solution(mesh):
    return jax.shard_map(
        body,
        mesh=mesh,
        in_specs=(
            P("dp", "seq", None),
            P("dp", "seq", None),
            P("dp"),
            P("dp", "seq", None),
            P(("dp", "seq")),
            P(("dp", "seq")),
            P(("dp", "seq")),
        ),
        out_specs=(
            P("dp", "seq", None),
            P("dp", "seq", None),
            P("dp", "seq", None),
            P(("dp", "seq")),
            P(("dp", "seq")),
            P(("dp", "seq")),
            P(("dp", "seq")),
        ),
        check_vma=False,
    )
```

```python
import functools
import math

import jax
import jax.numpy as jnp
from jax import lax
from jax.experimental import pallas as pl
from jax.experimental.pallas import tpu as pltpu
from jax.sharding import PartitionSpec as P

D = 1536
H = 8
KD = 64
VD = 192
FF = 3072
F = 192
STEP = 10
BLOCK = 256
PAIR = 2
CHUNK = 512
WIDE = 768
LANES = 128
ROWS = 11776
QKV_ROWS = 2560
TAIL = 24576
MARGIN = 288
UNIT = 16
UNITS = 288


eps_norm = 1e-05
beta_one = 0.5
beta_two = 0.5
adam_eps = 1e-08
decay_rate = 0.01
highest = lax.Precision.HIGHEST


def edge_rows(array):
    devices = lax.axis_size("seq")
    up = [(i, i + 1) for i in range(devices - 1)]
    first = lax.ppermute(array[1], "seq", up)
    last = lax.ppermute(array[0], "seq", [(j, i) for i, j in up])
    return (first, last)


def segment_ends():
    counts = [
        D * H * KD,
        D * H * KD,
        D * H * VD,
        H * VD * D,
        D * FF,
        FF * D,
        D * D,
        F * H,
        FF,
        12 * D,
    ]
    limits = []
    running = 0
    for amount in counts:
        running = running + amount
        limits.append(running)
    return limits


def rate_at(position):
    limits = segment_ends()
    step_rates = [
        2.0 / math.sqrt(D),
        2.0 / math.sqrt(D),
        2.0 / math.sqrt(D),
        8.0 / math.sqrt(H * VD),
        2.0 / math.sqrt(D),
        2.0 / math.sqrt(FF),
        2.0 / math.sqrt(D),
        3.0 / math.sqrt(F),
        0.4,
        0.4,
    ]
    result = jnp.full(position.shape, step_rates[-1], jnp.float32)
    for segment in range(len(limits) - 2, -1, -1):
        result = jnp.where(position < limits[segment], step_rates[segment], result)
    return result


def adam_update(param_old, first_old, second_old, gradient, position):
    step_rate = rate_at(position)
    first_new = beta_one * first_old + (1.0 - beta_one) * gradient
    second_new = beta_two * second_old + (1.0 - beta_two) * gradient * gradient
    first_hat = first_new / (1.0 - beta_one**STEP)
    second_hat = second_new / (1.0 - beta_two**STEP)
    param_new = param_old - step_rate * (
        first_hat / (jnp.sqrt(second_hat) + adam_eps) + decay_rate * param_old
    )
    return (param_new, first_new, second_new)


def position_basis(length):
    offsets = jnp.arange(2 * length - 1).astype(jnp.float32) - (length - 1)
    halves = F // 2
    ladder = jnp.arange(halves).astype(jnp.float32) / max(halves - 1, 1)
    lifetimes = jnp.exp(ladder * math.log(length))
    decays = jnp.exp(-jnp.abs(offsets)[:, None] * (math.log(2.0) / lifetimes)[None, :])
    return jnp.concatenate([decays, jnp.sign(offsets)[:, None] * decays], axis=1)


def layer_stats(inputs, norm_gain, norm_bias):
    centered = inputs - jnp.mean(inputs, axis=-1, keepdims=True)
    inverse = lax.rsqrt(jnp.mean(centered * centered, axis=-1, keepdims=True) + eps_norm)
    normed = centered * inverse
    return (normed * norm_gain + norm_bias, normed, inverse)


def norm_back(upstream, normed, inverse, norm_gain):
    scaled = upstream * norm_gain
    return inverse * (
        scaled
        - jnp.mean(scaled, axis=-1, keepdims=True)
        - normed * jnp.mean(scaled * normed, axis=-1, keepdims=True)
    )


def spread_rows(first_row, bands):
    start = pltpu.roll(first_row, 0, 1, stride=1, stride_axis=0)
    bands[0:8, :] = start
    height = 8
    while height < BLOCK:
        bands[height : 2 * height, :] = pltpu.roll(bands[0:height, :], height, 1)
        height *= 2


def collect_rows(bands, width):
    height = BLOCK // 2
    while height >= 8:
        bands[0:height, :] = bands[0:height, :] + pltpu.roll(
            bands[height : 2 * height, :], width - height, 1
        )
        height //= 2
    total = bands[0:1, :]
    for row in range(1, 8):
        total = total + pltpu.roll(bands[row : row + 1, :], width - row, 1)
    return total


def forward_kernel(
    table_ref, q_ref, k_ref, v_ref, out_ref, lse_ref, bands, key_rows, scores, *, blocks
):
    block = pl.program_id(0)

    @pl.when(block == 0)
    def _():
        for head in range(PAIR):
            spread_rows(table_ref[head], bands.at[head])
            key_rows[head] = k_ref[head * KD : (head + 1) * KD, :].T

    results = []
    for head in range(PAIR):
        queries = q_ref[head * KD : (head + 1) * KD, :]
        top = jnp.full((1, BLOCK), -jnp.inf, jnp.float32)
        for j in range(blocks):
            at = pl.multiple_of((block - j + blocks - 1) * BLOCK, BLOCK)
            span = slice(j * BLOCK, (j + 1) * BLOCK)
            part = (
                jnp.dot(key_rows[head, span, :], queries, preferred_element_type=jnp.float32)
                + bands[head, :, pl.ds(at, BLOCK)]
            )
            scores[span, :] = part
            top = jnp.maximum(top, jnp.max(part, axis=0, keepdims=True))
        total = jnp.zeros((1, BLOCK), jnp.float32)
        result = jnp.zeros((VD, BLOCK), jnp.float32)
        for j in range(blocks):
            span = slice(j * BLOCK, (j + 1) * BLOCK)
            grown = jnp.exp(scores[span, :] - top)
            total = total + jnp.sum(grown, axis=0, keepdims=True)
            result = result + jnp.dot(
                v_ref[head * VD : (head + 1) * VD, span],
                grown.astype(jnp.bfloat16),
                preferred_element_type=jnp.float32,
            )
        results.append(result * (1.0 / total))
        lse_ref[head : head + 1, :] = top + jnp.log(total)
    out_ref[...] = jnp.concatenate(results, axis=0).T.astype(jnp.bfloat16)


def attention_forward(tables, queries, keys, values):
    length = keys.shape[1]
    blocks = length // BLOCK
    return pl.pallas_call(
        functools.partial(forward_kernel, blocks=blocks),
        grid=(blocks,),
        in_specs=[
            pl.BlockSpec((PAIR, 8, 2 * length), lambda i: (0, 0, 0)),
            pl.BlockSpec((PAIR * KD, BLOCK), lambda i: (0, i)),
            pl.BlockSpec((PAIR * KD, length), lambda i: (0, 0)),
            pl.BlockSpec((PAIR * VD, length), lambda i: (0, 0)),
        ],
        out_specs=[
            pl.BlockSpec((BLOCK, PAIR * VD), lambda i: (i, 0)),
            pl.BlockSpec((PAIR, BLOCK), lambda i: (0, i)),
        ],
        out_shape=[
            jax.ShapeDtypeStruct((length, PAIR * VD), jnp.bfloat16),
            jax.ShapeDtypeStruct((PAIR, length), jnp.float32),
        ],
        scratch_shapes=[
            pltpu.VMEM((PAIR, BLOCK, 2 * length), jnp.float32),
            pltpu.VMEM((PAIR, length, KD), jnp.bfloat16),
            pltpu.VMEM((length, BLOCK), jnp.float32),
        ],
        compiler_params=pltpu.CompilerParams(vmem_limit_bytes=48 * 2**20),
        cost_estimate=pl.CostEstimate(
            flops=(4 * PAIR * length * length * 256) // 16,
            bytes_accessed=(8 * PAIR * length * (KD + VD)) // 16,
            transcendentals=PAIR * length * length // 16,
        ),
    )(tables, queries, keys, values)


def backward_kernel(
    table_ref,
    q_ref,
    k_ref,
    v_ref,
    out_ref,
    grad_ref,
    lse_ref,
    dq_ref,
    dk_ref,
    dv_ref,
    dt_ref,
    bands,
    grad_bands,
    key_rows,
    value_rows,
    dk_sum,
    dv_sum,
    *,
    blocks,
):
    block = pl.program_id(0)

    @pl.when(block == 0)
    def _():
        for head in range(PAIR):
            spread_rows(table_ref[head], bands.at[head])
            key_rows[head] = k_ref[head * KD : (head + 1) * KD, :].T
            value_rows[head] = v_ref[head * VD : (head + 1) * VD, :].T
        grad_bands[...] = jnp.zeros_like(grad_bands)
        dk_sum[...] = jnp.zeros_like(dk_sum)
        dv_sum[...] = jnp.zeros_like(dv_sum)

    grad_t = grad_ref[...].T
    out_t = out_ref[...].T
    products = grad_t.astype(jnp.float32) * out_t.astype(jnp.float32)
    results = []
    for head in range(PAIR):
        wide = slice(head * VD, (head + 1) * VD)
        delta = jnp.sum(products[wide, :], axis=0, keepdims=True)
        grad_here = grad_t[wide, :]
        grad_rows = grad_here.T
        queries = q_ref[head * KD : (head + 1) * KD, :]
        query_rows = queries.T
        lse = lse_ref[head : head + 1, :]
        dq = jnp.zeros((KD, BLOCK), jnp.float32)
        for j in range(blocks):
            span = slice(j * BLOCK, (j + 1) * BLOCK)
            at = pl.multiple_of((block - j + blocks - 1) * BLOCK, BLOCK)
            part = (
                jnp.dot(key_rows[head, span, :], queries, preferred_element_type=jnp.float32)
                + bands[head, :, pl.ds(at, BLOCK)]
            )
            soft = jnp.exp(part - lse)
            grad_soft = jnp.dot(
                value_rows[head, span, :], grad_here, preferred_element_type=jnp.float32
            )
            grad_scores = soft * (grad_soft - delta)
            grad_bands[head, :, pl.ds(at, BLOCK)] = (
                grad_bands[head, :, pl.ds(at, BLOCK)] + grad_scores
            )
            low = grad_scores.astype(jnp.bfloat16)
            dv_sum[head, span, :] = dv_sum[head, span, :] + jnp.dot(
                soft.astype(jnp.bfloat16), grad_rows, preferred_element_type=jnp.float32
            )
            dk_sum[head, span, :] = dk_sum[head, span, :] + jnp.dot(
                low, query_rows, preferred_element_type=jnp.float32
            )
            dq = dq + jnp.dot(
                k_ref[head * KD : (head + 1) * KD, span], low, preferred_element_type=jnp.float32
            )
        results.append(dq)
    dq_ref[...] = jnp.concatenate(results, axis=0).T.astype(jnp.bfloat16)

    @pl.when(block == blocks - 1)
    def _():
        dk_ref[...] = jnp.concatenate(
            [dk_sum[head] for head in range(PAIR)], axis=1
        ).astype(jnp.bfloat16)
        dv_ref[...] = jnp.concatenate(
            [dv_sum[head] for head in range(PAIR)], axis=1
        ).astype(jnp.bfloat16)
        for head in range(PAIR):
            dt_ref[head : head + 1, :] = collect_rows(
                grad_bands.at[head], grad_bands.shape[2]
            )


def attention_backward(tables, queries, keys, values, heads, grad_heads, lse):
    length = keys.shape[1]
    blocks = length // BLOCK
    return pl.pallas_call(
        functools.partial(backward_kernel, blocks=blocks),
        grid=(blocks,),
        in_specs=[
            pl.BlockSpec((PAIR, 8, 2 * length), lambda i: (0, 0, 0)),
            pl.BlockSpec((PAIR * KD, BLOCK), lambda i: (0, i)),
            pl.BlockSpec((PAIR * KD, length), lambda i: (0, 0)),
            pl.BlockSpec((PAIR * VD, length), lambda i: (0, 0)),
            pl.BlockSpec((BLOCK, PAIR * VD), lambda i: (i, 0)),
            pl.BlockSpec((BLOCK, PAIR * VD), lambda i: (i, 0)),
            pl.BlockSpec((PAIR, BLOCK), lambda i: (0, i)),
        ],
        out_specs=[
            pl.BlockSpec((BLOCK, PAIR * KD), lambda i: (i, 0)),
            pl.BlockSpec((length, PAIR * KD), lambda i: (0, 0)),
            pl.BlockSpec((length, PAIR * VD), lambda i: (0, 0)),
            pl.BlockSpec((PAIR, 2 * length), lambda i: (0, 0)),
        ],
        out_shape=[
            jax.ShapeDtypeStruct((length, PAIR * KD), jnp.bfloat16),
            jax.ShapeDtypeStruct((length, PAIR * KD), jnp.bfloat16),
            jax.ShapeDtypeStruct((length, PAIR * VD), jnp.bfloat16),
            jax.ShapeDtypeStruct((PAIR, 2 * length), jnp.float32),
        ],
        scratch_shapes=[
            pltpu.VMEM((PAIR, BLOCK, 2 * length), jnp.float32),
            pltpu.VMEM((PAIR, BLOCK, 2 * length), jnp.float32),
            pltpu.VMEM((PAIR, length, KD), jnp.bfloat16),
            pltpu.VMEM((PAIR, length, VD), jnp.bfloat16),
            pltpu.VMEM((PAIR, length, KD), jnp.float32),
            pltpu.VMEM((PAIR, length, VD), jnp.float32),
        ],
        compiler_params=pltpu.CompilerParams(vmem_limit_bytes=56 * 2**20),
        cost_estimate=pl.CostEstimate(
            flops=(10 * PAIR * length * length * 256) // 16,
            bytes_accessed=(16 * PAIR * length * (KD + VD)) // 16,
            transcendentals=PAIR * length * length // 16,
        ),
    )(tables, queries, keys, values, heads, grad_heads, lse)


def whole_block(array):
    zeros = (0,) * array.ndim
    return pl.BlockSpec(array.shape, lambda i: zeros, pipeline_mode=pl.Buffered(1))


LEFT, DOWN = ((96, 1, UNIT, D), (0, 0)), ((96, 2, UNIT, D), (1, 0))
OUT, POINT = ((48, 2, UNIT, D), (4, 0)), ((48, 2, UNIT, D), (5, 0))


def weight_block(weight):
    shape, place = weight
    return pl.BlockSpec(shape, lambda *i: place + (0, 0), pipeline_mode=pl.Buffered(1))


def up_half(half):
    return pl.BlockSpec(
        (96, 1, UNIT, D), lambda i: (0, half, 0, 0), pipeline_mode=pl.Buffered(1)
    )


def unit_rows(first, rows):
    first, units = (first // (2 * UNIT), rows // (2 * UNIT))
    return pl.BlockSpec(
        (pl.Element(units), pl.Element(2), pl.Element(UNIT), pl.Element(D)),
        lambda i: (first, 0, 0, 0),
        pipeline_mode=pl.Buffered(1),
    )


def up_units_kernel(lower_ref, upper_ref, out_ref, *, steps):
    units = out_ref.shape[0]

    def put(rows_ref):
        rows = rows_ref[...].astype(jnp.float32).reshape(units, 2, 2, 8, D)
        out_ref[...] = (
            jnp.swapaxes(rows, 1, 2).reshape(units, 2, UNIT, D).astype(jnp.bfloat16)
        )

    pl.when(pl.program_id(0) < steps)(lambda: put(lower_ref))
    pl.when(pl.program_id(0) >= steps)(lambda: put(upper_ref))


def up_units(lower, upper):
    units = 8
    start = UP_ROWS[0] // UNIT // (2 * units)
    steps = lower.shape[0] // (2 * units) - start
    return pl.pallas_call(
        functools.partial(up_units_kernel, steps=steps),
        grid=(96 // units,),
        in_specs=[
            pl.BlockSpec(
                (2 * units, UNIT, D), lambda i: (start + jnp.minimum(i, steps - 1), 0, 0)
            ),
            pl.BlockSpec((2 * units, UNIT, D), lambda i: (jnp.maximum(i - steps, 0), 0, 0)),
        ],
        out_specs=pl.BlockSpec((units, 2, UNIT, D), lambda i: (i, 0, 0, 0)),
        out_shape=jax.ShapeDtypeStruct((96, 2, UNIT, D), jnp.bfloat16),
        compiler_params=pltpu.CompilerParams(vmem_limit_bytes=32 * 2**20),
    )(lower, upper)


OUT_ROWS, UP_ROWS, DOWN_ROWS, POINT_ROWS = (2560, D), (4096, FF), (1280, FF), (4352, D)


def step_block(array, count):
    shape = (count,) + array.shape[1:]
    rest = (0,) * (array.ndim - 1)
    return pl.BlockSpec(shape, lambda i: (i,) + rest)


def times_transposed(left, right):
    return lax.dot_general(
        left, right, (((1,), (1,)), ((), ())), preferred_element_type=jnp.float32
    )


def dense_kernel(
    core_ref,
    inputs_ref,
    own_a,
    own_b,
    other_a,
    other_b,
    vectors_ref,
    up_bias_ref,
    w_out_ref,
    w_left_ref,
    w_right_ref,
    w_down_ref,
    heads_ref,
    hidden_ref,
    low_ref,
    active_ref,
    slope_ref,
    after_ref,
    *,
    count,
    rows,
):
    core = core_ref[0]
    total = count * rows
    width = own_a.shape[2]
    hidden = inputs_ref[...].reshape(total, D).astype(jnp.float32) + vectors_ref[4:5, :]
    for number, piece in enumerate((own_a, own_b, other_a, other_b)):
        group = core if number < 2 else 1 - core
        at = pl.multiple_of(group * (2 * width) + (number % 2) * width, 128)
        unit = group * 24 + (number % 2) * 12
        held = piece[...]
        heads_ref[:, :, pl.ds(at, width)] = held
        hidden = hidden + jnp.dot(
            held.reshape(total, width),
            w_out_ref[pl.ds(unit, 12)].reshape(width, D),
            preferred_element_type=jnp.float32,
        )
    hidden_ref[...] = hidden.reshape(count, rows, D)
    normed, _, _ = layer_stats(hidden, vectors_ref[2:3, :], vectors_ref[3:4, :])
    low = normed.astype(jnp.bfloat16)
    low_ref[...] = low.reshape(count, rows, D)
    after = hidden + vectors_ref[5:6, :]
    for number in range(FF // WIDE):
        span = slice(number * WIDE, (number + 1) * WIDE)
        half = (w_left_ref, w_right_ref)[number * WIDE // D]
        start = number * WIDE % D
        units = slice(number * WIDE // 32, (number + 1) * WIDE // 32)
        before = (
            jnp.dot(
                low,
                half[:, 0, :, start : start + WIDE].reshape(D, WIDE),
                preferred_element_type=jnp.float32,
            )
            + up_bias_ref[:, span]
        )
        phi = 0.5 * (1.0 + lax.erf(before * (1.0 / math.sqrt(2.0))))
        slope = phi + before * jnp.exp(-0.5 * before * before) * (1.0 / math.sqrt(2.0 * math.pi))
        active = (before * phi).astype(jnp.bfloat16)
        active_ref[:, :, span] = active.reshape(count, rows, WIDE)
        slope_ref[:, :, span] = slope.astype(jnp.bfloat16).reshape(count, rows, WIDE)
        after = after + jnp.dot(
            active, w_down_ref[units].reshape(WIDE, D), preferred_element_type=jnp.float32
        )
    after_ref[...] = after.reshape(count, rows, D)


def dense_forward(core, inputs, pieces, vectors, up_bias, weights):
    windows, rows, _ = inputs.shape
    count = max(1, 256 // rows)
    shapes = [
        jax.ShapeDtypeStruct((windows, rows, D), jnp.bfloat16),
        jax.ShapeDtypeStruct((windows, rows, D), jnp.float32),
        jax.ShapeDtypeStruct((windows, rows, D), jnp.bfloat16),
        jax.ShapeDtypeStruct((windows, rows, FF), jnp.bfloat16),
        jax.ShapeDtypeStruct((windows, rows, FF), jnp.bfloat16),
        jax.ShapeDtypeStruct((windows, rows, D), jnp.float32),
    ]
    lower, upper, w_up = weights
    return pl.pallas_call(
        functools.partial(dense_kernel, count=count, rows=rows),
        grid=(windows // count,),
        in_specs=[pl.BlockSpec(memory_space=pltpu.SMEM), step_block(inputs, count)]
        + [step_block(piece, count) for piece in pieces]
        + [whole_block(vectors), whole_block(up_bias)]
        + [unit_rows(*OUT_ROWS), up_half(0), up_half(1), unit_rows(*DOWN_ROWS)],
        out_specs=[step_block(shape, count) for shape in shapes],
        out_shape=shapes,
        compiler_params=pltpu.CompilerParams(vmem_limit_bytes=60 * 2**20),
        cost_estimate=pl.CostEstimate(
            flops=(2 * windows * rows * D * (D + 2 * FF)) // 16,
            bytes_accessed=(2 * D * (D + 2 * FF) + 26 * windows * rows * D) // 16,
            transcendentals=2 * windows * rows * FF // 16,
        ),
    )(core, inputs, *pieces, vectors, up_bias, lower, w_up, w_up, upper)


def shifted(rows, first, last):
    count = rows.shape[0]
    place = lax.broadcasted_iota(jnp.int32, rows.shape, 0)
    earlier = jnp.where(place == 0, first, pltpu.roll(rows, 1, 0))
    later = jnp.where(place == count - 1, last, pltpu.roll(rows, count - 1, 0))
    return (earlier, later)


def point_kernel(
    after_ref,
    skip_ref,
    upstream_ref,
    first_ref,
    last_ref,
    gain_ref,
    vectors_ref,
    w_ref,
    out_ref,
    grad_conv_ref,
    grad_w_ref,
    gain_rows_ref,
    sums_ref,
    doubled,
    summed,
    grad_w,
    *,
    rows,
):
    step = pl.program_id(0)

    @pl.when(step == 0)
    def _():
        grad_w[...] = jnp.zeros_like(grad_w)
        sums_ref[...] = jnp.zeros_like(sums_ref)

    for number in range(D // LANES):
        span = slice(number * LANES, (number + 1) * LANES)
        after = after_ref[0, :, span]
        doubled[number, pl.ds(0, rows, stride=2), :] = after
        doubled[number, pl.ds(1, rows, stride=2), :] = after
        summed[:, span] = doubled[number] + skip_ref[0, :, span].astype(jnp.float32)
    low = summed[...].astype(jnp.bfloat16).astype(jnp.float32)
    earlier, later = shifted(
        low, first_ref[0].astype(jnp.float32), last_ref[0].astype(jnp.float32)
    )
    conv = (
        vectors_ref[7:8, :] * earlier + vectors_ref[8:9, :] * low + vectors_ref[9:10, :] * later
    ).astype(jnp.bfloat16)
    conv_t = conv.T
    grad_conv = jnp.zeros((2 * rows, D), jnp.float32)
    for number in range(D // CHUNK):
        span = slice(number * CHUNK, (number + 1) * CHUNK)
        weight = w_ref[:, :, :, span].reshape(D, CHUNK)
        gain = gain_ref[0, :, span]
        upstream = upstream_ref[0, :, span].astype(jnp.float32)
        pointed = (
            jnp.dot(conv, weight, preferred_element_type=jnp.float32) + vectors_ref[6:7, span]
        )
        out_ref[0, :, span] = (summed[:, span] + gain * pointed).astype(jnp.bfloat16)
        gain_rows_ref[0, :, span] = jnp.sum(upstream * pointed, axis=0, keepdims=True)
        grad_point = (gain * upstream).astype(jnp.bfloat16)
        sums_ref[0:1, span] = sums_ref[0:1, span] + jnp.sum(
            grad_point.astype(jnp.float32), axis=0, keepdims=True
        )
        grad_conv = grad_conv + times_transposed(grad_point, weight)
        grad_w[:, span] = grad_w[:, span] + jnp.dot(
            conv_t, grad_point, preferred_element_type=jnp.float32
        )
    grad_low = grad_conv.astype(jnp.bfloat16)
    grad_conv_ref[0] = grad_low
    grad_wide = grad_low.astype(jnp.float32)
    for number, rows_here in enumerate((earlier, low, later)):
        sums_ref[number + 1 : number + 2, :] = sums_ref[number + 1 : number + 2, :] + jnp.sum(
            grad_wide * rows_here, axis=0, keepdims=True
        )

    @pl.when(step == pl.num_programs(0) - 1)
    def _():
        grad_w_ref[...] = grad_w[...].astype(jnp.bfloat16).reshape(POINT[0])


def point_layer(after, skip, upstream, first, last, gains, vectors, weights):
    windows, rows, _ = after.shape
    shapes = [
        jax.ShapeDtypeStruct((windows, 2 * rows, D), jnp.bfloat16),
        jax.ShapeDtypeStruct((windows, 2 * rows, D), jnp.bfloat16),
        jax.ShapeDtypeStruct((UNITS, 2, UNIT, D), jnp.bfloat16),
        jax.ShapeDtypeStruct((windows, 1, D), jnp.float32),
        jax.ShapeDtypeStruct((8, D), jnp.float32),
    ]
    moving = (after, skip, upstream, first, last, gains)
    return pl.pallas_call(
        functools.partial(point_kernel, rows=rows),
        grid=(windows,),
        in_specs=[step_block(array, 1) for array in moving]
        + [whole_block(vectors), unit_rows(*POINT_ROWS)],
        out_specs=[
            step_block(shapes[0], 1),
            step_block(shapes[1], 1),
            weight_block(POINT),
            step_block(shapes[3], 1),
            whole_block(shapes[4]),
        ],
        out_shape=shapes,
        scratch_shapes=[
            pltpu.VMEM((D // LANES, 2 * rows, LANES), jnp.float32),
            pltpu.VMEM((2 * rows, D), jnp.float32),
            pltpu.VMEM((D, D), jnp.float32),
        ],
        compiler_params=pltpu.CompilerParams(vmem_limit_bytes=60 * 2**20),
        cost_estimate=pl.CostEstimate(
            flops=(12 * windows * rows * D * D) // 16,
            bytes_accessed=(4 * D * D + 20 * windows * rows * D) // 16,
            transcendentals=0,
        ),
    )(*moving, vectors, weights[1])


def dense_back_kernel(
    core_ref,
    upstream_ref,
    grad_conv_ref,
    first_ref,
    last_ref,
    slope_ref,
    hidden_ref,
    vectors_ref,
    w_out_ref,
    w_left_ref,
    w_right_ref,
    w_down_ref,
    skip_grad_ref,
    grad_mid_ref,
    grad_down_ref,
    grad_before_ref,
    grad_att_ref,
    own_a,
    own_b,
    other_a,
    other_b,
    sums_ref,
    up_sums_ref,
    doubled,
    *,
    count,
    rows,
):
    core = core_ref[0]
    total = count * rows
    width = own_a.shape[2]

    @pl.when(pl.program_id(0) == 0)
    def _():
        sums_ref[...] = jnp.zeros_like(sums_ref)
        up_sums_ref[...] = jnp.zeros_like(up_sums_ref)

    grads = []
    for window in range(count):
        here = grad_conv_ref[window].astype(jnp.float32)
        earlier, later = shifted(
            here, first_ref[window].astype(jnp.float32), last_ref[window].astype(jnp.float32)
        )
        skip_grad = (
            upstream_ref[window].astype(jnp.float32)
            + vectors_ref[7:8, :] * later
            + vectors_ref[8:9, :] * here
            + vectors_ref[9:10, :] * earlier
        )
        skip_grad_ref[window] = skip_grad
        for number in range(D // LANES):
            doubled[number] = skip_grad[:, number * LANES : (number + 1) * LANES]
        grads.append(
            jnp.concatenate(
                [
                    doubled[number, pl.ds(0, rows, stride=2), :]
                    + doubled[number, pl.ds(1, rows, stride=2), :]
                    for number in range(D // LANES)
                ],
                axis=1,
            )
        )
    grad = jnp.concatenate(grads, axis=0)
    low = grad.astype(jnp.bfloat16)
    grad_down_ref[...] = low.reshape(count, rows, D)
    sums_ref[0:1, :] = sums_ref[0:1, :] + jnp.sum(
        low.astype(jnp.float32), axis=0, keepdims=True
    )
    grad_norm = jnp.zeros((total, D), jnp.float32)
    for number in range(FF // WIDE):
        span = slice(number * WIDE, (number + 1) * WIDE)
        half = (w_left_ref, w_right_ref)[number * WIDE // D]
        start = number * WIDE % D
        units = slice(number * WIDE // 32, (number + 1) * WIDE // 32)
        slope = slope_ref[:, :, span].reshape(total, WIDE).astype(jnp.float32)
        grad_active = times_transposed(low, w_down_ref[units].reshape(WIDE, D))
        grad_before = (grad_active * slope).astype(jnp.bfloat16)
        grad_before_ref[:, :, span] = grad_before.reshape(count, rows, WIDE)
        up_sums_ref[0:1, span] = up_sums_ref[0:1, span] + jnp.sum(
            grad_before.astype(jnp.float32), axis=0, keepdims=True
        )
        grad_norm = grad_norm + times_transposed(
            grad_before, half[:, 0, :, start : start + WIDE].reshape(D, WIDE)
        )
    hidden = hidden_ref[...].reshape(total, D)
    gain = vectors_ref[2:3, :]
    _, stats, inverse = layer_stats(hidden, gain, vectors_ref[3:4, :])
    sums_ref[1:2, :] = sums_ref[1:2, :] + jnp.sum(grad_norm * stats, axis=0, keepdims=True)
    sums_ref[2:3, :] = sums_ref[2:3, :] + jnp.sum(grad_norm, axis=0, keepdims=True)
    mid = grad + norm_back(grad_norm, stats, inverse, gain)
    grad_mid_ref[...] = mid.reshape(count, rows, D)
    mid_low = mid.astype(jnp.bfloat16)
    grad_att_ref[...] = mid_low.reshape(count, rows, D)
    sums_ref[3:4, :] = sums_ref[3:4, :] + jnp.sum(
        mid_low.astype(jnp.float32), axis=0, keepdims=True
    )
    for number, piece in enumerate((own_a, own_b, other_a, other_b)):
        group = core if number < 2 else 1 - core
        unit = group * 24 + (number % 2) * 12
        piece[...] = (
            times_transposed(mid_low, w_out_ref[pl.ds(unit, 12)].reshape(width, D))
            .astype(jnp.bfloat16)
            .reshape(count, rows, width)
        )


def dense_backward(
    core, upstream, grad_conv, first, last, slope, hidden, vectors, weights
):
    windows, rows, _ = hidden.shape
    count = max(1, 256 // rows)
    width = H * VD // 4
    shapes = (
        [
            jax.ShapeDtypeStruct((windows, 2 * rows, D), jnp.float32),
            jax.ShapeDtypeStruct((windows, rows, D), jnp.float32),
            jax.ShapeDtypeStruct((windows, rows, D), jnp.bfloat16),
            jax.ShapeDtypeStruct((windows, rows, FF), jnp.bfloat16),
            jax.ShapeDtypeStruct((windows, rows, D), jnp.bfloat16),
        ]
        + [jax.ShapeDtypeStruct((windows, rows, width), jnp.bfloat16)] * 4
        + [jax.ShapeDtypeStruct((8, D), jnp.float32), jax.ShapeDtypeStruct((8, FF), jnp.float32)]
    )
    moving = (upstream, grad_conv, first, last, slope, hidden)
    lower, upper, w_up = weights
    return pl.pallas_call(
        functools.partial(dense_back_kernel, count=count, rows=rows),
        grid=(windows // count,),
        in_specs=[pl.BlockSpec(memory_space=pltpu.SMEM)]
        + [step_block(array, count) for array in moving]
        + [whole_block(vectors)]
        + [unit_rows(*OUT_ROWS), up_half(0), up_half(1), unit_rows(*DOWN_ROWS)],
        out_specs=[step_block(shape, count) for shape in shapes[:9]]
        + [whole_block(shape) for shape in shapes[9:]],
        out_shape=shapes,
        scratch_shapes=[pltpu.VMEM((D // LANES, 2 * rows, LANES), jnp.float32)],
        compiler_params=pltpu.CompilerParams(vmem_limit_bytes=62 * 2**20),
        cost_estimate=pl.CostEstimate(
            flops=(2 * windows * rows * D * (D + 2 * FF)) // 16,
            bytes_accessed=(2 * D * (D + 2 * FF) + 40 * windows * rows * D) // 16,
            transcendentals=0,
        ),
    )(core, *moving, vectors, lower, w_up, w_up, upper)


def weight_grad_kernel(left_ref, right_ref, *refs):
    out_ref = refs[-1]
    total = left_ref.shape[0] * left_ref.shape[1]
    left = left_ref[...].reshape(total, left_ref.shape[2])
    right = right_ref[...].reshape(total, D)
    out_ref[...] = (
        jnp.dot(left.T, right, preferred_element_type=jnp.float32)
        .astype(jnp.bfloat16)
        .reshape(out_ref.shape)
    )


def weight_grad(left, right, held, place):
    windows, rows, depth = left.shape
    halves = right.shape[2] // D
    step = D // 4
    count = step // UNIT // (2 // halves)
    first = place[0][0] * place[1][0] // count
    return pl.pallas_call(
        weight_grad_kernel,
        grid=(halves, depth // step),
        in_specs=[
            pl.BlockSpec((windows, rows, step), lambda h, m: (0, 0, m)),
            pl.BlockSpec((windows, rows, D), lambda h, m: (0, 0, h)),
            pl.BlockSpec(memory_space=pl.ANY),
        ],
        out_specs=pl.BlockSpec(
            (count, 2 // halves, UNIT, D), lambda h, m: (first + m, h, 0, 0)
        ),
        out_shape=jax.ShapeDtypeStruct(held.shape, held.dtype),
        input_output_aliases={2: 0},
        compiler_params=pltpu.CompilerParams(vmem_limit_bytes=48 * 2**20),
        cost_estimate=pl.CostEstimate(
            flops=(2 * windows * rows * depth * right.shape[2]) // 16,
            bytes_accessed=(2 * (windows * rows * (depth + right.shape[2]) + depth * right.shape[2])) // 16,
            transcendentals=0,
        ),
    )(left, right, held)


def ordered(own, other, is_first, axis):
    return jnp.concatenate(
        [jnp.where(is_first, own, other), jnp.where(is_first, other, own)], axis=axis
    )


class Places:
    def __init__(self, windows, local_rows):
        self.dp = lax.axis_size("dp")
        self.seq = lax.axis_size("seq")
        self.windows = windows
        self.rows = local_rows
        self.length = local_rows * self.seq
        self.group = self.seq // (2 * windows)
        self.heads = H // (2 * self.group)
        self.core = lax.axis_index("dp") % 2
        self.is_first = self.core == 0
        self.place = lax.axis_index("seq") % self.group
        self.part = self.rows // (2 * self.group)
        self.head_start = (self.core * self.group + self.place) * self.heads

    def swap(self, array):
        return lax.ppermute(array, "dp", [(i, i ^ 1) for i in range(self.dp)])

    def rows_to_windows(self, own):
        kept, sent = own
        return ordered(kept, self.swap(sent), self.is_first, 0)

    def halves(self, array, axis):
        size = array.shape[axis] // 2
        kept = lax.dynamic_slice_in_dim(array, self.core * size, size, axis)
        sent = lax.dynamic_slice_in_dim(array, (1 - self.core) * size, size, axis)
        return (kept, sent)

    def exchange(self, array):
        return lax.all_to_all(array, "seq", split_axis=0, concat_axis=0, tiled=True)

    def inputs_to_windows(self, inputs):
        both = self.rows_to_windows(self.halves(inputs, 1))
        return both.reshape(self.seq, self.part, inputs.shape[2])

    def gather_rows(self, array):
        features = array.shape[2]
        array = array[:, None]
        if self.group > 1:
            hops = [
                (i, i - i % self.group + (i + 1) % self.group) for i in range(self.seq)
            ]
            pieces = [array]
            for _ in range(self.group - 1):
                pieces.append(lax.ppermute(pieces[-1], "seq", hops))
            pieces = jnp.concatenate(pieces, axis=1)
            order = (self.place - jnp.arange(self.group)) % self.group
            array = jnp.take(pieces, order, axis=1)
        array = ordered(
            array[:, None], self.swap(array)[:, None], self.is_first, 1
        )
        return array.reshape(self.length, features)

    def sum_rows(self, partial):
        features = partial.shape[1]
        partial = partial.reshape(self.seq, 2, self.group * self.part, features)
        kept, sent = self.halves(partial, 1)
        total = kept[:, 0].astype(jnp.float32) + self.swap(
            sent[:, 0].astype(jnp.bfloat16)
        ).astype(jnp.float32)
        if self.group > 1:
            total = lax.psum_scatter(
                total.reshape(self.seq, self.group, self.part, features),
                "seq",
                scatter_dimension=1,
                axis_index_groups=[
                    list(range(i, i + self.group)) for i in range(0, self.seq, self.group)
                ],
                tiled=True,
            )
            total = total[:, 0]
        return total.astype(jnp.bfloat16)

    def sums_to_rows(self, array):
        features = array.shape[2]
        back = array.reshape(2 * self.windows, self.group * self.part, features)
        kept, sent = self.halves(back, 0)
        return ordered(kept, self.swap(sent), self.is_first, 1)

    def heads_to_rows(self, chunk):
        count = chunk.shape[1]
        back = self.exchange(chunk.reshape(self.seq, self.rows, count))
        kept, sent = self.halves(
            back.reshape(2 * self.windows, self.group, self.rows, count), 0
        )
        return (kept, self.swap(sent))

    def rows_to_heads(self, kept, sent):
        count = kept.shape[3]
        both = self.rows_to_windows((kept, sent))
        back = self.exchange(both.reshape(self.seq, self.rows, count))
        return back.reshape(self.length, count)


def bias_tables(special, at):
    length, own = (at.length, at.heads)
    pos_low = special[: F * H].reshape(F, H)
    pos_basis = position_basis(length)
    own_pos = lax.dynamic_slice_in_dim(pos_low, at.head_start, own, 1)
    tables = jnp.dot(own_pos.T, pos_basis.T, precision=highest)
    tables = jnp.roll(jnp.pad(tables, ((0, 0), (0, 1))), 1 - BLOCK, axis=1)
    tables = jnp.broadcast_to(tables[:, None, :], (own, 8, 2 * length))
    return (pos_basis, tables)


def gather_weights(params, sent, at):
    devices = lax.axis_size(("dp", "seq"))
    index = lax.axis_index(("dp", "seq"))
    dp, seq = lax.axis_size("dp"), lax.axis_size("seq")
    shard = params.shape[0]
    own_rows = ROWS // devices
    extra = shard - own_rows * D
    rest = extra * devices
    tail = params[shard - TAIL :].astype(jnp.bfloat16)
    before = lax.ppermute(tail, ("dp", "seq"), [(i, i + 1) for i in range(devices - 1)])
    joined = jnp.concatenate([before.astype(jnp.float32), params])
    piece = lax.dynamic_slice_in_dim(joined, TAIL - extra * index, own_rows * D)
    piece = piece.astype(jnp.bfloat16).reshape(own_rows, D)
    special = jnp.where(index == devices - 1, tail, jnp.zeros_like(tail))
    for axis, bit in axis_bits("dp"):
        special = special + partner(special, axis, bit)
    special = jnp.broadcast_to(special.reshape(1, TAIL // D, D), (seq, TAIL // D, D))
    special = lax.all_to_all(special, "seq", split_axis=0, concat_axis=0, tiled=True)[seq - 1]
    special, sent = lax.optimization_barrier((special, sent))
    ready = lax.all_to_all(sent, "seq", split_axis=0, concat_axis=0, tiled=True)
    special = special.astype(jnp.float32).reshape(-1)[TAIL - rest :]
    pos_basis, tables = bias_tables(special, at)
    if own_rows % UNIT == 0:
        here = piece.reshape(own_rows // UNIT, UNIT, D)
        other = jnp.swapaxes(piece.reshape(own_rows // UNIT, 8, 2, D), 1, 2).reshape(here.shape)
        row = own_rows * index + UNIT * jnp.arange(own_rows // UNIT)
        inside = (row >= UP_ROWS[0]) & (row < UP_ROWS[0] + UP_ROWS[1])
        piece = jnp.where(inside[:, None, None], other, here).reshape(piece.shape)
    half = own_rows // 2
    if dp == 2 and half % 8 == 0:
        second = lax.axis_index("dp") == 1
        given = jnp.where(second, piece[:half], piece[half:])
        taken = partner(given, "dp", 0)
        low = jnp.where(second, taken, piece[:half])
        high = jnp.where(second, piece[half:], taken)
        lower = lax.all_gather(low, ("seq", "dp"), axis=0, tiled=True)
        high, lower, ready, tables = lax.optimization_barrier((high, lower, ready, tables))
        upper = lax.all_gather(high, ("seq", "dp"), axis=0, tiled=True)
    else:
        everything = lax.all_gather(piece, ("dp", "seq"), axis=0, tiled=True)
        lower, upper = (everything[: ROWS // 2], everything[ROWS // 2 :])
    if own_rows % UNIT == 0:
        w_up = up_units(lower.reshape(-1, UNIT, D), upper.reshape(-1, UNIT, D))
    else:
        w_up = jnp.concatenate([lower[UP_ROWS[0] :], upper[: UP_ROWS[0] + UP_ROWS[1] - ROWS // 2]])
        w_up = jnp.swapaxes(w_up.reshape(96, UNIT, 2, D), 1, 2)
    views = [array.reshape(-1, 2, UNIT, D) for array in (lower, upper)]
    return (lower, (*views, w_up), special, ready, pos_basis, tables)


def axis_bits(axis):
    return [(axis, bit) for bit in range(lax.axis_size(axis).bit_length() - 2, -1, -1)]


def partner(array, axis, bit):
    pairs = [(i, i ^ (1 << bit)) for i in range(lax.axis_size(axis))]
    return lax.ppermute(array, axis, pairs)


def turned(number):
    along = axis_bits("seq")[::-1]
    return (along, along[1:2] + along[:1] + along[2:], along[2:] + along[:2])[number % 3]


def halves_apart(rows, first, outer, inner):
    units = rows.shape[0] // (2 * UNIT)
    here = rows.reshape(units, 2 * UNIT, D)
    other = jnp.swapaxes(rows.reshape(units, outer, inner, D), 1, 2).reshape(here.shape)
    inside = first + 2 * UNIT * jnp.arange(units) < 2 * D
    return jnp.where(inside[:, None, None], other, here).reshape(rows.shape)


class Sums:
    def __init__(self, rows):
        self.bits = axis_bits("dp") + axis_bits("seq")
        self.states = [rows.reshape((2,) * len(self.bits) + (-1, D))]
        self.left = [list(self.bits)]
        self.orders = [axis_bits("dp")[::-1]]
        self.steps = len(self.bits)

    def send(self):
        self.steps -= 1
        if not self.orders[0]:
            band = D // 3
            self.states = [self.states[0][..., k * band : (k + 1) * band] for k in range(3)]
            self.left = [list(self.left[0]) for _ in range(3)]
            self.orders = [turned(k) for k in range(3)]
        for k, state in enumerate(self.states):
            axis, bit = self.orders[k][0]
            self.orders[k] = self.orders[k][1:]
            dim = self.left[k].index((axis, bit))
            self.left[k].pop(dim)
            mine = (lax.axis_index(axis) >> bit) & 1
            sent = lax.dynamic_index_in_dim(state, 1 - mine, dim, False)
            kept = lax.dynamic_index_in_dim(state, mine, dim, False)
            self.states[k] = (kept, sent, axis, bit)

    def before(self, array):
        sent, array = lax.optimization_barrier(([state[1] for state in self.states], array))
        self.states = [
            (kept, there, axis, bit)
            for (kept, _, axis, bit), there in zip(self.states, sent, strict=True)
        ]
        return array

    def move(self):
        self.states = [
            (kept, partner(sent, axis, bit), axis, bit) for kept, sent, axis, bit in self.states
        ]

    def add(self):
        self.states = [
            (kept.astype(jnp.float32) + other.astype(jnp.float32)).astype(jnp.bfloat16)
            for kept, other, _, _ in self.states
        ]

    def finish(self, left=0):
        while self.steps > left:
            self.send()
            self.move()
            self.add()
        return jnp.concatenate(self.states, axis=1) if left == 0 else None


PARTS = ((4096, 6144), (2560, 1536), (10240, 1536))
QKV_PARTS = ((0, 2560),)


def moves(parts, more):
    devices = lax.axis_size(("dp", "seq"))
    own_rows = ROWS // devices
    count = sum(rows for _, rows in parts) // devices
    found, start = ([], 0)
    for first, rows in parts:
        for t in range(devices):
            low, high = (max(count * t, start), min(count * (t + 1), start + rows))
            if low >= high:
                continue
            row = first + low - start
            for i in range(devices):
                if row < own_rows * (i + 1) + more and row + high - low > own_rows * i:
                    found.append((i, t, high - low, row - own_rows * i, low - count * t))
        start += rows
    rounds = []
    for move in found:
        for held in rounds:
            if all(move[0] != other[0] and move[1] != other[1] for other in held):
                held.append(move)
                break
        else:
            rounds.append([move])
    return (rounds, count)


def per_device(values):
    index = lax.axis_index(("dp", "seq"))
    result = jnp.zeros((), jnp.int32)
    for place, value in values:
        if value != 0:
            result = jnp.where(index == place, value, result)
    return result


def to_owners(buffer, share, parts):
    rounds, most = moves(parts, TAIL // D)
    starts = [value for held in rounds for move in held for value in move[2:]]
    size = math.gcd(UNIT, MARGIN, most, buffer.shape[0], *starts)
    blocks = most // size
    share = jnp.pad(share.reshape(blocks, size, D), ((0, blocks), (0, 0), (0, 0)))
    buffer = buffer.reshape(-1, size, D)
    arrived = []
    for held in rounds:
        start = per_device([(t, offset // size) for _, t, _, _, offset in held])
        arrived.append(
            lax.ppermute(
                lax.dynamic_slice_in_dim(share, start, blocks, 0),
                ("dp", "seq"),
                [(t, i) for i, t, _, _, _ in held],
            )
        )
    for held, moved in zip(rounds, arrived, strict=True):
        place = per_device([(i, (MARGIN + low) // size) for i, _, _, low, _ in held])
        count = per_device([(i, rows // size) for i, _, rows, _, _ in held])
        inside = jnp.arange(blocks) < count
        moved = jnp.where(inside[:, None, None], moved, jnp.zeros_like(moved))
        there = lax.dynamic_slice_in_dim(buffer, place, blocks, 0)
        buffer = lax.dynamic_update_slice_in_dim(buffer, there + moved, place, 0)
    return buffer.reshape(-1, D)


def own_entries(buffer, special):
    devices = lax.axis_size(("dp", "seq"))
    index = lax.axis_index(("dp", "seq"))
    own_rows = ROWS // devices
    rest = special.shape[0]
    extra = rest // devices
    held = buffer[MARGIN : MARGIN + own_rows + TAIL // D].astype(jnp.float32)
    after = held[own_rows:].reshape(-1)
    after = jnp.where(index == devices - 1, jnp.pad(special, (0, TAIL - rest)), after)
    joined = jnp.concatenate([held[:own_rows].reshape(-1), after])
    return lax.dynamic_slice_in_dim(joined, extra * index, own_rows * D + extra)


def body(block_input, skip_input, species, cotangent, params, first_moment, second_moment):
    windows, local_rows, _ = block_input.shape
    at = Places(windows, local_rows)
    length = at.length
    own = at.heads
    scale = 1.0 / math.sqrt(KD)
    f32, bf16 = jnp.float32, jnp.bfloat16

    early, weights, special, moved, pos_basis, tables = gather_weights(
        params, at.inputs_to_windows(block_input), at
    )
    up_bias = special[F * H : F * H + FF]
    vectors = special[F * H + FF :].reshape(12, D)

    def columns(matrix, width):
        return lax.dynamic_slice_in_dim(matrix, at.head_start * width, own * width, 1)

    w_own = jnp.concatenate(
        [
            columns(early[:512].reshape(D, H * KD), KD) * jnp.asarray(scale, bf16),
            columns(early[512:1024].reshape(D, H * KD), KD),
            columns(early[1024:2560].reshape(D, H * VD), VD),
        ],
        axis=1,
    )
    low_part, _, _ = layer_stats(moved.astype(f32), vectors[0], vectors[1])
    low_all = at.gather_rows(low_part.astype(bf16))
    projected = jnp.einsum("rd,dk->kr", low_all, w_own, preferred_element_type=f32).astype(bf16)
    queries, keys, values = (
        projected[: own * KD],
        projected[own * KD : 2 * own * KD],
        projected[2 * own * KD :],
    )

    operands, saved, pieces = ([], [], ([], []))
    for pair in range(own // PAIR):
        narrow = slice(pair * PAIR * KD, (pair + 1) * PAIR * KD)
        wide = slice(pair * PAIR * VD, (pair + 1) * PAIR * VD)
        given = (
            tables[pair * PAIR : (pair + 1) * PAIR],
            queries[narrow],
            keys[narrow],
            values[wide],
        )
        result, log_total = attention_forward(*given)
        operands.append(given)
        saved.append((result, log_total))
        for held, part in zip(pieces, at.heads_to_rows(result), strict=True):
            held.append(part)
    pairs = own // PAIR
    pieces = [
        held[pair][:, place] for held in pieces for place in range(at.group) for pair in range(pairs)
    ]

    core = jnp.asarray(at.core, jnp.int32).reshape(1)
    heads, hidden_one, low_two, activated, slope, hidden_two = dense_forward(
        core, block_input, pieces, vectors, up_bias[None], weights
    )
    ends = [
        (hidden_two[:, row : row + 1] + skip_input[:, up : up + 1].astype(f32)).astype(bf16)
        for row, up in ((0, 0), (local_rows - 1, 2 * local_rows - 1))
    ]
    first, last = edge_rows(ends)
    is_mouse = (species == 1).astype(f32)[:, None]
    species_gain = (1.0 - is_mouse) * vectors[10] + is_mouse * vectors[11]
    block_out, grad_conv, dense_grads, gain_rows, point_sums = point_layer(
        hidden_two,
        skip_input,
        cotangent,
        first,
        last,
        species_gain[:, None, :],
        vectors,
        weights,
    )
    gain_rows = gain_rows[:, 0]
    grad_human = jnp.sum((1.0 - is_mouse) * gain_rows, axis=0)
    grad_mouse = jnp.sum(is_mouse * gain_rows, axis=0)
    first, last = edge_rows([grad_conv[:, :1], grad_conv[:, 2 * local_rows - 1 :]])
    (
        skip_grad,
        grad_mid,
        grad_down_low,
        grad_before,
        grad_attn_low,
        *grad_pieces,
        dense_sums,
        up_sums,
    ) = dense_backward(
        core,
        cotangent,
        grad_conv,
        first,
        last,
        slope,
        hidden_one,
        vectors,
        weights,
    )
    grad_pieces = [
        jnp.stack(
            [
                grad_pieces[2 * group + place * pairs + pair]
                for place in range(at.group)
            ],
            axis=1,
        )
        for group in range(2)
        for pair in range(pairs)
    ]

    middle = jnp.concatenate(
        [
            up_sums[0],
            dense_sums[1],
            dense_sums[2],
            dense_sums[3],
            dense_sums[0],
            point_sums[:4].reshape(-1),
            grad_human,
            grad_mouse,
        ]
    )
    devices = lax.axis_size(("dp", "seq"))
    chunks = [at.rows_to_heads(grad_pieces[pair], grad_pieces[pairs + pair]) for pair in range(pairs)]
    dense_grads = weight_grad(activated, grad_down_low, dense_grads, DOWN)
    dense_grads = weight_grad(low_two, grad_before, dense_grads, LEFT)
    dense_grads = weight_grad(heads, grad_attn_low, dense_grads, OUT).reshape(-1, D)
    even = dense_grads.shape[0] // devices % (2 * UNIT) == 0
    if not even:
        dense_grads = halves_apart(dense_grads, 0, 2, UNIT)
    dense_grads, chunks[0] = lax.optimization_barrier((dense_grads, chunks[0]))
    dense = lax.psum_scatter(dense_grads, ("dp", "seq"), scatter_dimension=0, tiled=True)

    dq, dk, dv, dt = ([], [], [], [])
    for pair in range(pairs):
        result, log_total = saved[pair]
        grads = attention_backward(*operands[pair], result, chunks[pair], log_total)
        if pair + 1 < pairs:
            grads, chunks[pair + 1] = lax.optimization_barrier((grads, chunks[pair + 1]))
        for piece, held in zip(grads, (dq, dk, dv, dt), strict=True):
            held.append(piece)
    grad_own = jnp.concatenate(dq + dk + dv, axis=1)
    partial = jnp.einsum("rk,dk->rd", grad_own, w_own, preferred_element_type=f32).astype(bf16)
    partial, grad_own = lax.optimization_barrier((partial, grad_own))
    back = at.exchange(at.sum_rows(partial))
    grad_w_own = jnp.einsum("rd,rk->dk", low_all, grad_own, preferred_element_type=f32)
    grad_w_query = grad_w_own[:, : own * KD] * scale
    grad_w_key = grad_w_own[:, own * KD : 2 * own * KD]
    grad_w_value = grad_w_own[:, 2 * own * KD :]

    def all_columns(matrix, width):
        whole = jnp.zeros((D, H * width), bf16)
        return lax.dynamic_update_slice_in_dim(
            whole, matrix.astype(bf16), at.head_start * width, 1
        ).reshape(-1, D)

    first_rows = jnp.concatenate(
        [
            all_columns(grad_w_query, KD),
            all_columns(grad_w_key, KD),
            all_columns(grad_w_value, VD),
        ],
        axis=0,
    )
    first_sums = Sums(first_rows)
    first_sums.finish(2)
    first_sums.states, back = lax.optimization_barrier((first_sums.states, back))
    grad_norm_one = at.sums_to_rows(back).astype(f32)
    _, stats_one, inverse_one = layer_stats(block_input.astype(f32), vectors[0], vectors[1])
    input_grad = grad_mid + norm_back(grad_norm_one, stats_one, inverse_one, vectors[0])
    grad_gain_one = jnp.sum(grad_norm_one * stats_one, axis=(0, 1))
    grad_bias_one = jnp.sum(grad_norm_one, axis=(0, 1))
    grad_tables = jnp.roll(jnp.concatenate(dt, axis=0), BLOCK - 1, axis=1)[:, : 2 * length - 1]
    grad_pos = jnp.dot(pos_basis.T, grad_tables.T, precision=highest)
    grad_pos = lax.dynamic_update_slice_in_dim(
        jnp.zeros((F, H), f32), grad_pos, at.head_start, 1
    )
    late = jnp.concatenate([grad_pos.reshape(-1), grad_gain_one, grad_bias_one])
    summed = jnp.concatenate([late, middle])
    for axis, bit in axis_bits("dp") + axis_bits("seq"):
        other = partner(summed, axis, bit)
        if first_sums.steps > 0:
            first_sums.send()
            first_sums.move()
            first_sums.add()
            first_sums.states, other = lax.optimization_barrier((first_sums.states, other))
        summed = summed + other
    late, middle = (summed[: late.shape[0]], summed[late.shape[0] :])
    special_grads = jnp.concatenate(
        [late[: F * H], middle[:FF], late[F * H :], middle[FF:]]
    )
    buffer = jnp.zeros((ROWS // devices + TAIL // D + 2 * MARGIN, D), bf16)
    buffer = to_owners(buffer, first_sums.finish(), QKV_PARTS)
    share, buffer = lax.optimization_barrier((dense, buffer))
    if even:
        share = halves_apart(share, lax.axis_index(("dp", "seq")) * share.shape[0], 2, UNIT)
    buffer = to_owners(buffer, share, PARTS)
    reduced = own_entries(buffer, special_grads)
    shard_len = params.shape[0]
    position = lax.axis_index(("dp", "seq")) * shard_len + jnp.arange(shard_len)
    param_new, first_new, second_new = adam_update(
        params, first_moment, second_moment, reduced, position
    )
    return (
        block_out,
        input_grad,
        skip_grad,
        param_new,
        first_new,
        second_new,
        param_new.astype(bf16),
    )


def solution(mesh):
    return jax.shard_map(
        body,
        mesh=mesh,
        in_specs=(
            P("dp", "seq", None),
            P("dp", "seq", None),
            P("dp"),
            P("dp", "seq", None),
            P(("dp", "seq")),
            P(("dp", "seq")),
            P(("dp", "seq")),
        ),
        out_specs=(
            P("dp", "seq", None),
            P("dp", "seq", None),
            P("dp", "seq", None),
            P(("dp", "seq")),
            P(("dp", "seq")),
            P(("dp", "seq")),
            P(("dp", "seq")),
        ),
        check_vma=False,
    )
```
